32 devices in a mesh: pipe: 2 (over core), dp: 16 (over z, y, x).
Axes of the slice: x: 2, y: 2, z: 4, core: 2. Of those that a mesh axis runs over, the one named last changes fastest.
Arguments:
- tokens: bfloat16 [32768, 512], P('dp'), may hold values from -6 to 6
- lengths: int32 [32], P('dp'), may hold values from 513 to 1024, as said below
- memory_init: bfloat16 [64, 512], replicated, may hold values from -6 to 6
- attn_gain: float32 [2, 512], P('pipe'), may hold values from 0.5 to 1.5
- qkv_weight: bfloat16 [2, 512, 1536], P('pipe'), may hold values from -0.25 to 0.25
- proj_weight: bfloat16 [2, 512, 512], P('pipe'), may hold values from -0.75 to 0.75
- ffn_gain: float32 [2, 512], P('pipe'), may hold values from 0.5 to 1.5
- in_weight: bfloat16 [2, 512, 2048], P('pipe'), may hold values from -0.25 to 0.25
- out_weight: bfloat16 [2, 2048, 512], P('pipe'), may hold values from -0.125 to 0.125
- cot_tokens: bfloat16 [32768, 512], P('dp'), may hold values from -6 to 6
- cot_memory: bfloat16 [32, 64, 512], P('dp'), may hold values from -6 to 6
Outputs:
- activations: bfloat16 [32768, 512], P('dp')
- final_memory: bfloat16 [32, 64, 512], P('dp')
- grad_tokens: bfloat16 [32768, 512], P('dp', 'pipe')
- grad_memory_init: float32 [64, 512], replicated
- grad_attn_gain: float32 [2, 512], P('pipe')
- grad_qkv_weight: float32 [2, 512, 1536], P('pipe')
- grad_proj_weight: float32 [2, 512, 512], P('pipe')
- grad_ffn_gain: float32 [2, 512], P('pipe')
- grad_in_weight: float32 [2, 512, 2048], P('pipe')
- grad_out_weight: float32 [2, 2048, 512], P('pipe')
The draws below stay inside these ranges and needn't reach their ends.
Inputs may be any that keep to these rules, and one draw needn't show every extreme that they name: `lengths`: every document is longer than 1 segments, so only its last segment has invalid positions; some document has the full 2 * 512 tokens.
All inputs are finite; a program needn't handle non-finite values.
Results may differ from the reference program's by a relative error of at most 0.018.
Values may be sent and summed in bfloat16 or wider, within the bound.
No kernel may reach another device: no remote copies, remote signals or barrier semaphores. Data moves between devices by JAX's collectives and lax.ppermute only.
A program may use at most 320 MiB of HBM per device.

```python
import jax
import jax.numpy as jnp
from jax import lax

D = 512
HEADS = 8
HEAD_DIM = 64
FF = 2048
SLOTS = 64
SEG_LEN = 512
SEGS = 2
DOCS = 32
TOKENS = 32768
N_PIPE = 2


def draw_lengths(key, part):
    key = jax.random.fold_in(key, 11)
    first_key, second_key = jax.random.split(key)
    shortest = (SEGS - 1) * SEG_LEN + 1
    drawn = jax.random.randint(first_key, (DOCS,), shortest, SEGS * SEG_LEN + 1)
    chosen = jax.random.randint(second_key, (), 0, DOCS)
    return jnp.where(jnp.arange(DOCS) == chosen, SEGS * SEG_LEN, drawn).astype(jnp.int32)


def level_of(own_key, dims, pieces, low, high):
    def one(dim, shards_of):
        draws = jax.random.uniform(jax.random.fold_in(jax.random.fold_in(own_key, 6), dim), (shards_of,), jnp.float32, low / len(pieces), high / len(pieces))
        return jnp.repeat(jnp.exp(draws), dims[dim] // shards_of).reshape((-1,) + (1,) * (len(dims) - dim - 1))

    loudness = one(*pieces[0])
    for cut in pieces[1:]:
        loudness = loudness * one(*cut)
    return loudness


def scatter_about(stream_key, extent, deviation, most, cuts=(), held_as=jnp.bfloat16):
    level = level_of(stream_key, extent, cuts, -0.22, 0.18) if cuts else 1.0
    values = jax.random.normal(stream_key, extent, jnp.float32) * deviation * level
    return jnp.minimum(jnp.maximum(values, -most), most).astype(held_as)


def setup_inputs(seed: int = 0) -> dict:
    arg_keys = jax.random.split(jax.random.key(seed), 12)
    tokens = scatter_about(arg_keys[0], (TOKENS, D), 1.0, 6.0, ((0, 16),))
    lengths = draw_lengths(jax.random.fold_in(arg_keys[11], 71), 0)
    memory_init = scatter_about(arg_keys[2], (SLOTS, D), 1.0, 6.0)
    attn_gain = jnp.clip(1.0 + 0.1 * jax.random.normal(arg_keys[3], (N_PIPE, D), jnp.float32), 0.5, 1.5)
    qkv_weight = scatter_about(arg_keys[4], (N_PIPE, D, 3 * D), D ** -0.5, 0.25, ((0, 2),))
    proj_weight = scatter_about(arg_keys[5], (N_PIPE, D, D), (D // 8) ** -0.5, 0.75, ((0, 2),))
    ffn_gain = jnp.clip(1.0 + 0.1 * jax.random.normal(arg_keys[6], (N_PIPE, D), jnp.float32), 0.5, 1.5)
    in_weight = scatter_about(arg_keys[7], (N_PIPE, D, FF), D ** -0.5, 0.25, ((0, 2),))
    out_weight = scatter_about(arg_keys[8], (N_PIPE, FF, D), FF ** -0.5, 0.125, ((0, 2),))
    cot_tokens = scatter_about(arg_keys[9], (TOKENS, D), 1.0, 6.0, ((0, 16),))
    cot_memory = scatter_about(arg_keys[10], (DOCS, SLOTS, D), 1.0, 6.0, ((0, 16),))
    return dict(tokens=tokens, lengths=lengths, memory_init=memory_init, attn_gain=attn_gain, qkv_weight=qkv_weight, proj_weight=proj_weight, ffn_gain=ffn_gain, in_weight=in_weight, out_weight=out_weight, cot_tokens=cot_tokens, cot_memory=cot_memory)


@jax.custom_vjp
def low(v):
    return lax.optimization_barrier(v.astype(jnp.bfloat16)).astype(jnp.float32)

@jax.custom_vjp
def low_back(v):
    return v

def low_keep(v):
    return (low(v), None)

def low_pass(kept, grad):
    return (grad,)

def back_keep(v):
    return (v, None)

def back_low(kept, grad):
    return (low(grad),)
low.defvjp(low_keep, low_pass)
low_back.defvjp(back_keep, back_low)
epsilon = 1e-05
masked_bias = -1000000000.0

def layer_norm(values, gain):
    centred = values - lax.optimization_barrier(jnp.mean(values, axis=-1, keepdims=True))
    spread = lax.optimization_barrier(jnp.mean(centred * centred, axis=-1, keepdims=True))
    return centred * lax.rsqrt(spread + epsilon) * gain

def product(left, right):
    return jnp.dot(left, right, precision=lax.Precision.HIGHEST, preferred_element_type=jnp.float32)

def layer(params, segment, memory, key_bias, writer):
    attn_gain, qkv_weight, proj_weight, ffn_gain, in_weight, out_weight = params
    length = segment.shape[0]
    all_rows = jnp.concatenate([segment, memory], axis=0)
    normed = low(layer_norm(all_rows, attn_gain))
    query_rows = normed[length:] if writer else normed[:length]
    queries = low_back(low(product(query_rows, qkv_weight[:, :D])))
    key_rows = low_back(low(product(normed, qkv_weight[:, D:2 * D])))
    value_rows = low_back(low(product(normed, qkv_weight[:, 2 * D:])))
    head_queries = queries.reshape(-1, HEADS, HEAD_DIM)
    head_keys = key_rows.reshape(-1, HEADS, HEAD_DIM)
    head_values = value_rows.reshape(-1, HEADS, HEAD_DIM)
    raw_scores = jnp.einsum('qhd,khd->hqk', head_queries, head_keys, precision=lax.Precision.HIGHEST) * HEAD_DIM ** (-0.5)
    scores = low_back(raw_scores) + key_bias[None, None, :]
    attention = jax.nn.softmax(scores, axis=-1)
    mixed_heads = jnp.einsum('hqk,khd->qhd', low(attention), head_values, precision=lax.Precision.HIGHEST)
    mixed_rows = low_back(low(mixed_heads.reshape(-1, D)))
    attended = low_back(product(mixed_rows, proj_weight))
    hidden = (memory if writer else segment) + attended
    normed_ffn = low(layer_norm(hidden, ffn_gain))
    pre_active = low_back(product(normed_ffn, in_weight))
    active = low(jax.nn.gelu(pre_active))
    branch = low_back(product(active, out_weight))
    if writer:
        return low(memory + jax.nn.sigmoid(branch) * attended)
    return hidden + branch

def reference(tokens, lengths, memory_init, attn_gain, qkv_weight, proj_weight, ffn_gain, in_weight, out_weight, cot_tokens, cot_memory):
    positions = jnp.arange(SEGS * SEG_LEN, dtype=jnp.int32)
    token_valid = positions[None, :] < lengths[:, None]
    row_bias = jnp.where(token_valid, 0.0, masked_bias).astype(jnp.float32).reshape(DOCS, SEGS, SEG_LEN)
    key_bias = jnp.concatenate([row_bias, jnp.zeros((DOCS, SEGS, SLOTS), jnp.float32)], axis=2)

    def forward(tokens_f, memory_f, gain_attn, qkv_f, proj_f, gain_ffn, inner_f, outer_f):
        first_params = (gain_attn[0], qkv_f[0], proj_f[0], gain_ffn[0], inner_f[0], outer_f[0])
        second_params = (gain_attn[1], qkv_f[1], proj_f[1], gain_ffn[1], inner_f[1], outer_f[1])

        def one_document(carry, item):
            doc_tokens, doc_bias = item
            memory_front = memory_f
            memory_back = memory_f
            outputs = []
            for index in range(SEGS):
                result = layer(first_params, doc_tokens[index], memory_front, doc_bias[index], False)
                outputs.append(result)
                memory_back = layer(second_params, low_back(low(result)), memory_back, doc_bias[index], True)
                memory_front = low_back(memory_back)
            return (carry, (jnp.stack(outputs), memory_back))
        unused, (rows_out, memory_out) = lax.scan(one_document, jnp.zeros((), jnp.float32), (tokens_f.reshape(DOCS, SEGS, SEG_LEN, D), key_bias))
        return (rows_out.reshape(DOCS * SEGS * SEG_LEN, D), memory_out)
    primals = (tokens.astype(jnp.float32), memory_init.astype(jnp.float32), attn_gain.astype(jnp.float32), qkv_weight.astype(jnp.float32), proj_weight.astype(jnp.float32), ffn_gain.astype(jnp.float32), in_weight.astype(jnp.float32), out_weight.astype(jnp.float32))
    (rows_out, memory_out), backward = jax.vjp(forward, *primals)
    grads = backward((cot_tokens.astype(jnp.float32), cot_memory.astype(jnp.float32)))
    return (rows_out.astype(jnp.bfloat16), memory_out.astype(jnp.bfloat16), grads[0].astype(jnp.bfloat16), grads[1], grads[2], grads[3], grads[4], grads[5], grads[6], grads[7])
```

```python
import jax
import jax.numpy as jnp
from jax import lax
from jax.experimental import pallas as pl
from jax.experimental.pallas import tpu as pltpu
from jax.sharding import PartitionSpec as P

D = 512
HEADS = 8
HEAD_DIM = 64
FF = 2048
SLOTS = 64
SEG_LEN = 512
SEGS = 2
ROWS = SEG_LEN + SLOTS
TILE = 512
BLOCKS = 12
HALF = TILE // 2
PIECE = 3 * HALF

epsilon = 1e-05
masked_bias = -1000000000.0
score_scale = HEAD_DIM ** (-0.5)
exponent_scale = score_scale * 1.4426950408889634
gelu_a = 0.7978845608028654
gelu_b = 0.044715 * gelu_a

BF16 = jnp.bfloat16
F32 = jnp.float32


def dot(left, right):
    return jnp.dot(left, right, preferred_element_type=F32)


def dot_t(left, right):
    return lax.dot_general(left, right, (((1,), (1,)), ((), ())), preferred_element_type=F32)


def normalise(values):
    centred = values - jnp.mean(values, axis=-1, keepdims=True)
    spread = jnp.mean(centred * centred, axis=-1, keepdims=True)
    inverse = lax.rsqrt(spread + epsilon)
    return centred * inverse, inverse


def layer_norm(values, gain):
    return normalise(values)[0] * gain


def layer_norm_back(values, gain, grads):
    scaled, inverse = normalise(values)
    gain_grad = jnp.sum(grads * scaled, axis=0, keepdims=True)
    inner = grads * gain
    mean_inner = jnp.mean(inner, axis=-1, keepdims=True)
    mean_scaled = jnp.mean(inner * scaled, axis=-1, keepdims=True)
    return inverse * (inner - mean_inner - scaled * mean_scaled), gain_grad


def gelu_both(values):
    square = values * values
    tangent = jnp.tanh(values * (gelu_a + gelu_b * square))
    half = 0.5 + 0.5 * tangent
    slope = half + (0.5 * values) * (1.0 - tangent * tangent) * (gelu_a + 3.0 * gelu_b * square)
    return values * half, slope


def iota(shape, dim):
    return lax.broadcasted_iota(jnp.int32, shape, dim)


def repeat_matrix():
    return (iota((SLOTS, D), 0) == iota((SLOTS, D), 1) % SLOTS).astype(BF16)


def head_blocks():
    return iota((D, D), 0) // HEAD_DIM == iota((D, D), 1) // SLOTS


class Mover:
    def __init__(self, sems):
        self.sems = sems
        self.used = 0
        self.coming = {}
        self.leaving = []

    def slot(self):
        self.used += 1
        return self.sems.at[self.used - 1]

    def bring(self, target, source):
        sem = self.slot()
        pltpu.make_async_copy(source, target, sem).start()
        self.coming[id(target)] = (source, target, sem)

    def bring_either(self, target, pick_first, first, second):
        sem = self.slot()

        @pl.when(pick_first)
        def _():
            pltpu.make_async_copy(first, target, sem).start()

        @pl.when(jnp.logical_not(pick_first))
        def _():
            pltpu.make_async_copy(second, target, sem).start()

        self.coming[id(target)] = (first, target, sem)

    def need(self, *targets):
        for target in targets:
            if id(target) in self.coming:
                pltpu.make_async_copy(*self.coming.pop(id(target))).wait()

    def send(self, source, target):
        copy = pltpu.make_async_copy(source, target, self.slot())
        copy.start()
        self.leaving.append(copy)
        return copy

    def left(self, *copies):
        for copy in copies:
            copy.wait()
            self.leaving = [other for other in self.leaving if other is not copy]

    def finish(self):
        for copy in self.leaving:
            copy.wait()


def valid_keys(shape, valid_rows):
    row = iota(shape, 0)
    return (row < valid_rows) | (row >= SEG_LEN)


def encoder_attention(need, x, m, bias, gain, wqkv, wproj, n, qt, kv, vt, probs, inv, mixt, hidden):
    need(x, m)
    n[:SEG_LEN] = layer_norm(x[...].astype(F32), gain).astype(BF16)
    n[SEG_LEN:] = layer_norm(m[...].astype(F32), gain).astype(BF16)
    need(wqkv)
    qt[...] = dot_t(wqkv[:, :D].T, n[:SEG_LEN]).astype(BF16)
    kv[:, :D] = dot(n[...], wqkv[:, D : 2 * D]).astype(BF16)
    values = dot(n[...], wqkv[:, 2 * D :]).astype(BF16)
    kv[:, D:] = values
    vt[...] = values.T
    low_lanes = iota((ROWS, 128), 1) < HEAD_DIM
    ones_row = (iota((HEAD_DIM, SEG_LEN), 0) == 0).astype(BF16)

    def pair(index, carry):
        base = pl.multiple_of(index * 128, 128)
        keys = kv[:, pl.ds(base, 128)]
        for half in range(2):
            head = 2 * index + half
            rows = pl.ds(pl.multiple_of(base + half * HEAD_DIM, HEAD_DIM), HEAD_DIM)
            queries = qt[rows]
            if half == 0:
                left = jnp.where(low_lanes, keys, bias[...])
                right = jnp.concatenate([queries, ones_row], axis=0)
            else:
                left = jnp.where(low_lanes, bias[...], keys)
                right = jnp.concatenate([ones_row, queries], axis=0)
            scores = dot(left, right)
            top = jnp.max(scores, axis=0, keepdims=True)
            grown = jnp.exp2(scores * exponent_scale - top * exponent_scale)
            inverse = 1.0 / jnp.sum(grown, axis=0, keepdims=True)
            low = grown.astype(BF16)
            probs[head] = low
            inv[head] = inverse
            mixt[rows] = (dot(vt[rows], low) * inverse).astype(BF16)
        return carry

    lax.fori_loop(0, HEADS // 2, pair, 0)
    need(wproj)
    hidden[...] = x[...].astype(F32) + dot(mixt[...].T, wproj[...])


def encoder_ffn(need, hidden, gain, win, wout, y, nf, act, slope, total):
    need(hidden)
    nf[...] = layer_norm(hidden[...], gain).astype(BF16)
    total[...] = hidden[...]
    need(win, wout)

    def step(index, carry):
        span = pl.ds(pl.multiple_of(index * TILE, TILE), TILE)
        active, grad = gelu_both(dot(nf[...], win[:, span]))
        low = active.astype(BF16)
        act[:, span] = low
        slope[:, span] = grad.astype(BF16)
        total[...] += dot(low, wout[span])
        return carry

    lax.fori_loop(0, FF // TILE, step, 0)
    y[...] = total[...].astype(BF16)


def memory_forward(need, y, m, valid_rows, gain, ffn_gain, weights, result, kept, index, vt):
    wqkv, wproj, win, wout = weights
    n, kv, keyed, probs, inv, mixm, mixed, attended, hidden, nf, act, slope, branch = [ref.at[index] for ref in kept]
    need(m)
    mf = m[...].astype(F32)
    n[:SEG_LEN] = layer_norm(y[...].astype(F32), gain).astype(BF16)
    slots = layer_norm(mf, gain).astype(BF16)
    n[SEG_LEN:] = slots
    need(wqkv)
    kv[:, :D] = dot(n[...], wqkv[:, D : 2 * D]).astype(BF16)
    values = dot(n[...], wqkv[:, 2 * D :]).astype(BF16)
    kv[:, D:] = values
    vt[...] = values.T
    blocks = head_blocks()
    queries = dot_t(wqkv[:, :D].T, jnp.concatenate([slots] * HEADS, axis=0))
    keyed[...] = jnp.where(blocks, queries, 0.0).astype(BF16)
    scores = dot(kv[:, :D], keyed[...])
    if valid_rows is not None:
        scores = jnp.where(valid_keys((ROWS, D), valid_rows), scores, masked_bias)
    top = jnp.max(scores, axis=0, keepdims=True)
    grown = jnp.exp2(scores * exponent_scale - top * exponent_scale)
    inverse = 1.0 / jnp.sum(grown, axis=0, keepdims=True)
    probs[...] = grown.astype(BF16)
    inv[...] = inverse
    mixm[...] = jnp.where(blocks, dot(vt[...], probs[...]) * inverse, 0.0).astype(BF16)
    mixed[...] = dot_t(repeat_matrix(), mixm[...]).astype(BF16)
    need(wproj)
    attended[...] = dot(mixed[...], wproj[...])
    hidden[...] = mf + attended[...]
    nf[...] = layer_norm(hidden[...], ffn_gain).astype(BF16)
    need(win)
    active, grad = gelu_both(dot(nf[...], win[...]))
    act[...] = active.astype(BF16)
    slope[...] = grad.astype(BF16)
    need(wout)
    branch[...] = dot(act[...], wout[...])
    result[...] = (mf + jax.nn.sigmoid(branch[...]) * attended[...]).astype(BF16)


def memory_backward(go, y, m, gain, ffn_gain, weights, kept, index, grad_y, grad_m, grads):
    wqkv, wproj, win, wout = weights
    n, kv, keyed, probs, inv, mixm, mixed, attended, hidden, nf, act, slope, branch = [ref.at[index] for ref in kept]
    gb, gpre, ga, gq, gkv = [ref.at[index] for ref in grads]
    blocks = head_blocks()
    gate = jax.nn.sigmoid(branch[...])
    gof = go[...].astype(F32)
    gb[...] = (gof * attended[...] * gate * (1.0 - gate)).astype(BF16)
    gpre[...] = (slope[...].astype(F32) * dot_t(gb[...], wout[...])).astype(BF16)
    ghidden, ffn_gain_grad = layer_norm_back(hidden[...], ffn_gain, dot_t(gpre[...], win[...]))
    gattended = (ghidden + gof * gate).astype(BF16)
    ga[...] = gattended
    gmixed = dot_t(wproj[...], jnp.concatenate([gattended] * HEADS, axis=0)).astype(BF16).astype(F32)
    gmixed = jnp.where(blocks, gmixed * inv[...], 0.0)
    low_mixed = gmixed.astype(BF16)
    centre = jnp.sum(mixm[...].astype(F32) * gmixed, axis=0, keepdims=True)
    gprobs = dot(kv[:, D:], low_mixed)
    gscores = (probs[...].astype(F32) * (gprobs - centre)).astype(BF16)
    gqueries = dot(kv[:, :D].T, gscores) * score_scale
    gqueries = jnp.where(blocks, gqueries, 0.0).astype(BF16)
    gq[...] = dot_t(repeat_matrix(), gqueries).astype(BF16)
    gkv[:, :D] = (dot_t(gscores, keyed[...]) * score_scale).astype(BF16)
    gkv[:, D:] = dot_t(probs[...], low_mixed).astype(BF16)
    grows = dot_t(gkv[...], wqkv[:, D:])
    gslots = grows[SEG_LEN:] + dot_t(gq[...], wqkv[:, :D])
    grad_rows, gain_rows = layer_norm_back(y[...].astype(F32), gain, grows[:SEG_LEN])
    grad_slots, gain_slots = layer_norm_back(m[...].astype(F32), gain, gslots)
    grad_y[...] = grad_rows.astype(BF16)
    grad_m[...] = grad_slots + ghidden + gof
    return gain_rows + gain_slots, ffn_gain_grad


def encoder_ffn_backward(need, cot, grad_y, hidden, gain, win, wout, slope, gb, gnf, ga, ghidden):
    need(cot, grad_y)
    go = cot[...].astype(F32) + grad_y[...].astype(F32)
    gb[...] = go.astype(BF16)
    ghidden[...] = go
    gnf[...] = jnp.zeros_like(gnf)
    need(wout, slope, win)

    def step(index, carry):
        span = pl.ds(pl.multiple_of(index * TILE, TILE), TILE)
        low = (slope[:, span].astype(F32) * dot_t(gb[...], wout[span])).astype(BF16)
        slope[:, span] = low
        gnf[...] += dot_t(low, win[:, span])
        return carry

    lax.fori_loop(0, FF // TILE, step, 0)
    need(hidden)
    grad, gain_grad = layer_norm_back(hidden[...], gain, gnf[...])
    grad = grad + ghidden[...]
    ghidden[...] = grad
    ga[...] = grad.astype(BF16)
    return gain_grad


def encoder_attention_backward(
    need, x, m, gain, wqkv, wproj, qt, kv, probs, inv, mixt, ga, ghidden, kt, gmt, gqkvt, grad_x, grad_m
):
    need(wproj, ga)
    gmt[...] = dot_t(wproj[...], ga[...]).astype(BF16)
    need(kv)
    kt[...] = kv[:, :D].T
    gqkvt[:D, SEG_LEN:] = jnp.zeros((D, SLOTS), BF16)
    empty = jnp.zeros((HEAD_DIM, SEG_LEN), BF16)
    need(inv, mixt, qt, probs)

    def pair(index, carry):
        base = pl.multiple_of(index * 128, 128)
        values = kv[:, pl.ds(pl.multiple_of(D + base, 128), 128)]
        for half in range(2):
            head = 2 * index + half
            start = pl.multiple_of(base + half * HEAD_DIM, HEAD_DIM)
            rows = pl.ds(start, HEAD_DIM)
            scaled = gmt[rows].astype(F32) * inv[head]
            centre = jnp.sum(mixt[rows].astype(F32) * scaled, axis=0, keepdims=True)
            low = scaled.astype(BF16)
            if half == 0:
                right = jnp.concatenate([low, empty], axis=0)
            else:
                right = jnp.concatenate([empty, low], axis=0)
            gprobs = dot(values, right)
            gscores = (probs[head].astype(F32) * (gprobs - centre)).astype(BF16)
            gqkvt[rows, :SEG_LEN] = (dot(kt[rows], gscores) * score_scale).astype(BF16)
            gqkvt[pl.ds(pl.multiple_of(D + start, HEAD_DIM), HEAD_DIM)] = (
                dot_t(qt[rows], gscores) * score_scale
            ).astype(BF16)
            gqkvt[pl.ds(pl.multiple_of(2 * D + start, HEAD_DIM), HEAD_DIM)] = dot_t(low, probs[head]).astype(BF16)
        return carry

    lax.fori_loop(0, HEADS // 2, pair, 0)
    need(wqkv, x, m, ghidden)
    grows = dot(wqkv[...], gqkvt[...]).T
    grad_rows, gain_rows = layer_norm_back(x[...].astype(F32), gain, grows[:SEG_LEN])
    grad_slots, gain_slots = layer_norm_back(m[...].astype(F32), gain, grows[SEG_LEN:])
    grad_x[...] = (grad_rows + ghidden[...]).astype(BF16)
    grad_m[...] = grad_slots
    return gain_rows + gain_slots


def pack_row(block):
    if block < 8:
        return (block // 2) * PIECE + block % 2 * HALF
    return (block - 8) * PIECE + 2 * HALF


def halves(core):
    return [pl.ds(pl.multiple_of(side * HALF, HALF), HALF) for side in (core, 1 - core)]


def memory_weights(mover, core, kept, grads, packs, stage, act_t, nf_t, mixed_t, slots_t, n0_t, n1_t):
    n, kv, keyed, probs, inv, mixm, mixed, attended, hidden, nf, act, slope, branch = kept
    gb, gpre, ga, gq, gkv = grads

    def both(ref, *index):
        return jnp.concatenate([ref[(k,) + index] for k in range(SEGS)], axis=0)

    whole = slice(None)
    for block in range(4):
        span = slice(block * TILE, (block + 1) * TILE)
        act_t[span] = both(act, whole, span).T
    nf_t[...] = both(nf).T
    mixed_t[...] = both(mixed).T
    slots_t[...] = both(n, slice(SEG_LEN, ROWS)).T
    n0_t[...] = n[0].T
    n1_t[...] = n[1].T
    flying = [None] * BLOCKS
    for pack, rows in zip(packs, halves(core)):

        def put(block, value, pack=pack):
            if flying[block] is not None:
                mover.left(flying[block])
            stage[block] = value.astype(BF16)
            flying[block] = mover.send(stage.at[block], pack.at[pl.ds(pack_row(block), HALF)])

        for block in range(4):
            span = slice(block * TILE, (block + 1) * TILE)
            put(block, dot(act_t.at[span][rows], both(gb)))
            put(4 + block, dot(nf_t[rows], both(gpre, whole, span)))
        put(8, dot(mixed_t[rows], both(ga)))
        put(9, dot(slots_t[rows], both(gq)))
        for block in range(2):
            span = slice(block * TILE, (block + 1) * TILE)
            put(10 + block, dot(n0_t[rows], gkv[0, :, span]) + dot(n1_t[rows], gkv[1, :, span]))


def encoder_ffn_weights(need, core, acts, gbs, nfs, gpres, packs, left, left_nf):
    need(*gbs, *acts)

    def outer(block, carry):
        span = pl.ds(pl.multiple_of(block * TILE, TILE), TILE)
        for k in range(SEGS):
            left[k] = acts[k][:, span].T
        start = pl.multiple_of((block // 2) * PIECE + block % 2 * HALF, HALF)
        for pack, rows in zip(packs, halves(core)):
            pack[pl.ds(start, HALF)] = (
                dot(left[0, rows], gbs[0][...]) + dot(left[1, rows], gbs[1][...])
            ).astype(BF16)
        return carry

    lax.fori_loop(0, 4, outer, 0)
    need(*nfs, *gpres)
    for k in range(SEGS):
        left_nf[k] = nfs[k][...].T

    def inner(block, carry):
        span = pl.ds(pl.multiple_of(block * TILE, TILE), TILE)
        start = pl.multiple_of((2 + block // 2) * PIECE + block % 2 * HALF, HALF)
        for pack, rows in zip(packs, halves(core)):
            pack[pl.ds(start, HALF)] = (
                dot(left_nf[0, rows], gpres[0][:, span]) + dot(left_nf[1, rows], gpres[1][:, span])
            ).astype(BF16)
        return carry

    lax.fori_loop(0, 4, inner, 0)


def encoder_attention_weights(need, core, mixts, gas, ns, gqkvts, packs, left):
    need(*mixts, *gas)
    for pack, rows in zip(packs, halves(core)):
        pack[2 * HALF : PIECE] = (dot(mixts[0][rows], gas[0][...]) + dot(mixts[1][rows], gas[1][...])).astype(BF16)
    need(*ns, *gqkvts)
    for k in range(SEGS):
        left[k] = ns[k][...].T

    def third(block, carry):
        span = pl.ds(pl.multiple_of(block * TILE, TILE), TILE)
        start = pl.multiple_of((1 + block) * PIECE + 2 * HALF, HALF)
        for pack, rows in zip(packs, halves(core)):
            pack[pl.ds(start, HALF)] = (
                dot_t(left[0, rows], gqkvts[0][span]) + dot_t(left[1, rows], gqkvts[1][span])
            ).astype(BF16)
        return carry

    lax.fori_loop(0, 3, third, 0)


SCALAR = pl.BlockSpec(memory_space=pltpu.SMEM)
HELD = pl.BlockSpec(memory_space=pltpu.VMEM)
FAR = pl.BlockSpec(memory_space=pl.ANY)

WEIGHTS = (((D, 3 * D), BF16), ((D, D), BF16), ((D, FF), BF16), ((FF, D), BF16))
ROW_LOW = ((SEG_LEN, D), BF16)
ROW_FULL = ((SEG_LEN, D), F32)
WIDE = ((SEG_LEN, FF), BF16)
ALL_LOW = ((ROWS, D), BF16)
ALL_TURNED = ((D, ROWS), BF16)
TURNED = ((D, SEG_LEN), BF16)
SLOT_LOW = ((SLOTS, D), BF16)
SLOT_FULL = ((SLOTS, D), F32)
SLOT_WIDE = ((SLOTS, FF), BF16)
SLOT_TURNED = ((D, SEGS * SLOTS), BF16)
SQUARE = ((D, D), BF16)
PROBS = ((HEADS, ROWS, SEG_LEN), BF16)
INVERSE = ((HEADS, 1, SEG_LEN), F32)
KEYS_VALUES = ((ROWS, 2 * D), BF16)
GRAD_TURNED = ((3 * D, ROWS), BF16)
GAINS = ((8, D), F32)
BIAS = ((ROWS, 128), BF16)
EXTRAS = SLOTS + 16
PARCEL = BLOCKS * HALF + SEGS * SEG_LEN + SLOTS


def pack_of(blocks):
    return ((blocks * HALF, D), BF16)


def twice(item):
    return ((SEGS,) + item[0], item[1])


def call(body, kinds, outs, scratch, copies, name):
    out_kinds, outs = zip(*outs)
    specs = {"s": SCALAR, "v": HELD, "f": FAR}
    inputs = len(kinds)

    def kernel(*refs):
        ins, results = refs[:inputs], refs[inputs : inputs + len(outs)]
        held, sems = refs[inputs + len(outs) : -1], refs[-1]
        body(Mover(sems), ins, results, held)

    cost = pl.CostEstimate(flops=20_000_000_000, bytes_accessed=10_000_000, transcendentals=0)
    return pl.pallas_call(
        kernel,
        out_shape=[jax.ShapeDtypeStruct(shape, kind) for shape, kind in outs],
        in_specs=[specs[kind] for kind in kinds],
        out_specs=[specs[kind] for kind in out_kinds],
        scratch_shapes=[pltpu.VMEM(shape, kind) for shape, kind in scratch] + [pltpu.SemaphoreType.DMA((copies,))],
        compiler_params=pltpu.CompilerParams(vmem_limit_bytes=60 * 2**20),
        cost_estimate=cost,
        name=name,
    )


def own_gains(own, other, front):
    return jnp.where(front, own[...], other[...])


def document_rows(core, segment):
    return pl.ds(pl.multiple_of((core * SEGS + segment) * SEG_LEN, SEG_LEN), SEG_LEN)


def column_halves(core):
    return [pl.ds(pl.multiple_of(side * (D // 2), D // 2), D // 2) for side in (core, 1 - core)]


def first_kernel(mover, ins, outs, held):
    tokens, m, gains_own, gains_other, qkv_own, qkv_other, proj_own, proj_other = ins
    x, n, qt, kv, probs, inv, mixt, hidden, vt, wqkv, wproj, bias = held
    core = lax.axis_index("pipe")
    gains = own_gains(gains_own, gains_other, core == 0)
    bias[...] = jnp.zeros_like(bias)
    mover.bring(x, tokens.at[document_rows(core, 0)])
    mover.bring_either(wqkv, core == 0, qkv_own, qkv_other)
    mover.bring_either(wproj, core == 0, proj_own, proj_other)
    encoder_attention(mover.need, x, m, bias, gains[0:1], wqkv, wproj, n, qt, kv, vt, probs, inv, mixt, hidden)
    for source, target in zip((hidden, n, qt, kv, probs, inv, mixt), outs):
        mover.send(source, target)
    mover.finish()


FIRST = (ROW_FULL, ALL_LOW, TURNED, KEYS_VALUES, PROBS, INVERSE, TURNED)


def first_call(tokens, m, gains, weights):
    return call(
        first_kernel,
        "fvvvffff",
        [("f", item) for item in FIRST],
        [ROW_LOW, ALL_LOW, TURNED, KEYS_VALUES, PROBS, INVERSE, TURNED, ROW_FULL, ALL_TURNED, WEIGHTS[0], WEIGHTS[1], BIAS],
        10,
        "encoder_attention",
    )(tokens, m, *gains, *weights[0], *weights[1])


MEMORY_KEPT = (
    ALL_LOW, KEYS_VALUES, SQUARE, ALL_LOW, ((1, D), F32), SQUARE, SLOT_LOW, SLOT_FULL, SLOT_FULL,
    SLOT_LOW, SLOT_WIDE, SLOT_WIDE, SLOT_FULL,
)
MEMORY_GRADS = (SLOT_LOW, SLOT_WIDE, SLOT_LOW, SLOT_LOW, KEYS_VALUES)


def middle_kernel(mover, ins, outs, held):
    lengths, m0, gains_own, gains_other, cot_memory, hidden0, tokens, cots = ins[:8]
    pairs = ins[8:]
    (parcel, mine, out_nf, out_act, out_slope, out_n, out_mixt, out_gb, out_ga, out_gqkvt, out_grad_y, out_grad_x,
     out_grad_m, out_gains) = outs
    theirs = parcel.at[pl.ds(0, BLOCKS * HALF)]
    out_y = [parcel.at[pl.ds(BLOCKS * HALF + k * SEG_LEN, SEG_LEN)] for k in range(SEGS)]
    out_final = parcel.at[pl.ds(BLOCKS * HALF + SEGS * SEG_LEN, SLOTS)]
    enc_weights, mem_weights, held = held[:4], held[4:8], held[8:]
    kept, held = held[: len(MEMORY_KEPT)], held[len(MEMORY_KEPT) :]
    grads, held = held[: len(MEMORY_GRADS)], held[len(MEMORY_GRADS) :]
    (x, cot, cot_slots, hidden, n, qt, kv, probs, inv, mixt, nf, act, slope, y0, y1, turned, total, gnf, gmt, gb, ga,
     gqkvt, grad_y, grad_x, m1, final, grad_m, grad_m1, stage, act_t, nf_t, mixed_t, slots_t, bias) = held
    core = lax.axis_index("pipe")
    front = core == 0
    enc_gains = own_gains(gains_own, gains_other, front)
    mem_gains = own_gains(gains_other, gains_own, front)
    valid_rows = lengths[core] - SEG_LEN
    lanes = iota(BIAS[0], 1) % HEAD_DIM == 0
    bias[...] = jnp.where(lanes & ~valid_keys(BIAS[0], valid_rows), masked_bias, 0.0).astype(BF16)
    need = mover.need
    wqkv, wproj, win, wout = enc_weights
    mover.bring(hidden, hidden0)
    for index in (2, 3):
        mover.bring_either(enc_weights[index], front, *pairs[2 * index : 2 * index + 2])
    for index in range(4):
        own, other = pairs[2 * index : 2 * index + 2]
        mover.bring_either(mem_weights[index], front, other, own)
    mover.bring(x, tokens.at[document_rows(core, 1)])
    for index in (0, 1):
        mover.bring_either(enc_weights[index], front, *pairs[2 * index : 2 * index + 2])
    mover.bring(cot_slots, cot_memory.at[core])
    mover.bring(cot, cots.at[document_rows(core, 1)])
    enc_attn, enc_ffn = enc_gains[0:1], enc_gains[1:2]
    mem_attn, mem_ffn = mem_gains[0:1], mem_gains[1:2]

    encoder_ffn(need, hidden, enc_ffn, win, wout, y0, nf, act, slope, total)
    mover.send(y0, out_y[0])
    early = [mover.send(nf, out_nf.at[0]), mover.send(act, out_act.at[0]), mover.send(slope, out_slope.at[0])]
    memory_forward(need, y0, m0, None, mem_attn, mem_ffn, mem_weights, m1, kept, 0, turned)
    encoder_attention(need, x, m1, bias, enc_attn, wqkv, wproj, n, qt, kv, turned, probs, inv, mixt, hidden)
    mover.send(n, out_n)
    mover.send(mixt, out_mixt)
    mover.left(*early)
    encoder_ffn(need, hidden, enc_ffn, win, wout, y1, nf, act, slope, total)
    mover.send(y1, out_y[1])
    mover.send(nf, out_nf.at[1])
    mover.send(act, out_act.at[1])
    memory_forward(need, y1, m1, valid_rows, mem_attn, mem_ffn, mem_weights, final, kept, 1, turned)
    mover.send(final, out_final)

    need(cot_slots)
    attn_gain1, ffn_gain1 = memory_backward(
        cot_slots, y1, m1, mem_attn, mem_ffn, mem_weights, kept, 1, grad_y, grad_m, grads
    )
    out_gains[1:2] = encoder_ffn_backward(need, cot, grad_y, hidden, enc_ffn, win, wout, slope, gb, gnf, ga, total)
    mover.send(gb, out_gb)
    mover.send(ga, out_ga)
    mover.send(slope, out_slope.at[1])
    out_gains[0:1] = encoder_attention_backward(
        need, x, m1, enc_attn, wqkv, wproj, qt, kv, probs, inv, mixt, ga, total, turned, gmt, gqkvt, grad_x, grad_m1
    )
    turned_out = mover.send(gqkvt, out_gqkvt)
    mover.send(grad_x, out_grad_x)
    grad_m[...] = grad_m[...] + grad_m1[...].astype(BF16).astype(F32)
    attn_gain0, ffn_gain0 = memory_backward(
        grad_m, y0, m0, mem_attn, mem_ffn, mem_weights, kept, 0, grad_y, out_grad_m, grads
    )
    mover.send(grad_y, out_grad_y)
    out_gains[2:3] = attn_gain0 + attn_gain1
    out_gains[3:4] = ffn_gain0 + ffn_gain1
    out_gains[4:8] = jnp.zeros((4, D), F32)
    mover.left(turned_out)
    memory_weights(
        mover, core, kept, grads, (mine, theirs), stage, act_t, nf_t, mixed_t, slots_t,
        gqkvt.at[pl.ds(0, D)], gqkvt.at[pl.ds(D, D)],
    )
    mover.finish()


def middle_call(lengths, m0, gains, cot_memory, hidden, tokens, cots, weights):
    outs = [
        ("f", ((PARCEL, D), BF16)), ("f", pack_of(BLOCKS)), ("f", twice(ROW_LOW)), ("f", twice(WIDE)),
        ("f", twice(WIDE)), ("f", ALL_LOW), ("f", TURNED), ("f", ROW_LOW), ("f", ROW_LOW), ("f", GRAD_TURNED),
        ("f", ROW_LOW), ("f", ROW_LOW), ("v", SLOT_FULL), ("v", GAINS),
    ]
    scratch = [
        *WEIGHTS, *WEIGHTS, *[twice(item) for item in MEMORY_KEPT], *[twice(item) for item in MEMORY_GRADS],
        ROW_LOW, ROW_LOW, SLOT_LOW, ROW_FULL, ALL_LOW, TURNED, KEYS_VALUES, PROBS, INVERSE, TURNED, ROW_LOW, WIDE,
        WIDE, ROW_LOW, ROW_LOW, ALL_TURNED, ROW_FULL, ROW_FULL, TURNED, ROW_LOW, ROW_LOW, GRAD_TURNED, ROW_LOW,
        ROW_LOW, SLOT_LOW, SLOT_LOW, SLOT_FULL, SLOT_FULL, ((BLOCKS, HALF, D), BF16), ((FF, SEGS * SLOTS), BF16),
        SLOT_TURNED, SLOT_TURNED, SLOT_TURNED, BIAS,
    ]
    return call(middle_kernel, "svvvffff" + "f" * 8, outs, scratch, 64, "middle")(
        lengths, m0, *gains, cot_memory, hidden, tokens, cots,
        *[item for pair in weights for item in pair],
    )


def feed_kernel(mover, ins, outs, held):
    gains_own, gains_other, grad_gains, cots, grad_y0, hidden0, slopes, in_own, in_other, out_own, out_other = ins
    out_gpre, out_gb, out_ga, out_ghidden, out_gains = outs
    win, wout, cot, grad_y, hidden, gpre, gb, gnf, ga, ghidden = held
    core = lax.axis_index("pipe")
    gains = own_gains(gains_own, gains_other, core == 0)
    mover.bring(cot, cots.at[document_rows(core, 0)])
    mover.bring(grad_y, grad_y0)
    mover.bring_either(wout, core == 0, out_own, out_other)
    mover.bring(gpre, slopes.at[0])
    mover.bring_either(win, core == 0, in_own, in_other)
    mover.bring(hidden, hidden0)
    gain_grad = encoder_ffn_backward(
        mover.need, cot, grad_y, hidden, gains[1:2], win, wout, gpre, gb, gnf, ga, ghidden
    )
    for source, target in ((gpre, out_gpre), (gb, out_gb), (ga, out_ga), (ghidden, out_ghidden)):
        mover.send(source, target)
    out_gains[...] = grad_gains[...]
    out_gains[1:2] = grad_gains[1:2] + gain_grad
    mover.finish()


def feed_call(gains, grad_gains, cots, grad_y, hidden, slopes, weights):
    return call(
        feed_kernel,
        "vvvffffffff",
        [("f", WIDE), ("f", ROW_LOW), ("f", ROW_LOW), ("f", ROW_FULL), ("v", GAINS)],
        [WEIGHTS[2], WEIGHTS[3], ROW_LOW, ROW_LOW, ROW_FULL, WIDE, ROW_LOW, ROW_FULL, ROW_LOW, ROW_FULL],
        10,
        "encoder_feed",
    )(*gains, grad_gains, cots, grad_y, hidden, slopes, *weights[2], *weights[3])


def last_kernel(mover, ins, outs, held):
    acts, slopes, nfs, gpre0, gb0, gb1 = ins[:6]
    (m0, gains_own, gains_other, grad_gains, grad_m, tokens, qt0, kv0, probs0, inv0, mixt0, ga0, ghidden0, grad_x1,
     n0, n1, mixt1, ga1, gqkvt1, qkv_own, qkv_other, proj_own, proj_other) = ins[6:]
    mine, out_keep, parcel, *sooner = outs
    act_held, nf_held, gpre_held, gb_held, left_nf, left_n = held[0:2], held[2:4], held[4:6], held[6:8], held[8], held[9]
    (wqkv, wproj, x, qt, kv, probs, inv, mixt, ga, ghidden, gqkvt, kt, gmt, grad_x, grad_x1_held, grad_m0,
     extras, mine_held, theirs_held, n0_held, n1_held, mixt1_held, ga1_held, gqkvt1_held, left) = held[10:]
    core = lax.axis_index("pipe")
    gains = own_gains(gains_own, gains_other, core == 0)
    packs = (mine_held, theirs_held)
    for target, source in zip(gb_held, (gb0, gb1)):
        mover.bring(target, source)
    for k in range(SEGS):
        mover.bring(act_held[k], acts.at[k])
    for k in range(SEGS):
        mover.bring(nf_held[k], nfs.at[k])
    mover.bring(gpre_held[0], gpre0)
    mover.bring(gpre_held[1], slopes.at[1])
    mover.bring_either(wproj, core == 0, proj_own, proj_other)
    mover.bring(ga, ga0)
    mover.bring(kv, kv0)
    mover.bring(inv, inv0)
    mover.bring(mixt, mixt0)
    mover.bring(qt, qt0)
    mover.bring(probs, probs0)
    mover.bring_either(wqkv, core == 0, qkv_own, qkv_other)
    mover.bring(x, tokens.at[document_rows(core, 0)])
    mover.bring(ghidden, ghidden0)
    mover.bring(grad_x1_held, grad_x1)
    mover.bring(mixt1_held, mixt1)
    mover.bring(ga1_held, ga1)
    mover.bring(n0_held, n0)
    mover.bring(n1_held, n1)
    mover.bring(gqkvt1_held, gqkvt1)
    need = mover.need
    encoder_ffn_weights(need, core, act_held, gb_held, nf_held, gpre_held, packs, left, left_nf)
    gain_grad = encoder_attention_backward(
        need, x, m0, gains[0:1], wqkv, wproj, qt, kv, probs, inv, mixt, ga, ghidden, kt, gmt, gqkvt, grad_x, grad_m0
    )
    extras[:SLOTS] = (grad_m[...] + grad_m0[...]).astype(BF16)
    low = jnp.concatenate(
        [grad_gains[0:1] + gain_grad, grad_gains[1:4], jnp.zeros((EXTRAS - SLOTS - 4, D), F32)], axis=0
    )
    extras[SLOTS:] = low.astype(BF16)
    mover.send(extras, sooner[0].at[pl.ds(PIECE // 2, EXTRAS)])
    keep, give = column_halves(core)
    for segment, source in enumerate((grad_x, grad_x1_held)):
        need(source)
        columns = pl.ds(segment * (D // 2), D // 2)
        mover.send(source.at[:, keep], out_keep.at[:, columns])
        mover.send(source.at[:, give], parcel.at[pl.ds(2 * PIECE, SEG_LEN), columns])
    encoder_attention_weights(
        need, core, (mixt, mixt1_held), (ga, ga1_held), (n0_held, n1_held), (gqkvt, gqkvt1_held), packs, left_n
    )
    device = lax.axis_index("dp")
    for part in range(2):
        stays = (device >> part) & 1
        goes = pl.multiple_of((2 * part + 1 - stays) * PIECE, PIECE)
        stays = pl.multiple_of((2 * part + stays) * PIECE, PIECE)
        for k in range(2):
            mover.send(
                theirs_held.at[pl.ds(goes + k * (PIECE // 2), PIECE // 2)],
                sooner[2 * part + k].at[pl.ds(0, PIECE // 2)],
            )
        mover.send(mine_held.at[pl.ds(goes, PIECE)], mine.at[pl.ds(part * PIECE, PIECE)])
        mover.send(mine_held.at[pl.ds(stays, PIECE)], mine.at[pl.ds((2 + part) * PIECE, PIECE)])
        mover.send(theirs_held.at[pl.ds(stays, PIECE)], parcel.at[pl.ds(part * PIECE, PIECE)])
    mover.finish()


LAST_PARCEL = 2 * PIECE + SEG_LEN


def last_call(
    acts, slopes, nfs, gpre0, gb0, gb1, m0, gains, grad_gains, grad_m, tokens, qt0, kv0, probs0, inv0, mixt0, ga0,
    ghidden0, grad_x1, n0, n1, mixt1, ga1, gqkvt1, weights,
):
    return call(
        last_kernel,
        "ffffff" + "vvvvv" + "f" * 18,
        [("f", pack_of(BLOCKS)), ("f", ROW_LOW), ("f", ((LAST_PARCEL, D), BF16))]
        + [("f", ((PIECE // 2 + (0 if k else EXTRAS), D), BF16)) for k in range(4)],
        [
            WIDE, WIDE, ROW_LOW, ROW_LOW, WIDE, WIDE, ROW_LOW, ROW_LOW, twice(SQUARE), twice(ALL_TURNED),
            WEIGHTS[0], WEIGHTS[1], ROW_LOW, TURNED, KEYS_VALUES, PROBS, INVERSE, TURNED, ROW_LOW, ROW_FULL,
            GRAD_TURNED, ALL_TURNED, TURNED, ROW_LOW, ROW_LOW, SLOT_FULL, ((EXTRAS, D), BF16), pack_of(BLOCKS),
            pack_of(BLOCKS), ALL_LOW, ALL_LOW, TURNED, ROW_LOW, GRAD_TURNED, twice(SQUARE),
        ],
        41,
        "encoder_last",
    )(
        acts, slopes, nfs, gpre0, gb0, gb1, m0, *gains, grad_gains, grad_m, tokens, qt0, kv0, probs0, inv0, mixt0,
        ga0, ghidden0, grad_x1, n0, n1, mixt1, ga1, gqkvt1, *weights[0], *weights[1],
    )


def assemble_kernel(mover, ins, outs, held):
    parcel, parcel_other, keep0, last_other = ins
    activations, final_memory, grad_tokens = outs
    core = lax.axis_index("pipe")
    rows = SEGS * SEG_LEN
    start = BLOCKS * HALF
    for source, y, final in zip((parcel, parcel_other), held[0:2], held[2:4]):
        mover.bring(y, source.at[pl.ds(start, rows)])
        mover.bring(final, source.at[pl.ds(start + rows, SLOTS)])
    keep, give = held[4:6]
    mover.bring(keep, keep0)
    mover.bring(give, last_other.at[pl.ds(2 * PIECE, SEG_LEN)])
    for document, y, final, grads in zip((core, 1 - core), held[0:2], held[2:4], held[4:6]):
        mover.need(y, final, grads)
        mover.send(y, activations.at[pl.ds(pl.multiple_of(document * rows, rows), rows)])
        mover.send(final, final_memory.at[document])
        for segment in range(SEGS):
            columns = grads.at[:, pl.ds(segment * (D // 2), D // 2)]
            mover.send(columns, grad_tokens.at[document_rows(document, segment)])
    mover.finish()


def assemble_call(*operands):
    rows = 2 * SEGS * SEG_LEN
    outs = [("f", ((rows, D), BF16)), ("f", ((2, SLOTS, D), BF16)), ("f", ((rows, D // 2), BF16))]
    y = ((SEGS * SEG_LEN, D), BF16)
    return call(
        assemble_kernel, "ffff", outs, [y, y, SLOT_LOW, SLOT_LOW, ROW_LOW, ROW_LOW], 16, "assemble"
    )(*operands)


def place_block(block):
    if block < 4:
        return 0, lambda row: (pl.ds(block * TILE + row, HALF), slice(None))
    if block < 8:
        return 1, lambda row: (pl.ds(row, HALF), slice((block - 4) * TILE, (block - 3) * TILE))
    if block == 8:
        return 2, lambda row: (pl.ds(row, HALF), slice(None))
    return 3, lambda row: (pl.ds(row, HALF), slice((block - 9) * TILE, (block - 8) * TILE))


def unpack_kernel(mover, ins, outs, held):
    sources = ins[:4], ins[4:8], ins[8:12], ins[12:16]
    pieces, wide = held
    core = lax.axis_index("pipe")
    device = lax.axis_index("dp")
    for side in range(2):
        for part in range(2):
            near = (device >> part) & 1
            for distance in range(2):
                place = 4 * side + 2 * part + (near if distance == 0 else 1 - near)
                index = 2 * part + distance
                mover.bring_either(
                    pieces.at[place], core == 0, sources[side][index], sources[2 + side][index]
                )
    arrivals = list(mover.coming.values())
    for side in range(2):
        row = pl.multiple_of((core if side == 0 else 1 - core) * HALF, HALF)
        for copy in arrivals[4 * side : 4 * side + 4]:
            pltpu.make_async_copy(*copy).wait()
        for block in range(BLOCKS):
            start = pack_row(block)
            piece, first = 4 * side + start // PIECE, start % PIECE
            wide[side, block] = pieces[piece, first : first + HALF].astype(F32)
            which, spot = place_block(block)
            mover.send(wide.at[side, block], outs[which].at[spot(row)])
    mover.finish()


def unpack_call(*operands):
    outs = [("f", ((FF, D), F32)), ("f", ((D, FF), F32)), ("f", ((D, D), F32)), ("f", ((D, 3 * D), F32))]
    return call(
        unpack_kernel, "f" * 16, outs, [((8, PIECE, D), BF16), ((2, BLOCKS, HALF, D), F32)], 8 + 2 * BLOCKS, "unpack"
    )(*operands)


def swap(block):
    return lax.ppermute(block, "pipe", [(0, 1), (1, 0)])


def neighbour(block, bit):
    devices = lax.axis_size("dp")
    return lax.ppermute(block, "dp", [(k, k ^ (1 << bit)) for k in range(devices)])


def bit_of(bit):
    return (lax.axis_index("dp") >> bit) & 1


def after(value, *others):
    return lax.optimization_barrier((value,) + others)[0]


def rows_of(block, start, size):
    return lax.dynamic_slice_in_dim(block, start, size)


def total_of(blocks):
    return sum(block.astype(F32) for block in blocks).astype(BF16)


class Part:
    def __init__(self, size, pieces):
        self.size = size
        self.pieces = pieces

    def sum_of(self, shift, size):
        return total_of([rows_of(array, start + shift, size) for array, start in self.pieces])

    def value(self):
        return self.sum_of(0, self.size)


class Line:
    def __init__(self):
        self.last = None

    def send(self, block, bit):
        if self.last is not None:
            block = after(block, self.last)
        self.last = block
        return neighbour(block, bit)

    def trade(self, part, bit, extra=None):
        half = part.size // 2
        give = part.sum_of((1 - bit_of(bit)) * half, half)
        if extra is not None:
            give = jnp.concatenate([give, extra], axis=0)
        return self.send(give, bit)


def settle(part, bit, came):
    half = part.size // 2
    shift = bit_of(bit) * half
    return Part(half, [(array, start + shift) for array, start in part.pieces] + [(came, 0)])


def join(block, came, bit):
    low = bit_of(bit) == 0
    return jnp.concatenate([jnp.where(low, block, came), jnp.where(low, came, block)], axis=0)


def local(
    tokens, lengths, memory_init, attn_gain, qkv_weight, proj_weight, ffn_gain, in_weight, out_weight,
    cot_tokens, cot_memory,
):
    core = lax.axis_index("pipe")
    front = core == 0
    gains = jnp.concatenate([attn_gain, ffn_gain], axis=0)
    gains = (gains, swap(gains))
    weights = [(held[0], swap(held[0])) for held in (qkv_weight, proj_weight, in_weight, out_weight)]

    hidden0, n0, qt0, kv0, probs0, inv0, mixt0 = first_call(tokens, memory_init, gains, weights)
    (parcel, mem_mine, nfs, acts, slopes, n1, mixt1, gb1, ga1, gqkvt1, grad_y0, grad_x1, grad_m,
     grad_gains) = middle_call(lengths, memory_init, gains, cot_memory, hidden0, tokens, cot_tokens, weights)
    parcel_other = swap(parcel)
    gpre0, gb0, ga0, ghidden0, grad_gains = feed_call(
        gains, grad_gains, cot_tokens, grad_y0, hidden0, slopes, weights
    )

    bits = lax.axis_size("dp").bit_length() - 1
    line = Line()
    both = range(2)
    parcel_other, gb0 = lax.optimization_barrier((parcel_other, gb0))
    mem = [Part(2 * PIECE, [(mem_mine, k * 2 * PIECE), (parcel_other, k * 2 * PIECE)]) for k in both]
    mem_came = [line.trade(mem[k], k) for k in both]
    enc_mine, out_keep, last_parcel, *sooner = last_call(
        acts, slopes, nfs, gpre0, after(gb0, line.last), gb1, memory_init, gains, grad_gains, grad_m, tokens, qt0, kv0,
        probs0, inv0, mixt0, ga0, ghidden0, grad_x1, n0, n1, mixt1, ga1, gqkvt1, weights,
    )
    sooner_other = [swap(block) for block in sooner]
    last_other = swap(last_parcel)
    *mem_came, enc_mine = lax.optimization_barrier((*mem_came, enc_mine))
    mem = [settle(mem[k], k, mem_came[k]) for k in both]
    mem_came = [line.trade(mem[k], 1 - k) for k in both]
    quarter = PIECE // 2
    rest = list(range(2, bits))

    def merged(parts, came):
        kept = [settle(parts[k], 1 - k, came[k]).value() for k in both]
        return Part(2 * quarter, [(jnp.concatenate(kept, axis=0), 0)])

    def split(block):
        return [block[k * quarter : (k + 1) * quarter] for k in both]

    half = PIECE // 2
    gives = [
        jnp.concatenate(
            [total_of([rows_of(enc_mine, k * PIECE + j * half, half), sooner_other[2 * k + j][:half]]) for j in both], axis=0
        )
        for k in both
    ]
    extras = total_of([block[half:] for block in (sooner[0], sooner_other[0])])
    enc_came = [line.send(jnp.concatenate([gives[0], extras], axis=0), 0), line.send(gives[1], 1)]
    mem = merged(mem, mem_came)
    for bit in rest:
        mem = settle(mem, bit, line.trade(mem, bit))
    mem = mem.value()
    enc = [
        Part(PIECE, [(enc_mine, (2 + k) * PIECE), (last_other, k * PIECE), (enc_came[k], 0)]) for k in both
    ]
    extras = total_of([extras, enc_came[0][PIECE:]])
    enc_came = [line.trade(enc[0], 1, extras), line.trade(enc[1], 0)]
    for bit in rest[:0:-1]:
        mem = join(mem, line.send(mem, bit), bit)
    enc = merged(enc, enc_came)
    extras = total_of([extras, enc_came[0][quarter:]])
    for bit in rest:
        came = line.trade(enc, bit, extras)
        extras = total_of([extras, came[enc.size // 2 :]])
        enc = settle(enc, bit, came)
        if bit == rest[0]:
            mem = join(mem, line.send(mem, bit), bit)
            mem_parts = split(mem)
    enc = enc.value()
    mem_came = [line.send(mem_parts[k], 1 - k) for k in both]
    for bit in rest[::-1]:
        if bit == rest[0]:
            mem_near = [join(mem_parts[k], mem_came[k], 1 - k) for k in both]
            mem_far = [line.send(mem_near[k], k) for k in both]
        enc = join(enc, line.send(enc, bit), bit)
    enc_parts = split(enc)
    enc_came = [line.send(enc_parts[k], 1 - k) for k in both]
    enc_near = [join(enc_parts[k], enc_came[k], 1 - k) for k in both]
    enc_far = [line.send(enc_near[k], k) for k in both]

    def ordered(near, far):
        own = [block for k in both for block in (near[k], far[k])]
        return own, [swap(block) for block in own]

    enc_own, enc_other = ordered(enc_near, enc_far)
    mem_own, mem_other = ordered(mem_near, mem_far)
    grad_out, grad_in, grad_proj, grad_qkv = unpack_call(*enc_own, *enc_other, *mem_own, *mem_other)
    extras = extras.astype(F32)
    gain_grads = jnp.where(front, extras[SLOTS : SLOTS + 2], extras[SLOTS + 2 : SLOTS + 4])
    activations, final_memory, grad_tokens = assemble_call(parcel, parcel_other, out_keep, last_other)
    return (
        activations,
        final_memory,
        grad_tokens,
        extras[:SLOTS],
        gain_grads[0:1],
        grad_qkv[None],
        grad_proj[None],
        gain_grads[1:2],
        grad_in[None],
        grad_out[None],
    )


def solution(mesh):
    placed = (
        P("dp", None),
        P("dp"),
        P(),
        P("pipe", None),
        P("pipe", None, None),
        P("pipe", None, None),
        P("pipe", None),
        P("pipe", None, None),
        P("pipe", None, None),
        P("dp", None),
        P("dp", None, None),
    )
    return jax.shard_map(
        local,
        mesh=mesh,
        in_specs=placed,
        out_specs=(
            P("dp", None),
            P("dp", None, None),
            P("dp", "pipe"),
            P(),
            P("pipe", None),
            P("pipe", None, None),
            P("pipe", None, None),
            P("pipe", None),
            P("pipe", None, None),
            P("pipe", None, None),
        ),
        check_vma=False,
    )
```

```python
import jax
import jax.numpy as jnp
from jax import lax
from jax.experimental import pallas as pl
from jax.experimental.pallas import tpu as pltpu
from jax.sharding import PartitionSpec as P

D = 512
HEADS = 8
HEAD_DIM = 64
FF = 2048
SLOTS = 64
SEG_LEN = 512
SEGS = 2
ROWS = SEG_LEN + SLOTS
TILE = 512
BLOCKS = 12
HALF = TILE // 2
PIECE = 3 * HALF

epsilon = 1e-05
masked_bias = -1000000000.0
score_scale = HEAD_DIM ** (-0.5)
exponent_scale = score_scale * 1.4426950408889634
gelu_a = 0.7978845608028654
gelu_b = 0.044715 * gelu_a

BF16 = jnp.bfloat16
F32 = jnp.float32


def dot(left, right):
    return jnp.dot(left, right, preferred_element_type=F32)


def dot_t(left, right):
    return lax.dot_general(left, right, (((1,), (1,)), ((), ())), preferred_element_type=F32)


def normalise(values):
    centred = values - jnp.mean(values, axis=-1, keepdims=True)
    spread = jnp.mean(centred * centred, axis=-1, keepdims=True)
    inverse = lax.rsqrt(spread + epsilon)
    return centred * inverse, inverse


def layer_norm(values, gain):
    return normalise(values)[0] * gain


def layer_norm_back(values, gain, grads):
    scaled, inverse = normalise(values)
    gain_grad = jnp.sum(grads * scaled, axis=0, keepdims=True)
    inner = grads * gain
    mean_inner = jnp.mean(inner, axis=-1, keepdims=True)
    mean_scaled = jnp.mean(inner * scaled, axis=-1, keepdims=True)
    return inverse * (inner - mean_inner - scaled * mean_scaled), gain_grad


def gelu_both(values):
    square = values * values
    tangent = jnp.tanh(values * (gelu_a + gelu_b * square))
    half = 0.5 + 0.5 * tangent
    slope = half + (0.5 * values) * (1.0 - tangent * tangent) * (gelu_a + 3.0 * gelu_b * square)
    return values * half, slope


def iota(shape, dim):
    return lax.broadcasted_iota(jnp.int32, shape, dim)


def repeat_matrix():
    return (iota((SLOTS, D), 0) == iota((SLOTS, D), 1) % SLOTS).astype(BF16)


def head_blocks():
    return iota((D, D), 0) // HEAD_DIM == iota((D, D), 1) // SLOTS


class Mover:
    def __init__(self, sems):
        self.sems = sems
        self.used = 0
        self.coming = {}
        self.leaving = []

    def slot(self):
        self.used += 1
        return self.sems.at[self.used - 1]

    def bring(self, target, source):
        sem = self.slot()
        pltpu.make_async_copy(source, target, sem).start()
        self.coming[id(target)] = (source, target, sem)

    def bring_either(self, target, pick_first, first, second):
        sem = self.slot()

        @pl.when(pick_first)
        def _():
            pltpu.make_async_copy(first, target, sem).start()

        @pl.when(jnp.logical_not(pick_first))
        def _():
            pltpu.make_async_copy(second, target, sem).start()

        self.coming[id(target)] = (first, target, sem)

    def need(self, *targets):
        for target in targets:
            if id(target) in self.coming:
                pltpu.make_async_copy(*self.coming.pop(id(target))).wait()

    def send(self, source, target):
        copy = pltpu.make_async_copy(source, target, self.slot())
        copy.start()
        self.leaving.append(copy)
        return copy

    def left(self, *copies):
        for copy in copies:
            copy.wait()
            self.leaving = [other for other in self.leaving if other is not copy]

    def finish(self):
        for copy in self.leaving:
            copy.wait()


def valid_keys(shape, valid_rows):
    row = iota(shape, 0)
    return (row < valid_rows) | (row >= SEG_LEN)


def encoder_attention(
    need, x, m, bias, gain, wqkv, wproj, n, qt, kv, vt, probs, inv, mixt, hidden, ready=lambda *refs: None
):
    need(x, m)
    n[:SEG_LEN] = layer_norm(x[...].astype(F32), gain).astype(BF16)
    n[SEG_LEN:] = layer_norm(m[...].astype(F32), gain).astype(BF16)
    need(wqkv)
    qt[...] = dot_t(wqkv[:, :D].T, n[:SEG_LEN]).astype(BF16)
    kv[:, :D] = dot(n[...], wqkv[:, D : 2 * D]).astype(BF16)
    values = dot(n[...], wqkv[:, 2 * D :]).astype(BF16)
    kv[:, D:] = values
    vt[...] = values.T
    ready(n, qt, kv)
    low_lanes = iota((ROWS, 128), 1) < HEAD_DIM
    ones_row = (iota((HEAD_DIM, SEG_LEN), 0) == 0).astype(BF16)

    def pair(index, carry):
        base = pl.multiple_of(index * 128, 128)
        keys = kv[:, pl.ds(base, 128)]
        for half in range(2):
            head = 2 * index + half
            rows = pl.ds(pl.multiple_of(base + half * HEAD_DIM, HEAD_DIM), HEAD_DIM)
            queries = qt[rows]
            if half == 0:
                left = jnp.where(low_lanes, keys, bias[...])
                right = jnp.concatenate([queries, ones_row], axis=0)
            else:
                left = jnp.where(low_lanes, bias[...], keys)
                right = jnp.concatenate([ones_row, queries], axis=0)
            scores = dot(left, right)
            top = jnp.max(scores, axis=0, keepdims=True)
            grown = jnp.exp2(scores * exponent_scale - top * exponent_scale)
            inverse = 1.0 / jnp.sum(grown, axis=0, keepdims=True)
            low = grown.astype(BF16)
            probs[head] = low
            inv[head] = inverse
            mixt[rows] = (dot(vt[rows], low) * inverse).astype(BF16)
        return carry

    lax.fori_loop(0, HEADS // 2, pair, 0)
    ready(probs, inv, mixt)
    need(wproj)
    hidden[...] = x[...].astype(F32) + dot(mixt[...].T, wproj[...])
    ready(hidden)


def encoder_ffn(need, hidden, gain, win, wout, y, nf, act, slope, total):
    need(hidden)
    nf[...] = layer_norm(hidden[...], gain).astype(BF16)
    total[...] = hidden[...]
    need(win, wout)

    def step(index, carry):
        span = pl.ds(pl.multiple_of(index * TILE, TILE), TILE)
        active, grad = gelu_both(dot(nf[...], win[:, span]))
        low = active.astype(BF16)
        act[:, span] = low
        slope[:, span] = grad.astype(BF16)
        total[...] += dot(low, wout[span])
        return carry

    lax.fori_loop(0, FF // TILE, step, 0)
    y[...] = total[...].astype(BF16)


def memory_forward(need, y, m, valid_rows, gain, ffn_gain, weights, result, kept, index, vt):
    wqkv, wproj, win, wout = weights
    n, kv, keyed, probs, inv, mixm, mixed, attended, hidden, nf, act, slope, branch = [ref.at[index] for ref in kept]
    need(m)
    mf = m[...].astype(F32)
    n[:SEG_LEN] = layer_norm(y[...].astype(F32), gain).astype(BF16)
    slots = layer_norm(mf, gain).astype(BF16)
    n[SEG_LEN:] = slots
    need(wqkv)
    kv[:, :D] = dot(n[...], wqkv[:, D : 2 * D]).astype(BF16)
    values = dot(n[...], wqkv[:, 2 * D :]).astype(BF16)
    kv[:, D:] = values
    vt[...] = values.T
    blocks = head_blocks()
    queries = dot_t(wqkv[:, :D].T, jnp.concatenate([slots] * HEADS, axis=0))
    keyed[...] = jnp.where(blocks, queries, 0.0).astype(BF16)
    scores = dot(kv[:, :D], keyed[...])
    if valid_rows is not None:
        scores = jnp.where(valid_keys((ROWS, D), valid_rows), scores, masked_bias)
    top = jnp.max(scores, axis=0, keepdims=True)
    grown = jnp.exp2(scores * exponent_scale - top * exponent_scale)
    inverse = 1.0 / jnp.sum(grown, axis=0, keepdims=True)
    probs[...] = grown.astype(BF16)
    inv[...] = inverse
    mixm[...] = jnp.where(blocks, dot(vt[...], probs[...]) * inverse, 0.0).astype(BF16)
    mixed[...] = dot_t(repeat_matrix(), mixm[...]).astype(BF16)
    need(wproj)
    attended[...] = dot(mixed[...], wproj[...])
    hidden[...] = mf + attended[...]
    nf[...] = layer_norm(hidden[...], ffn_gain).astype(BF16)
    need(win)
    active, grad = gelu_both(dot(nf[...], win[...]))
    act[...] = active.astype(BF16)
    slope[...] = grad.astype(BF16)
    need(wout)
    branch[...] = dot(act[...], wout[...])
    result[...] = (mf + jax.nn.sigmoid(branch[...]) * attended[...]).astype(BF16)


def memory_backward(go, y, m, gain, ffn_gain, weights, kept, index, grad_y, grad_m, grads):
    wqkv, wproj, win, wout = weights
    n, kv, keyed, probs, inv, mixm, mixed, attended, hidden, nf, act, slope, branch = [ref.at[index] for ref in kept]
    gb, gpre, ga, gq, gkv = [ref.at[index] for ref in grads]
    blocks = head_blocks()
    gate = jax.nn.sigmoid(branch[...])
    gof = go[...].astype(F32)
    gb[...] = (gof * attended[...] * gate * (1.0 - gate)).astype(BF16)
    gpre[...] = (slope[...].astype(F32) * dot_t(gb[...], wout[...])).astype(BF16)
    ghidden, ffn_gain_grad = layer_norm_back(hidden[...], ffn_gain, dot_t(gpre[...], win[...]))
    gattended = (ghidden + gof * gate).astype(BF16)
    ga[...] = gattended
    gmixed = dot_t(wproj[...], jnp.concatenate([gattended] * HEADS, axis=0)).astype(BF16).astype(F32)
    gmixed = jnp.where(blocks, gmixed * inv[...], 0.0)
    low_mixed = gmixed.astype(BF16)
    centre = jnp.sum(mixm[...].astype(F32) * gmixed, axis=0, keepdims=True)
    gprobs = dot(kv[:, D:], low_mixed)
    gscores = (probs[...].astype(F32) * (gprobs - centre)).astype(BF16)
    gqueries = dot(kv[:, :D].T, gscores) * score_scale
    gqueries = jnp.where(blocks, gqueries, 0.0).astype(BF16)
    gq[...] = dot_t(repeat_matrix(), gqueries).astype(BF16)
    gkv[:, :D] = (dot_t(gscores, keyed[...]) * score_scale).astype(BF16)
    gkv[:, D:] = dot_t(probs[...], low_mixed).astype(BF16)
    grows = dot_t(gkv[...], wqkv[:, D:])
    gslots = grows[SEG_LEN:] + dot_t(gq[...], wqkv[:, :D])
    grad_rows, gain_rows = layer_norm_back(y[...].astype(F32), gain, grows[:SEG_LEN])
    grad_slots, gain_slots = layer_norm_back(m[...].astype(F32), gain, gslots)
    grad_y[...] = grad_rows.astype(BF16)
    grad_m[...] = grad_slots + ghidden + gof
    return gain_rows + gain_slots, ffn_gain_grad


def encoder_ffn_backward(need, cot, grad_y, hidden, gain, win, wout, slope, gb, gnf, ga, ghidden):
    need(cot, grad_y)
    go = cot[...].astype(F32) + grad_y[...].astype(F32)
    gb[...] = go.astype(BF16)
    ghidden[...] = go
    gnf[...] = jnp.zeros_like(gnf)
    need(wout, slope, win)

    def step(index, carry):
        span = pl.ds(pl.multiple_of(index * TILE, TILE), TILE)
        low = (slope[:, span].astype(F32) * dot_t(gb[...], wout[span])).astype(BF16)
        slope[:, span] = low
        gnf[...] += dot_t(low, win[:, span])
        return carry

    lax.fori_loop(0, FF // TILE, step, 0)
    need(hidden)
    grad, gain_grad = layer_norm_back(hidden[...], gain, gnf[...])
    grad = grad + ghidden[...]
    ghidden[...] = grad
    ga[...] = grad.astype(BF16)
    return gain_grad


def encoder_attention_backward(
    need, x, m, gain, wqkv, wproj, qt, kv, probs, inv, mixt, ga, ghidden, kt, gmt, gqkvt, grad_x, grad_m
):
    need(wproj, ga)
    gmt[...] = dot_t(wproj[...], ga[...]).astype(BF16)
    need(kv)
    kt[...] = kv[:, :D].T
    gqkvt[:D, SEG_LEN:] = jnp.zeros((D, SLOTS), BF16)
    empty = jnp.zeros((HEAD_DIM, SEG_LEN), BF16)
    need(inv, mixt, qt, probs)

    def pair(index, carry):
        base = pl.multiple_of(index * 128, 128)
        values = kv[:, pl.ds(pl.multiple_of(D + base, 128), 128)]
        for half in range(2):
            head = 2 * index + half
            start = pl.multiple_of(base + half * HEAD_DIM, HEAD_DIM)
            rows = pl.ds(start, HEAD_DIM)
            scaled = gmt[rows].astype(F32) * inv[head]
            centre = jnp.sum(mixt[rows].astype(F32) * scaled, axis=0, keepdims=True)
            low = scaled.astype(BF16)
            if half == 0:
                right = jnp.concatenate([low, empty], axis=0)
            else:
                right = jnp.concatenate([empty, low], axis=0)
            gprobs = dot(values, right)
            gscores = (probs[head].astype(F32) * (gprobs - centre)).astype(BF16)
            gqkvt[rows, :SEG_LEN] = (dot(kt[rows], gscores) * score_scale).astype(BF16)
            gqkvt[pl.ds(pl.multiple_of(D + start, HEAD_DIM), HEAD_DIM)] = (
                dot_t(qt[rows], gscores) * score_scale
            ).astype(BF16)
            gqkvt[pl.ds(pl.multiple_of(2 * D + start, HEAD_DIM), HEAD_DIM)] = dot_t(low, probs[head]).astype(BF16)
        return carry

    lax.fori_loop(0, HEADS // 2, pair, 0)
    need(wqkv, x, m, ghidden)
    grows = dot(wqkv[...], gqkvt[...]).T
    grad_rows, gain_rows = layer_norm_back(x[...].astype(F32), gain, grows[:SEG_LEN])
    grad_slots, gain_slots = layer_norm_back(m[...].astype(F32), gain, grows[SEG_LEN:])
    grad_x[...] = (grad_rows + ghidden[...]).astype(BF16)
    grad_m[...] = grad_slots
    return gain_rows + gain_slots


def spot_of(block):
    if block < 8:
        return block // 2, pl.ds(block % 2, 1), slice(0, LONG_ROWS)
    return block - 8, pl.ds(0, 2), slice(LONG_ROWS, CHUNK)


def halves(core):
    return [pl.ds(pl.multiple_of(side * HALF, HALF), HALF) for side in (core, 1 - core)]


def memory_weights(mover, core, kept, grads, packs, stage, short_stage, act_t, nf_t, mixed_t, slots_t, n0_t, n1_t):
    n, kv, keyed, probs, inv, mixm, mixed, attended, hidden, nf, act, slope, branch = kept
    gb, gpre, ga, gq, gkv = grads

    def both(ref, *index):
        return jnp.concatenate([ref[(k,) + index] for k in range(SEGS)], axis=0)

    whole = slice(None)
    for block in range(4):
        span = slice(block * TILE, (block + 1) * TILE)
        act_t[span] = both(act, whole, span).T
    nf_t[...] = both(nf).T
    mixed_t[...] = both(mixed).T
    slots_t[...] = both(n, slice(SEG_LEN, ROWS)).T
    n0_t[...] = n[0].T
    n1_t[...] = n[1].T
    flying = [None] * BLOCKS
    for pack, rows in zip(packs, halves(core)):

        def put(block, value, pack=pack):
            if flying[block] is not None:
                mover.left(flying[block])
            piece, half, rows = spot_of(block)
            held = stage.at[block] if block < 8 else short_stage.at[block - 8]
            held[...] = value.astype(BF16).reshape(held.shape)
            flying[block] = mover.send(held, pack.at[piece, half, :, rows])

        for block in range(4):
            span = slice(block * TILE, (block + 1) * TILE)
            put(block, dot(act_t.at[span][rows], both(gb)))
            put(4 + block, dot(nf_t[rows], both(gpre, whole, span)))
        put(8, dot(mixed_t[rows], both(ga)))
        put(9, dot(slots_t[rows], both(gq)))
        for block in range(2):
            span = slice(block * TILE, (block + 1) * TILE)
            put(10 + block, dot(n0_t[rows], gkv[0, :, span]) + dot(n1_t[rows], gkv[1, :, span]))


def encoder_ffn_weights(need, core, acts, gbs, nfs, gpres, packs, left, left_nf):
    need(*gbs, *acts)

    def outer(block, carry):
        span = pl.ds(pl.multiple_of(block * TILE, TILE), TILE)
        for k in range(SEGS):
            left[k] = acts[k][:, span].T
        start = pl.multiple_of(block * HALF, HALF)
        for pack, rows in zip(packs, halves(core)):
            pack[pl.ds(start, HALF)] = (
                dot(left[0, rows], gbs[0][...]) + dot(left[1, rows], gbs[1][...])
            ).astype(BF16)
        return carry

    lax.fori_loop(0, 4, outer, 0)
    need(*nfs, *gpres)
    for k in range(SEGS):
        left_nf[k] = nfs[k][...].T

    def inner(block, carry):
        span = pl.ds(pl.multiple_of(block * TILE, TILE), TILE)
        start = pl.multiple_of((4 + block) * HALF, HALF)
        for pack, rows in zip(packs, halves(core)):
            pack[pl.ds(start, HALF)] = (
                dot(left_nf[0, rows], gpres[0][:, span]) + dot(left_nf[1, rows], gpres[1][:, span])
            ).astype(BF16)
        return carry

    lax.fori_loop(0, 4, inner, 0)


def encoder_attention_weights(need, core, mixts, gas, ns, gqkvts, packs, left):
    need(*mixts, *gas)
    for pack, rows in zip(packs, halves(core)):
        pack[:HALF] = (dot(mixts[0][rows], gas[0][...]) + dot(mixts[1][rows], gas[1][...])).astype(BF16)
    need(*ns, *gqkvts)
    for k in range(SEGS):
        left[k] = ns[k][...].T

    def third(block, carry):
        span = pl.ds(pl.multiple_of(block * TILE, TILE), TILE)
        start = pl.multiple_of((1 + block) * HALF, HALF)
        for pack, rows in zip(packs, halves(core)):
            pack[pl.ds(start, HALF)] = (
                dot_t(left[0, rows], gqkvts[0][span]) + dot_t(left[1, rows], gqkvts[1][span])
            ).astype(BF16)
        return carry

    lax.fori_loop(0, 3, third, 0)


SCALAR = pl.BlockSpec(memory_space=pltpu.SMEM)
HELD = pl.BlockSpec(memory_space=pltpu.VMEM)
FAR = pl.BlockSpec(memory_space=pl.ANY)

WEIGHTS = (((D, 3 * D), BF16), ((D, D), BF16), ((D, FF), BF16), ((FF, D), BF16))
ROW_LOW = ((SEG_LEN, D), BF16)
ROW_FULL = ((SEG_LEN, D), F32)
WIDE = ((SEG_LEN, FF), BF16)
ALL_LOW = ((ROWS, D), BF16)
ALL_TURNED = ((D, ROWS), BF16)
TURNED = ((D, SEG_LEN), BF16)
SLOT_LOW = ((SLOTS, D), BF16)
SLOT_FULL = ((SLOTS, D), F32)
SLOT_WIDE = ((SLOTS, FF), BF16)
SLOT_TURNED = ((D, SEGS * SLOTS), BF16)
SQUARE = ((D, D), BF16)
PROBS = ((HEADS, ROWS, SEG_LEN), BF16)
INVERSE = ((HEADS, 1, SEG_LEN), F32)
KEYS_VALUES = ((ROWS, 2 * D), BF16)
GRAD_TURNED = ((3 * D, ROWS), BF16)
GAINS = ((8, D), F32)
BIAS = ((ROWS, 128), BF16)
EXTRAS = SLOTS + 16
PARCEL = SEGS * SEG_LEN + SLOTS
CHUNKS = 4
LONG_ROWS = HALF // CHUNKS
SHORT_ROWS = LONG_ROWS // 2
CHUNK = LONG_ROWS + SHORT_ROWS
PACK = ((4, 2, CHUNKS, CHUNK, D), BF16)


def pack_of(blocks):
    return ((blocks * HALF, D), BF16)


def twice(item):
    return ((SEGS,) + item[0], item[1])


def call(body, kinds, outs, scratch, copies, name, aliases={}):
    out_kinds, outs = zip(*outs)
    specs = {"s": SCALAR, "v": HELD, "f": FAR}
    inputs = len(kinds)

    def kernel(*refs):
        ins, results = refs[:inputs], refs[inputs : inputs + len(outs)]
        held, sems = refs[inputs + len(outs) : -1], refs[-1]
        body(Mover(sems), ins, results, held)

    light = name in ("unpack", "assemble")
    cost = pl.CostEstimate(
        flops=1_000_000 if light else 20_000_000_000, bytes_accessed=1_000_000 if light else 10_000_000, transcendentals=0
    )
    return pl.pallas_call(
        kernel,
        out_shape=[jax.ShapeDtypeStruct(shape, kind) for shape, kind in outs],
        in_specs=[specs[kind] for kind in kinds],
        out_specs=[specs[kind] for kind in out_kinds],
        scratch_shapes=[pltpu.VMEM(shape, kind) for shape, kind in scratch] + [pltpu.SemaphoreType.DMA((copies,))],
        compiler_params=pltpu.CompilerParams(vmem_limit_bytes=60 * 2**20),
        cost_estimate=cost,
        input_output_aliases=aliases,
        name=name,
    )


def own_gains(own, other, front):
    return jnp.where(front, own[...], other[...])


def document_rows(core, segment):
    return pl.ds(pl.multiple_of((core * SEGS + segment) * SEG_LEN, SEG_LEN), SEG_LEN)


def column_halves(core):
    return [pl.ds(pl.multiple_of(side * (D // 2), D // 2), D // 2) for side in (core, 1 - core)]


def first_kernel(mover, ins, outs, held):
    tokens, m, gains_own, gains_other, qkv_own, qkv_other, proj_own, proj_other = ins
    x, n, qt, kv, probs, inv, mixt, hidden, vt, wqkv, wproj, bias = held
    core = lax.axis_index("pipe")
    gains = own_gains(gains_own, gains_other, core == 0)
    bias[...] = jnp.zeros_like(bias)
    mover.bring(x, tokens.at[document_rows(core, 0)])
    mover.bring_either(wqkv, core == 0, qkv_own, qkv_other)
    mover.bring_either(wproj, core == 0, proj_own, proj_other)
    targets = dict(zip((id(ref) for ref in (hidden, n, qt, kv, probs, inv, mixt)), outs))

    def ready(*sources):
        for source in sources:
            mover.send(source, targets[id(source)])

    encoder_attention(
        mover.need, x, m, bias, gains[0:1], wqkv, wproj, n, qt, kv, vt, probs, inv, mixt, hidden, ready
    )
    mover.finish()


FIRST = (ROW_FULL, ALL_LOW, TURNED, KEYS_VALUES, PROBS, INVERSE, TURNED)


def first_call(tokens, m, gains, weights):
    return call(
        first_kernel,
        "fvvvffff",
        [("f", item) for item in FIRST],
        [ROW_LOW, ALL_LOW, TURNED, KEYS_VALUES, PROBS, INVERSE, TURNED, ROW_FULL, ALL_TURNED, WEIGHTS[0], WEIGHTS[1], BIAS],
        10,
        "encoder_attention",
    )(tokens, m, *gains, *weights[0], *weights[1])


MEMORY_KEPT = (
    ALL_LOW, KEYS_VALUES, SQUARE, ALL_LOW, ((1, D), F32), SQUARE, SLOT_LOW, SLOT_FULL, SLOT_FULL,
    SLOT_LOW, SLOT_WIDE, SLOT_WIDE, SLOT_FULL,
)
MEMORY_GRADS = (SLOT_LOW, SLOT_WIDE, SLOT_LOW, SLOT_LOW, KEYS_VALUES)


def middle_kernel(mover, ins, outs, held):
    lengths, m0, gains_own, gains_other, cot_memory, hidden0, tokens, cots = ins[:8]
    pairs = ins[8:]
    (parcel, mine, theirs, out_nf, out_act, out_slope, out_n, out_mixt, out_gb, out_ga, out_gqkvt, out_grad_y, out_grad_x,
     out_grad_m, out_gains) = outs
    out_y = [parcel.at[pl.ds(k * SEG_LEN, SEG_LEN)] for k in range(SEGS)]
    out_final = parcel.at[pl.ds(SEGS * SEG_LEN, SLOTS)]
    enc_weights, mem_weights, held = held[:4], held[4:8], held[8:]
    kept, held = held[: len(MEMORY_KEPT)], held[len(MEMORY_KEPT) :]
    grads, held = held[: len(MEMORY_GRADS)], held[len(MEMORY_GRADS) :]
    (x, cot, cot_slots, hidden, n, qt, kv, probs, inv, mixt, nf, act, slope, y0, y1, turned, total, gnf, gmt, gb, ga,
     gqkvt, grad_y, grad_x, m1, final, grad_m, grad_m1, stage, short_stage, act_t, nf_t, mixed_t, slots_t, bias) = held
    core = lax.axis_index("pipe")
    front = core == 0
    enc_gains = own_gains(gains_own, gains_other, front)
    mem_gains = own_gains(gains_other, gains_own, front)
    valid_rows = lengths[core] - SEG_LEN
    lanes = iota(BIAS[0], 1) % HEAD_DIM == 0
    bias[...] = jnp.where(lanes & ~valid_keys(BIAS[0], valid_rows), masked_bias, 0.0).astype(BF16)
    need = mover.need
    wqkv, wproj, win, wout = enc_weights
    mover.bring(hidden, hidden0)
    for index in (2, 3):
        mover.bring_either(enc_weights[index], front, *pairs[2 * index : 2 * index + 2])
    for index in range(4):
        own, other = pairs[2 * index : 2 * index + 2]
        mover.bring_either(mem_weights[index], front, other, own)
    mover.bring(x, tokens.at[document_rows(core, 1)])
    for index in (0, 1):
        mover.bring_either(enc_weights[index], front, *pairs[2 * index : 2 * index + 2])
    mover.bring(cot_slots, cot_memory.at[core])
    mover.bring(cot, cots.at[document_rows(core, 1)])
    enc_attn, enc_ffn = enc_gains[0:1], enc_gains[1:2]
    mem_attn, mem_ffn = mem_gains[0:1], mem_gains[1:2]

    encoder_ffn(need, hidden, enc_ffn, win, wout, y0, nf, act, slope, total)
    mover.send(y0, out_y[0])
    early = [mover.send(nf, out_nf.at[0]), mover.send(act, out_act.at[0]), mover.send(slope, out_slope.at[0])]
    memory_forward(need, y0, m0, None, mem_attn, mem_ffn, mem_weights, m1, kept, 0, turned)
    encoder_attention(need, x, m1, bias, enc_attn, wqkv, wproj, n, qt, kv, turned, probs, inv, mixt, hidden)
    mover.send(n, out_n)
    mover.send(mixt, out_mixt)
    mover.left(*early)
    encoder_ffn(need, hidden, enc_ffn, win, wout, y1, nf, act, slope, total)
    mover.send(y1, out_y[1])
    mover.send(nf, out_nf.at[1])
    mover.send(act, out_act.at[1])
    memory_forward(need, y1, m1, valid_rows, mem_attn, mem_ffn, mem_weights, final, kept, 1, turned)
    mover.send(final, out_final)

    need(cot_slots)
    attn_gain1, ffn_gain1 = memory_backward(
        cot_slots, y1, m1, mem_attn, mem_ffn, mem_weights, kept, 1, grad_y, grad_m, grads
    )
    out_gains[1:2] = encoder_ffn_backward(need, cot, grad_y, hidden, enc_ffn, win, wout, slope, gb, gnf, ga, total)
    mover.send(gb, out_gb)
    mover.send(ga, out_ga)
    mover.send(slope, out_slope.at[1])
    out_gains[0:1] = encoder_attention_backward(
        need, x, m1, enc_attn, wqkv, wproj, qt, kv, probs, inv, mixt, ga, total, turned, gmt, gqkvt, grad_x, grad_m1
    )
    turned_out = mover.send(gqkvt, out_gqkvt)
    mover.send(grad_x, out_grad_x)
    grad_m[...] = grad_m[...] + grad_m1[...].astype(BF16).astype(F32)
    attn_gain0, ffn_gain0 = memory_backward(
        grad_m, y0, m0, mem_attn, mem_ffn, mem_weights, kept, 0, grad_y, out_grad_m, grads
    )
    mover.send(grad_y, out_grad_y)
    out_gains[2:3] = attn_gain0 + attn_gain1
    out_gains[3:4] = ffn_gain0 + ffn_gain1
    out_gains[4:8] = jnp.zeros((4, D), F32)
    mover.left(turned_out)
    memory_weights(
        mover, core, kept, grads, (mine, theirs), stage, short_stage, act_t, nf_t, mixed_t, slots_t,
        gqkvt.at[pl.ds(0, D)], gqkvt.at[pl.ds(D, D)],
    )
    mover.finish()


def middle_call(lengths, m0, gains, cot_memory, hidden, tokens, cots, weights):
    outs = [
        ("f", ((PARCEL, D), BF16)), ("f", PACK), ("f", PACK), ("f", twice(ROW_LOW)), ("f", twice(WIDE)),
        ("f", twice(WIDE)), ("f", ALL_LOW), ("f", TURNED), ("f", ROW_LOW), ("f", ROW_LOW), ("f", GRAD_TURNED),
        ("f", ROW_LOW), ("f", ROW_LOW), ("v", SLOT_FULL), ("v", GAINS),
    ]
    scratch = [
        *WEIGHTS, *WEIGHTS, *[twice(item) for item in MEMORY_KEPT], *[twice(item) for item in MEMORY_GRADS],
        ROW_LOW, ROW_LOW, SLOT_LOW, ROW_FULL, ALL_LOW, TURNED, KEYS_VALUES, PROBS, INVERSE, TURNED, ROW_LOW, WIDE,
        WIDE, ROW_LOW, ROW_LOW, ALL_TURNED, ROW_FULL, ROW_FULL, TURNED, ROW_LOW, ROW_LOW, GRAD_TURNED, ROW_LOW,
        ROW_LOW, SLOT_LOW, SLOT_LOW, SLOT_FULL, SLOT_FULL, ((8, 1, CHUNKS, LONG_ROWS, D), BF16), ((4, 2, CHUNKS, SHORT_ROWS, D), BF16),
        ((FF, SEGS * SLOTS), BF16),
        SLOT_TURNED, SLOT_TURNED, SLOT_TURNED, BIAS,
    ]
    return call(middle_kernel, "svvvffff" + "f" * 8, outs, scratch, 64, "middle")(
        lengths, m0, *gains, cot_memory, hidden, tokens, cots,
        *[item for pair in weights for item in pair],
    )


def feed_kernel(mover, ins, outs, held):
    gains_own, gains_other, grad_gains, cots, grad_y0, hidden0, slopes, in_own, in_other, out_own, out_other = ins
    out_gpre, out_gb, out_ga, out_ghidden, out_gains = outs
    win, wout, cot, grad_y, hidden, gpre, gb, gnf, ga, ghidden = held
    core = lax.axis_index("pipe")
    gains = own_gains(gains_own, gains_other, core == 0)
    mover.bring(cot, cots.at[document_rows(core, 0)])
    mover.bring(grad_y, grad_y0)
    mover.bring_either(wout, core == 0, out_own, out_other)
    mover.bring(gpre, slopes.at[0])
    mover.bring_either(win, core == 0, in_own, in_other)
    mover.bring(hidden, hidden0)
    gain_grad = encoder_ffn_backward(
        mover.need, cot, grad_y, hidden, gains[1:2], win, wout, gpre, gb, gnf, ga, ghidden
    )
    for source, target in ((gpre, out_gpre), (gb, out_gb), (ga, out_ga), (ghidden, out_ghidden)):
        mover.send(source, target)
    out_gains[...] = grad_gains[...]
    out_gains[1:2] = grad_gains[1:2] + gain_grad
    mover.finish()


def feed_call(gains, grad_gains, cots, grad_y, hidden, slopes, weights):
    return call(
        feed_kernel,
        "vvvffffffff",
        [("f", WIDE), ("f", ROW_LOW), ("f", ROW_LOW), ("f", ROW_FULL), ("v", GAINS)],
        [WEIGHTS[2], WEIGHTS[3], ROW_LOW, ROW_LOW, ROW_FULL, WIDE, ROW_LOW, ROW_FULL, ROW_LOW, ROW_FULL],
        10,
        "encoder_feed",
    )(*gains, grad_gains, cots, grad_y, hidden, slopes, *weights[2], *weights[3])


def ordered_pieces(device):
    pieces = []
    for part in range(2):
        stays = (device >> part) & 1
        pieces.append((2 * part + 1 - stays, 2 * part + stays))
    return pieces


def send_pieces(mover, device, packs, mine, soon, late, rows):
    for part, (goes, stays) in enumerate(ordered_pieces(device)):
        goes = pl.ds(pl.multiple_of(goes * rows, rows), rows)
        stays = pl.ds(pl.multiple_of(stays * rows, rows), rows)
        mover.send(packs[1].at[goes], soon[part] if isinstance(soon, (list, tuple)) else soon.at[pl.ds(part * rows, rows)])
        mover.send(packs[0].at[goes], mine.at[pl.ds(part * rows, rows)])
        mover.send(packs[0].at[stays], mine.at[pl.ds((2 + part) * rows, rows)])
        mover.send(packs[1].at[stays], late.at[pl.ds(part * rows, rows)])


LONG = 2 * HALF
SHORT = HALF


def outer_kernel(mover, ins, outs, held):
    acts, slopes, nfs, gpre0, gb0, gb1 = ins[:6]
    (m0, gains_own, gains_other, grad_gains, grad_m, tokens, qt0, kv0, probs0, inv0, mixt0, ga0, ghidden0, grad_x1,
     qkv_own, qkv_other, proj_own, proj_other) = ins[6:]
    mine, soon, late, out_keep, out_gqkvt, parcel = outs
    acts_held, nfs_held, gpres_held, gbs_held = [held[2 * k : 2 * k + 2] for k in range(4)]
    packs, left, left_nf = held[8:10], held[10], held[11]
    (wqkv, wproj, x, qt, kv, probs, inv, mixt, ga, ghidden, gqkvt, kt, gmt, grad_x, grad_x1_held, grad_m0,
     extras) = held[12:]
    core, device = lax.axis_index("pipe"), lax.axis_index("dp")
    gains = own_gains(gains_own, gains_other, core == 0)
    need = mover.need
    for target, source in zip(gbs_held, (gb0, gb1)):
        mover.bring(target, source)
    for k in range(SEGS):
        mover.bring(acts_held[k], acts.at[k])
    need(*gbs_held, *acts_held)
    for k in range(SEGS):
        mover.bring(nfs_held[k], nfs.at[k])
    mover.bring(gpres_held[0], gpre0)
    mover.bring(gpres_held[1], slopes.at[1])
    mover.bring_either(wproj, core == 0, proj_own, proj_other)
    mover.bring(ga, ga0)
    mover.bring(kv, kv0)
    mover.bring(inv, inv0)
    mover.bring(mixt, mixt0)
    mover.bring(qt, qt0)
    mover.bring(probs, probs0)
    mover.bring_either(wqkv, core == 0, qkv_own, qkv_other)
    mover.bring(x, tokens.at[document_rows(core, 0)])
    mover.bring(ghidden, ghidden0)
    mover.bring(grad_x1_held, grad_x1)
    encoder_ffn_weights(need, core, acts_held, gbs_held, nfs_held, gpres_held, packs, left, left_nf)
    send_pieces(mover, device, packs, mine, soon, late, LONG)
    gain_grad = encoder_attention_backward(
        need, x, m0, gains[0:1], wqkv, wproj, qt, kv, probs, inv, mixt, ga, ghidden, kt, gmt, gqkvt, grad_x, grad_m0
    )
    mover.send(gqkvt, out_gqkvt)
    extras[:SLOTS] = (grad_m[...] + grad_m0[...]).astype(BF16)
    low = jnp.concatenate(
        [grad_gains[0:1] + gain_grad, grad_gains[1:4], jnp.zeros((EXTRAS - SLOTS - 4, D), F32)], axis=0
    )
    extras[SLOTS:] = low.astype(BF16)
    mover.send(extras, parcel.at[pl.ds(0, EXTRAS)])
    keep, give = column_halves(core)
    for segment, source in enumerate((grad_x, grad_x1_held)):
        need(source)
        columns = pl.ds(segment * (D // 2), D // 2)
        mover.send(source.at[:, keep], out_keep.at[:, columns])
        mover.send(source.at[:, give], parcel.at[pl.ds(EXTRAS, SEG_LEN), columns])
    mover.finish()


def outer_call(
    acts, slopes, nfs, gpre0, gb0, gb1, m0, gains, grad_gains, grad_m, tokens, qt0, kv0, probs0, inv0, mixt0, ga0,
    ghidden0, grad_x1, weights,
):
    return call(
        outer_kernel,
        "ffffff" + "vvvvv" + "f" * 13,
        [
            ("f", ((4 * LONG, D), BF16)), ("f", ((2 * LONG, D), BF16)), ("f", ((2 * LONG, D), BF16)), ("f", ROW_LOW),
            ("f", GRAD_TURNED), ("f", ((EXTRAS + SEG_LEN, D), BF16)),
        ],
        [
            WIDE, WIDE, ROW_LOW, ROW_LOW, WIDE, WIDE, ROW_LOW, ROW_LOW, ((4 * LONG, D), BF16), ((4 * LONG, D), BF16),
            twice(SQUARE), twice(SQUARE), WEIGHTS[0], WEIGHTS[1], ROW_LOW, TURNED, KEYS_VALUES, PROBS, INVERSE,
            TURNED, ROW_LOW, ROW_FULL, GRAD_TURNED, ALL_TURNED, TURNED, ROW_LOW, ROW_LOW, SLOT_FULL,
            ((EXTRAS, D), BF16),
        ],
        33,
        "encoder_outer",
    )(
        acts, slopes, nfs, gpre0, gb0, gb1, m0, *gains, grad_gains, grad_m, tokens, qt0, kv0, probs0, inv0, mixt0,
        ga0, ghidden0, grad_x1, *weights[0], *weights[1],
    )


def inner_kernel(mover, ins, outs, held):
    mine, *soon, late = outs
    packs, left = held[8:10], held[10]
    for target, source in zip(held, ins):
        mover.bring(target, source)
    encoder_attention_weights(
        mover.need, lax.axis_index("pipe"), held[0:2], held[2:4], held[4:6], held[6:8], packs, left
    )
    send_pieces(mover, lax.axis_index("dp"), packs, mine, soon, late, SHORT)
    mover.finish()


def inner_call(*operands):
    pack = ((4 * SHORT, D), BF16)
    return call(
        inner_kernel,
        "ffffffff",
        [("f", pack), ("f", ((SHORT, D), BF16)), ("f", ((SHORT, D), BF16)), ("f", ((2 * SHORT, D), BF16))],
        [TURNED, TURNED, ROW_LOW, ROW_LOW, ALL_LOW, ALL_LOW, GRAD_TURNED, GRAD_TURNED, pack, pack, twice(ALL_TURNED)],
        16,
        "encoder_inner",
    )(*operands)


def assemble_kernel(mover, ins, outs, held):
    parcel, parcel_other, keep0, last_other = ins
    activations, final_memory, grad_tokens = outs
    core = lax.axis_index("pipe")
    rows = SEGS * SEG_LEN
    start = 0
    for source, y, final in zip((parcel, parcel_other), held[0:2], held[2:4]):
        mover.bring(y, source.at[pl.ds(start, rows)])
        mover.bring(final, source.at[pl.ds(start + rows, SLOTS)])
    keep, give = held[4:6]
    mover.bring(keep, keep0)
    mover.bring(give, last_other.at[pl.ds(EXTRAS, SEG_LEN)])
    for document, y, final, grads in zip((core, 1 - core), held[0:2], held[2:4], held[4:6]):
        mover.need(y, final, grads)
        mover.send(y, activations.at[pl.ds(pl.multiple_of(document * rows, rows), rows)])
        mover.send(final, final_memory.at[document])
        for segment in range(SEGS):
            columns = grads.at[:, pl.ds(segment * (D // 2), D // 2)]
            mover.send(columns, grad_tokens.at[document_rows(document, segment)])
    mover.finish()


def assemble_call(*operands):
    rows = 2 * SEGS * SEG_LEN
    outs = [("f", ((rows, D), BF16)), ("f", ((2, SLOTS, D), BF16)), ("f", ((rows, D // 2), BF16))]
    y = ((SEGS * SEG_LEN, D), BF16)
    return call(
        assemble_kernel, "ffff", outs, [y, y, SLOT_LOW, SLOT_LOW, ROW_LOW, ROW_LOW], 16, "assemble"
    )(*operands)


def place_block(block):
    if block < 4:
        return 0, lambda row: (pl.ds(block * TILE + row, HALF), slice(None))
    if block < 8:
        return 1, lambda row: (pl.ds(row, HALF), slice((block - 4) * TILE, (block - 3) * TILE))
    if block == 8:
        return 2, lambda row: (pl.ds(row, HALF), slice(None))
    return 3, lambda row: (pl.ds(row, HALF), slice((block - 9) * TILE, (block - 8) * TILE))


def unpack_kernel(distance, mover, ins, outs, held):
    pieces, wide, short_wide = held
    core = lax.axis_index("pipe")
    device = lax.axis_index("dp")
    for index in range(4):
        mover.bring_either(pieces.at[index], core == 0, ins[index], ins[4 + index])
    arrivals = list(mover.coming.values())
    for index in range(4):
        side, part = index // 2, index % 2
        pltpu.make_async_copy(*arrivals[index]).wait()
        near = (device >> part) & 1
        piece = 2 * part + (near if distance == 0 else 1 - near)
        row = pl.multiple_of((core if side == 0 else 1 - core) * HALF, HALF)
        for half in range(2):
            value = pieces[index, half, :, :LONG_ROWS].reshape(HALF, D).astype(F32)
            wide[index, half] = value
            if part == 0:
                start = pl.multiple_of((2 * piece + half) * TILE + row, HALF)
                mover.send(wide.at[index, half], outs[0].at[pl.ds(start, HALF)])
            else:
                column = pl.multiple_of((2 * (piece - 2) + half) * TILE, TILE)
                mover.send(wide.at[index, half], outs[1].at[pl.ds(row, HALF), pl.ds(column, TILE)])
        short_wide[index] = pieces[index, :, :, LONG_ROWS:].reshape(HALF, D).astype(F32)
        if part == 0:
            sem = mover.slot()
            targets = (outs[2].at[pl.ds(row, HALF)], outs[3].at[pl.ds(row, HALF), pl.ds(0, TILE)])
            for which, target in enumerate(targets):

                @pl.when(piece == which)
                def _(target=target):
                    pltpu.make_async_copy(short_wide.at[index], target, sem).start()

            mover.leaving.append(pltpu.make_async_copy(short_wide.at[index], targets[0], sem))
        else:
            column = pl.multiple_of((piece - 1) * TILE, TILE)
            mover.send(short_wide.at[index], outs[3].at[pl.ds(row, HALF), pl.ds(column, TILE)])
    mover.finish()


def unpack_call(distance, sources, begun):
    outs = [((FF, D), F32), ((D, FF), F32), ((D, D), F32), ((D, 3 * D), F32)]

    def body(mover, ins, results, held):
        unpack_kernel(distance, mover, ins, results, held)

    return call(
        body,
        "f" * (len(sources) + len(begun)),
        [("f", item) for item in outs],
        [((4, 2, CHUNKS, CHUNK, D), BF16), ((4, 2, HALF, D), F32), ((4, HALF, D), F32)],
        16,
        "unpack",
        {len(sources) + k: k for k in range(len(begun))},
    )(*sources, *begun)


def total_of(blocks):
    return sum(block.astype(F32) for block in blocks).astype(BF16)


def fold(outputs):
    arrays = []
    plan = []
    if any(rows % 16 for entries in outputs for rows, _ in entries):
        device = lax.axis_index("dp")
        sums = [
            [total_of([rows_of(array, start(device), rows) for array, start in pieces]) for rows, pieces in entries]
            for entries in outputs
        ]
        return [jnp.concatenate(entries, axis=0) for entries in sums]
    for entries in outputs:
        for rows, pieces in entries:
            for array, start in pieces:
                if not any(array is other for other in arrays):
                    arrays.append(array)
    for entries in outputs:
        plan.append([
            (rows, [([array is other for other in arrays].index(True), start) for array, start in pieces])
            for rows, pieces in entries
        ])
    sizes = [sum(rows for rows, _ in entries) for entries in plan]
    total = sum(rows * len(pieces) for entries in plan for rows, pieces in entries)

    def body(mover, ins, results, held):
        gathered, summed = held
        device = lax.axis_index("dp")
        arrivals, done = [], 0
        for entries in plan:
            for rows, pieces in entries:
                group = []
                for index, start in pieces:
                    target = gathered.at[pl.ds(done, rows)]
                    first = pl.multiple_of(jnp.asarray(start(device), jnp.int32), 16)
                    mover.bring(target, ins[index].at[pl.ds(first, rows)])
                    group.append((target, done))
                    done += rows
                arrivals.append(group)
        arrivals, done = iter(arrivals), 0
        for entries, size, result in zip(plan, sizes, results):
            begin = done
            for rows, pieces in entries:
                group = next(arrivals)
                mover.need(*[target for target, _ in group])
                summed[done : done + rows] = total_of([gathered[row : row + rows] for _, row in group])
                done += rows
            mover.send(summed.at[pl.ds(begin, size)], result)
        mover.finish()

    pieces_count = sum(len(pieces) for entries in plan for _, pieces in entries)
    return call(
        body, "f" * len(arrays), [("f", ((size, D), BF16)) for size in sizes],
        [((total, D), BF16), ((sum(sizes), D), BF16)], pieces_count + len(sizes), "fold",
    )(*arrays)


def swap(block):
    return lax.ppermute(block, "pipe", [(0, 1), (1, 0)])


def neighbour(block, bit):
    devices = lax.axis_size("dp")
    return lax.ppermute(block, "dp", [(k, k ^ (1 << bit)) for k in range(devices)])


def bit_of(bit):
    return (lax.axis_index("dp") >> bit) & 1


def after(value, *others):
    return lax.optimization_barrier((value,) + others)[0]


def rows_of(block, start, size):
    return lax.dynamic_slice_in_dim(block, start, size)


class Part:
    def __init__(self, size, pieces):
        self.size = size
        self.pieces = pieces

    def sum_of(self, shift, size):
        return total_of([rows_of(array, start + shift, size) for array, start in self.pieces])

    def value(self):
        return self.sum_of(0, self.size)


class Lazy:
    def __init__(self, size, pieces):
        self.size = size
        self.pieces = [(array, start if callable(start) else (lambda device, start=start: start)) for array, start in pieces]

    def entry(self):
        return self.size, self.pieces

    def half(self, bit, stays):
        size = self.size // 2

        def moved(start):
            def first(device):
                here = (device >> bit) & 1
                return start(device) + (here if stays else 1 - here) * size

            return first

        return Lazy(size, [(array, moved(start)) for array, start in self.pieces])

    def settled(self, bit, came, row):
        kept = self.half(bit, True)
        return Lazy(kept.size, kept.pieces + [(came, lambda device: row)])


def settle_lazy(parts, bit, came):
    results, done = [], 0
    for part in parts:
        results.append(part.settled(bit, came, done))
        done += results[-1].size
    return results


class Line:
    def __init__(self):
        self.last = None

    def send(self, block, bit):
        if self.last is not None:
            block = after(block, self.last)
        self.last = block
        return neighbour(block, bit)

    def trade(self, parts, bit, extra=None):
        give = [part.sum_of((1 - bit_of(bit)) * (part.size // 2), part.size // 2) for part in parts]
        if extra is not None:
            give.append(extra)
        return self.send(jnp.concatenate(give, axis=0) if len(give) > 1 else give[0], bit)


def settle(parts, bit, came):
    results, done = [], 0
    for part in parts:
        half = part.size // 2
        shift = bit_of(bit) * half
        results.append(Part(half, [(array, start + shift) for array, start in part.pieces] + [(came, done)]))
        done += half
    return results, came[done:]


def as_piece(block):
    rows = block.shape[1]
    if rows != CHUNK:
        long = rows * LONG_ROWS // CHUNK
        long, short = block[:, :long].reshape(-1, LONG_ROWS, D), block[:, long:].reshape(-1, SHORT_ROWS, D)
        block = jnp.concatenate([long, short], axis=1)
    return block.reshape(PACK[0][1:])


def join(block, came, bit):
    low = bit_of(bit) == 0
    return jnp.concatenate([jnp.where(low, block, came), jnp.where(low, came, block)], axis=0)


def local(
    tokens, lengths, memory_init, attn_gain, qkv_weight, proj_weight, ffn_gain, in_weight, out_weight,
    cot_tokens, cot_memory,
):
    core = lax.axis_index("pipe")
    front = core == 0
    gains = jnp.concatenate([attn_gain, ffn_gain], axis=0)
    gains = (gains, swap(gains))
    weights = [(held[0], swap(held[0])) for held in (qkv_weight, proj_weight, in_weight, out_weight)]

    hidden0, n0, qt0, kv0, probs0, inv0, mixt0 = first_call(tokens, memory_init, gains, weights)
    (parcel, mem_mine, mem_theirs, nfs, acts, slopes, n1, mixt1, gb1, ga1, gqkvt1, grad_y0, grad_x1, grad_m,
     grad_gains) = middle_call(lengths, memory_init, gains, cot_memory, hidden0, tokens, cot_tokens, weights)
    mem_theirs, parcel_other = swap(mem_theirs), swap(parcel)
    gpre0, gb0, ga0, ghidden0, grad_gains = feed_call(
        gains, grad_gains, cot_tokens, grad_y0, hidden0, slopes, weights
    )

    bits = lax.axis_size("dp").bit_length() - 1
    line = Line()
    both = range(2)
    mem_theirs, gb0 = lax.optimization_barrier((mem_theirs, gb0))
    rows = 2 * PIECE
    mem_mine, mem_theirs = mem_mine.reshape(-1, D), mem_theirs.reshape(-1, D)
    mem = [[Part(rows, [(mem_mine, k * rows), (mem_theirs, k * rows)])] for k in both]
    mem_came = [line.trade(mem[k], k) for k in both]
    long_mine, long_soon, long_late, out_keep, gqkvt0, last_parcel = outer_call(
        acts, slopes, nfs, gpre0, after(gb0, line.last), gb1, memory_init, gains, grad_gains, grad_m, tokens, qt0, kv0,
        probs0, inv0, mixt0, ga0, ghidden0, grad_x1, weights,
    )
    long_soon, last_other, long_late = swap(long_soon), swap(last_parcel), swap(long_late)
    *mem_came, gqkvt0 = lax.optimization_barrier((*mem_came, gqkvt0))
    mem = [settle(mem[k], k, mem_came[k])[0] for k in both]
    mem_came = [line.trade(mem[k], 1 - k) for k in both]
    short_mine, *short_soon, short_late = inner_call(
        mixt0, mixt1, ga0, ga1, n0, n1, after(gqkvt0, line.last), gqkvt1
    )
    short_soon, short_late = [swap(block) for block in short_soon], swap(short_late)
    *mem_came, long_soon, last_other, short_mine = lax.optimization_barrier(
        (*mem_came, long_soon, last_other, short_mine)
    )
    rest = list(range(2, bits))
    extras = Lazy(EXTRAS, [(last_parcel, 0), (last_other, 0)])
    enc = [
        [
            Lazy(LONG, [(long_mine, k * LONG), (long_soon, k * LONG)]),
            Lazy(SHORT, [(short_mine, k * SHORT), (short_soon[k], 0)]),
        ]
        for k in both
    ]
    gives = fold([[part.entry() for part in enc[0] + [extras]], [part.entry() for part in enc[1]]])
    enc_came = [line.send(gives[k], k) for k in both]
    extras = Lazy(EXTRAS, extras.pieces + [(enc_came[0], lambda device: PIECE)])
    mem = [settle(mem[k], 1 - k, mem_came[k])[0] for k in both]
    mem = mem[0] + mem[1]
    for bit in rest:
        mem = settle(mem, bit, line.trade(mem, bit))[0]
    mem = jnp.concatenate([part.value() for part in mem], axis=0)[None]
    enc = [
        [
            Lazy(LONG, [(long_mine, (2 + k) * LONG), (long_late, k * LONG), (enc_came[k], 0)]),
            Lazy(SHORT, [(short_mine, (2 + k) * SHORT), (short_late, k * SHORT), (enc_came[k], LONG)]),
        ]
        for k in both
    ]
    gives = fold([
        [part.half(1, False).entry() for part in enc[0]] + [extras.entry()],
        [part.half(0, False).entry() for part in enc[1]],
    ])
    enc_came = [line.send(gives[k], 1 - k) for k in both]
    extras = Lazy(EXTRAS, extras.pieces + [(enc_came[0], PIECE // 2)])
    for bit in rest[:0:-1]:
        mem = join(mem, line.send(mem, bit), bit)
    enc = settle_lazy(enc[0], 1, enc_came[0]) + settle_lazy(enc[1], 0, enc_came[1])
    for bit in rest:
        rows = sum(part.size for part in enc) // 2
        (give,) = fold([[part.half(bit, False).entry() for part in enc] + [extras.entry()]])
        came = line.send(give, bit)
        enc = settle_lazy(enc, bit, came)
        extras = Lazy(EXTRAS, extras.pieces + [(came, rows)])
        if bit == rest[0]:
            mem = join(mem, line.send(mem, bit), bit)

    def split(block):
        rows = block.shape[1] // 2
        return block[:, :rows], block[:, rows:]

    mem_parts = split(mem)
    enc, extras = fold([[part.entry() for part in enc], [extras.entry()]])
    enc = enc[None]
    mem_came = [line.send(mem_parts[k], 1 - k) for k in both]
    for bit in rest[::-1]:
        if bit == rest[0]:
            mem_near = [join(mem_parts[k], mem_came[k], 1 - k) for k in both]
            mem_far = [line.send(mem_near[k], k) for k in both]
        enc = join(enc, line.send(enc, bit), bit)
    *mem_far, enc = lax.optimization_barrier((*mem_far, enc))
    enc_parts = split(enc)
    enc_came = [line.send(enc_parts[k], 1 - k) for k in both]
    *enc_came, activations, final_memory, grad_tokens = lax.optimization_barrier(
        (*enc_came, *assemble_call(parcel, parcel_other, out_keep, last_other))
    )
    enc_near = [join(enc_parts[k], enc_came[k], 1 - k) for k in both]
    enc_far = [line.send(enc_near[k], k) for k in both]

    def with_other(blocks, whole_rows=False):
        blocks = [block.reshape(PACK[0][1:]) if whole_rows else as_piece(block) for block in blocks]
        return blocks + [swap(block) for block in blocks]

    begun = unpack_call(0, with_other(enc_near) + with_other(mem_near, True), ())
    tied = lax.optimization_barrier((*enc_far, *begun))
    enc_far, begun = tied[:2], tied[2:]
    grad_out, grad_in, grad_proj, grad_qkv = unpack_call(1, with_other(enc_far) + with_other(mem_far, True), begun)
    extras = extras.astype(F32)
    gain_grads = jnp.where(front, extras[SLOTS : SLOTS + 2], extras[SLOTS + 2 : SLOTS + 4])
    return (
        activations,
        final_memory,
        grad_tokens,
        extras[:SLOTS],
        gain_grads[0:1],
        grad_qkv[None],
        grad_proj[None],
        gain_grads[1:2],
        grad_in[None],
        grad_out[None],
    )


def solution(mesh):
    placed = (
        P("dp", None),
        P("dp"),
        P(),
        P("pipe", None),
        P("pipe", None, None),
        P("pipe", None, None),
        P("pipe", None),
        P("pipe", None, None),
        P("pipe", None, None),
        P("dp", None),
        P("dp", None, None),
    )
    return jax.shard_map(
        local,
        mesh=mesh,
        in_specs=placed,
        out_specs=(
            P("dp", None),
            P("dp", None, None),
            P("dp", "pipe"),
            P(),
            P("pipe", None),
            P("pipe", None, None),
            P("pipe", None, None),
            P("pipe", None),
            P("pipe", None, None),
            P("pipe", None, None),
        ),
        check_vma=False,
    )
```

```python
import jax
import jax.numpy as jnp
from jax import lax
from jax.experimental import pallas as pl
from jax.experimental.pallas import tpu as pltpu
from jax.sharding import PartitionSpec as P

D = 512
HEADS = 8
HEAD_DIM = 64
FF = 2048
SLOTS = 64
SEG_LEN = 512
SEGS = 2
ROWS = SEG_LEN + SLOTS
TILE = 512
BLOCKS = 12
HALF = TILE // 2
PIECE = 3 * HALF

epsilon = 1e-05
masked_bias = -1000000000.0
score_scale = HEAD_DIM ** (-0.5)
exponent_scale = score_scale * 1.4426950408889634
gelu_a = 0.7978845608028654
gelu_b = 0.044715 * gelu_a

BF16 = jnp.bfloat16
F32 = jnp.float32


def dot(left, right):
    return jnp.dot(left, right, preferred_element_type=F32)


def dot_t(left, right):
    return lax.dot_general(left, right, (((1,), (1,)), ((), ())), preferred_element_type=F32)


def normalise(values):
    centred = values - jnp.mean(values, axis=-1, keepdims=True)
    spread = jnp.mean(centred * centred, axis=-1, keepdims=True)
    inverse = lax.rsqrt(spread + epsilon)
    return centred * inverse, inverse


def layer_norm(values, gain):
    return normalise(values)[0] * gain


def layer_norm_back(values, gain, grads):
    scaled, inverse = normalise(values)
    gain_grad = jnp.sum(grads * scaled, axis=0, keepdims=True)
    inner = grads * gain
    mean_inner = jnp.mean(inner, axis=-1, keepdims=True)
    mean_scaled = jnp.mean(inner * scaled, axis=-1, keepdims=True)
    return inverse * (inner - mean_inner - scaled * mean_scaled), gain_grad


def gelu_both(values):
    square = values * values
    tangent = jnp.tanh(values * (gelu_a + gelu_b * square))
    half = 0.5 + 0.5 * tangent
    slope = half + (0.5 * values) * (1.0 - tangent * tangent) * (gelu_a + 3.0 * gelu_b * square)
    return values * half, slope


def iota(shape, dim):
    return lax.broadcasted_iota(jnp.int32, shape, dim)


def repeat_matrix():
    return (iota((SLOTS, D), 0) == iota((SLOTS, D), 1) % SLOTS).astype(BF16)


def head_blocks():
    return iota((D, D), 0) // HEAD_DIM == iota((D, D), 1) // SLOTS


class Mover:
    def __init__(self, sems):
        self.sems = sems
        self.used = 0
        self.coming = {}
        self.leaving = []

    def slot(self):
        self.used += 1
        return self.sems.at[self.used - 1]

    def bring(self, target, source):
        sem = self.slot()
        pltpu.make_async_copy(source, target, sem).start()
        self.coming[id(target)] = (source, target, sem)

    def bring_either(self, target, pick_first, first, second):
        sem = self.slot()

        @pl.when(pick_first)
        def _():
            pltpu.make_async_copy(first, target, sem).start()

        @pl.when(jnp.logical_not(pick_first))
        def _():
            pltpu.make_async_copy(second, target, sem).start()

        self.coming[id(target)] = (first, target, sem)

    def need(self, *targets):
        for target in targets:
            if id(target) in self.coming:
                pltpu.make_async_copy(*self.coming.pop(id(target))).wait()

    def send(self, source, target):
        copy = pltpu.make_async_copy(source, target, self.slot())
        copy.start()
        self.leaving.append(copy)
        return copy

    def left(self, *copies):
        for copy in copies:
            copy.wait()
            self.leaving = [other for other in self.leaving if other is not copy]

    def finish(self):
        for copy in self.leaving:
            copy.wait()


def valid_keys(shape, valid_rows):
    row = iota(shape, 0)
    return (row < valid_rows) | (row >= SEG_LEN)


def encoder_attention(
    need, x, m, bias, gain, wqkv, wproj, n, qt, kv, vt, probs, inv, mixt, hidden, ready=lambda *refs: None
):
    need(x, m)
    n[:SEG_LEN] = layer_norm(x[...].astype(F32), gain).astype(BF16)
    n[SEG_LEN:] = layer_norm(m[...].astype(F32), gain).astype(BF16)
    need(wqkv)
    qt[...] = dot_t(wqkv[:, :D].T, n[:SEG_LEN]).astype(BF16)
    kv[:, :D] = dot(n[...], wqkv[:, D : 2 * D]).astype(BF16)
    values = dot(n[...], wqkv[:, 2 * D :]).astype(BF16)
    kv[:, D:] = values
    vt[...] = values.T
    ready(n, qt, kv)
    low_lanes = iota((ROWS, 128), 1) < HEAD_DIM
    ones_row = (iota((HEAD_DIM, SEG_LEN), 0) == 0).astype(BF16)

    def pair(index, carry):
        base = pl.multiple_of(index * 128, 128)
        keys = kv[:, pl.ds(base, 128)]
        spans = [pl.ds(pl.multiple_of(base + half * HEAD_DIM, HEAD_DIM), HEAD_DIM) for half in range(2)]
        left = jnp.where(low_lanes, keys, bias[...]), jnp.where(low_lanes, bias[...], keys)
        right = (
            jnp.concatenate([qt[spans[0]], ones_row], axis=0), jnp.concatenate([ones_row, qt[spans[1]]], axis=0)
        )
        both = [dot(left[half], right[half]) for half in range(2)]
        for half, scores in enumerate(both):
            head, rows = 2 * index + half, spans[half]
            top = jnp.max(scores, axis=0, keepdims=True)
            grown = jnp.exp2(scores * exponent_scale - top * exponent_scale)
            inverse = 1.0 / jnp.sum(grown, axis=0, keepdims=True)
            low = grown.astype(BF16)
            probs[head] = low
            inv[head] = inverse
            mixt[rows] = (dot(vt[rows], low) * inverse).astype(BF16)
        return carry

    lax.fori_loop(0, HEADS // 2, pair, 0)
    ready(probs, inv, mixt)
    need(wproj)
    hidden[...] = x[...].astype(F32) + dot(mixt[...].T, wproj[...])
    ready(hidden)


def encoder_ffn(need, hidden, gain, win, wout, y, nf, act, slope, total, before=None):
    need(hidden)
    nf[...] = layer_norm(hidden[...], gain).astype(BF16)
    total[...] = hidden[...]
    need(win, wout)

    def step(index, carry):
        span = pl.ds(pl.multiple_of(index * TILE, TILE), TILE)
        active, grad = gelu_both(dot(nf[...], win[:, span]))
        low = active.astype(BF16)
        act[:, span] = low
        slope[:, span] = grad.astype(BF16)
        total[...] += dot(low, wout[span])
        return carry

    if before is None:
        lax.fori_loop(0, FF // TILE, step, 0)
    else:
        for index in range(FF // TILE):
            before(index)
            step(index, 0)
    y[...] = total[...].astype(BF16)


def memory_forward(need, y, m, valid_rows, gain, ffn_gain, weights, result, kept, index, vt):
    wqkv, wproj, win, wout = weights
    n, kv, keyed, probs, inv, mixm, mixed, attended, hidden, nf, act, slope, branch = [ref.at[index] for ref in kept]
    need(m)
    mf = m[...].astype(F32)
    n[:SEG_LEN] = layer_norm(y[...].astype(F32), gain).astype(BF16)
    slots = layer_norm(mf, gain).astype(BF16)
    n[SEG_LEN:] = slots
    need(wqkv)
    kv[:, :D] = dot(n[...], wqkv[:, D : 2 * D]).astype(BF16)
    values = dot(n[...], wqkv[:, 2 * D :]).astype(BF16)
    kv[:, D:] = values
    vt[...] = values.T
    blocks = head_blocks()
    queries = dot_t(wqkv[:, :D].T, jnp.concatenate([slots] * HEADS, axis=0))
    keyed[...] = jnp.where(blocks, queries, 0.0).astype(BF16)
    scores = dot(kv[:, :D], keyed[...])
    if valid_rows is not None:
        scores = jnp.where(valid_keys((ROWS, D), valid_rows), scores, masked_bias)
    top = jnp.max(scores, axis=0, keepdims=True)
    grown = jnp.exp2(scores * exponent_scale - top * exponent_scale)
    inverse = 1.0 / jnp.sum(grown, axis=0, keepdims=True)
    probs[...] = grown.astype(BF16)
    inv[...] = inverse
    mixm[...] = jnp.where(blocks, dot(vt[...], probs[...]) * inverse, 0.0).astype(BF16)
    mixed[...] = dot_t(repeat_matrix(), mixm[...]).astype(BF16)
    need(wproj)
    attended[...] = dot(mixed[...], wproj[...])
    hidden[...] = mf + attended[...]
    nf[...] = layer_norm(hidden[...], ffn_gain).astype(BF16)
    need(win)
    active, grad = gelu_both(dot(nf[...], win[...]))
    act[...] = active.astype(BF16)
    slope[...] = grad.astype(BF16)
    need(wout)
    branch[...] = dot(act[...], wout[...])
    result[...] = (mf + jax.nn.sigmoid(branch[...]) * attended[...]).astype(BF16)


def memory_backward(go, y, m, gain, ffn_gain, weights, kept, index, grad_y, grad_m, grads):
    wqkv, wproj, win, wout = weights
    n, kv, keyed, probs, inv, mixm, mixed, attended, hidden, nf, act, slope, branch = [ref.at[index] for ref in kept]
    gb, gpre, ga, gq, gkv = [ref.at[index] for ref in grads]
    blocks = head_blocks()
    gate = jax.nn.sigmoid(branch[...])
    gof = go[...].astype(F32)
    gb[...] = (gof * attended[...] * gate * (1.0 - gate)).astype(BF16)
    gpre[...] = (slope[...].astype(F32) * dot_t(gb[...], wout[...])).astype(BF16)
    ghidden, ffn_gain_grad = layer_norm_back(hidden[...], ffn_gain, dot_t(gpre[...], win[...]))
    gattended = (ghidden + gof * gate).astype(BF16)
    ga[...] = gattended
    gmixed = dot_t(wproj[...], jnp.concatenate([gattended] * HEADS, axis=0)).astype(BF16).astype(F32)
    gmixed = jnp.where(blocks, gmixed * inv[...], 0.0)
    low_mixed = gmixed.astype(BF16)
    centre = jnp.sum(mixm[...].astype(F32) * gmixed, axis=0, keepdims=True)
    gprobs = dot(kv[:, D:], low_mixed)
    gscores = (probs[...].astype(F32) * (gprobs - centre)).astype(BF16)
    gqueries = dot(kv[:, :D].T, gscores) * score_scale
    gqueries = jnp.where(blocks, gqueries, 0.0).astype(BF16)
    gq[...] = dot_t(repeat_matrix(), gqueries).astype(BF16)
    gkv[:, :D] = (dot_t(gscores, keyed[...]) * score_scale).astype(BF16)
    gkv[:, D:] = dot_t(probs[...], low_mixed).astype(BF16)
    grows = dot_t(gkv[...], wqkv[:, D:])
    gslots = grows[SEG_LEN:] + dot_t(gq[...], wqkv[:, :D])
    grad_rows, gain_rows = layer_norm_back(y[...].astype(F32), gain, grows[:SEG_LEN])
    grad_slots, gain_slots = layer_norm_back(m[...].astype(F32), gain, gslots)
    grad_y[...] = grad_rows.astype(BF16)
    grad_m[...] = grad_slots + ghidden + gof
    return gain_rows + gain_slots, ffn_gain_grad


def encoder_ffn_backward(
    need, cot, grad_y, hidden, gain, win, wout, slope, gb, gnf, ga, ghidden, before=None, behind=None
):
    need(cot, grad_y)
    go = cot[...].astype(F32) + grad_y[...].astype(F32)
    gb[...] = go.astype(BF16)
    ghidden[...] = go
    gnf[...] = jnp.zeros_like(gnf)
    need(wout, slope, win)

    def step(index, carry):
        span = pl.ds(pl.multiple_of(index * TILE, TILE), TILE)
        low = (slope[:, span].astype(F32) * dot_t(gb[...], wout[span])).astype(BF16)
        slope[:, span] = low
        gnf[...] += dot_t(low, win[:, span])
        return carry

    if before is None:
        lax.fori_loop(0, FF // TILE, step, 0)
    else:
        for index in range(FF // TILE):
            before(index)
            step(index, 0)
            behind(index)
    need(hidden)
    grad, gain_grad = layer_norm_back(hidden[...], gain, gnf[...])
    grad = grad + ghidden[...]
    ghidden[...] = grad
    ga[...] = grad.astype(BF16)
    return gain_grad


def encoder_attention_backward(
    need, x, m, gain, wqkv, wproj, qt, kv, probs, inv, mixt, ga, ghidden, kt, gmt, gqkvt, grad_x, grad_m
):
    need(wproj, ga)
    gmt[...] = dot_t(wproj[...], ga[...]).astype(BF16)
    need(kv)
    kt[...] = kv[:, :D].T
    gqkvt[:D, SEG_LEN:] = jnp.zeros((D, SLOTS), BF16)
    empty = jnp.zeros((HEAD_DIM, SEG_LEN), BF16)
    need(inv, mixt, qt, probs)

    def pair(index, carry):
        base = pl.multiple_of(index * 128, 128)
        values = kv[:, pl.ds(pl.multiple_of(D + base, 128), 128)]
        work = []
        for half in range(2):
            head = 2 * index + half
            start = pl.multiple_of(base + half * HEAD_DIM, HEAD_DIM)
            rows = pl.ds(start, HEAD_DIM)
            scaled = gmt[rows].astype(F32) * inv[head]
            centre = jnp.sum(mixt[rows].astype(F32) * scaled, axis=0, keepdims=True)
            low = scaled.astype(BF16)
            right = jnp.concatenate([low, empty] if half == 0 else [empty, low], axis=0)
            work.append((head, start, rows, centre, low, dot(values, right)))
        for head, start, rows, centre, low, gprobs in work:
            gscores = (probs[head].astype(F32) * (gprobs - centre)).astype(BF16)
            gqkvt[pl.ds(pl.multiple_of(2 * D + start, HEAD_DIM), HEAD_DIM)] = dot_t(low, probs[head]).astype(BF16)
            gqkvt[rows, :SEG_LEN] = (dot(kt[rows], gscores) * score_scale).astype(BF16)
            gqkvt[pl.ds(pl.multiple_of(D + start, HEAD_DIM), HEAD_DIM)] = (
                dot_t(qt[rows], gscores) * score_scale
            ).astype(BF16)
        return carry

    lax.fori_loop(0, HEADS // 2, pair, 0)
    need(wqkv, x, m, ghidden)
    grows = dot(wqkv[...], gqkvt[...]).T
    grad_rows, gain_rows = layer_norm_back(x[...].astype(F32), gain, grows[:SEG_LEN])
    grad_slots, gain_slots = layer_norm_back(m[...].astype(F32), gain, grows[SEG_LEN:])
    grad_x[...] = (grad_rows + ghidden[...]).astype(BF16)
    grad_m[...] = grad_slots
    return gain_rows + gain_slots


def spot_of(block):
    if block < 8:
        return block // 2, pl.ds(block % 2, 1), slice(0, LONG_ROWS)
    return block - 8, pl.ds(0, 2), slice(LONG_ROWS, CHUNK)


def halves(core):
    return [pl.ds(pl.multiple_of(side * HALF, HALF), HALF) for side in (core, 1 - core)]


def memory_weights(mover, core, kept, grads, packs, stage, short_stage, act_t, nf_t, mixed_t, slots_t, n0_t, n1_t):
    n, kv, keyed, probs, inv, mixm, mixed, attended, hidden, nf, act, slope, branch = kept
    gb, gpre, ga, gq, gkv = grads

    def both(ref, *index):
        return jnp.concatenate([ref[(k,) + index] for k in range(SEGS)], axis=0)

    whole = slice(None)
    for block in range(4):
        span = slice(block * TILE, (block + 1) * TILE)
        act_t[span] = both(act, whole, span).T
    nf_t[...] = both(nf).T
    mixed_t[...] = both(mixed).T
    slots_t[...] = both(n, slice(SEG_LEN, ROWS)).T
    n0_t[...] = n[0].T
    n1_t[...] = n[1].T
    flying = [None] * BLOCKS
    for pack, rows in zip(packs, halves(core)):

        def put(block, value, pack=pack):
            if flying[block] is not None:
                mover.left(flying[block])
            piece, half, rows = spot_of(block)
            held = stage.at[block] if block < 8 else short_stage.at[block - 8]
            held[...] = value.astype(BF16).reshape(held.shape)
            flying[block] = mover.send(held, pack.at[piece, half, :, rows])

        for block in range(4):
            span = slice(block * TILE, (block + 1) * TILE)
            put(block, dot(act_t.at[span][rows], both(gb)))
            put(4 + block, dot(nf_t[rows], both(gpre, whole, span)))
        put(8, dot(mixed_t[rows], both(ga)))
        put(9, dot(slots_t[rows], both(gq)))
        for block in range(2):
            span = slice(block * TILE, (block + 1) * TILE)
            put(10 + block, dot(n0_t[rows], gkv[0, :, span]) + dot(n1_t[rows], gkv[1, :, span]))


def encoder_ffn_weights(need, core, acts, gbs, nfs, gpres, packs, left, left_nf):
    need(*gbs, *acts)

    def outer(block, carry):
        span = pl.ds(pl.multiple_of(block * TILE, TILE), TILE)
        for k in range(SEGS):
            left[k] = acts[k][:, span].T
        start = pl.multiple_of(block * HALF, HALF)
        for pack, rows in zip(packs, halves(core)):
            pack[pl.ds(start, HALF)] = (
                dot(left[0, rows], gbs[0][...]) + dot(left[1, rows], gbs[1][...])
            ).astype(BF16)
        return carry

    lax.fori_loop(0, 4, outer, 0)
    need(*nfs, *gpres)
    for k in range(SEGS):
        left_nf[k] = nfs[k][...].T

    def inner(block, carry):
        span = pl.ds(pl.multiple_of(block * TILE, TILE), TILE)
        start = pl.multiple_of((4 + block) * HALF, HALF)
        for pack, rows in zip(packs, halves(core)):
            pack[pl.ds(start, HALF)] = (
                dot(left_nf[0, rows], gpres[0][:, span]) + dot(left_nf[1, rows], gpres[1][:, span])
            ).astype(BF16)
        return carry

    lax.fori_loop(0, 4, inner, 0)


def encoder_attention_weights(need, core, mixts, gas, ns, gqkvts, packs, left):
    need(*mixts, *gas)
    for pack, rows in zip(packs, halves(core)):
        pack[:HALF] = (dot(mixts[0][rows], gas[0][...]) + dot(mixts[1][rows], gas[1][...])).astype(BF16)
    need(*ns, *gqkvts)
    for k in range(SEGS):
        left[k] = ns[k][...].T

    def third(block, carry):
        span = pl.ds(pl.multiple_of(block * TILE, TILE), TILE)
        start = pl.multiple_of((1 + block) * HALF, HALF)
        for pack, rows in zip(packs, halves(core)):
            pack[pl.ds(start, HALF)] = (
                dot_t(left[0, rows], gqkvts[0][span]) + dot_t(left[1, rows], gqkvts[1][span])
            ).astype(BF16)
        return carry

    lax.fori_loop(0, 3, third, 0)


SCALAR = pl.BlockSpec(memory_space=pltpu.SMEM)
HELD = pl.BlockSpec(memory_space=pltpu.VMEM)
FAR = pl.BlockSpec(memory_space=pl.ANY)

WEIGHTS = (((D, 3 * D), BF16), ((D, D), BF16), ((D, FF), BF16), ((FF, D), BF16))
ROW_LOW = ((SEG_LEN, D), BF16)
ROW_FULL = ((SEG_LEN, D), F32)
WIDE = ((SEG_LEN, FF), BF16)
ALL_LOW = ((ROWS, D), BF16)
ALL_TURNED = ((D, ROWS), BF16)
TURNED = ((D, SEG_LEN), BF16)
SLOT_LOW = ((SLOTS, D), BF16)
SLOT_FULL = ((SLOTS, D), F32)
SLOT_WIDE = ((SLOTS, FF), BF16)
SLOT_TURNED = ((D, SEGS * SLOTS), BF16)
SQUARE = ((D, D), BF16)
PROBS = ((HEADS, ROWS, SEG_LEN), BF16)
INVERSE = ((HEADS, 1, SEG_LEN), F32)
KEYS_VALUES = ((ROWS, 2 * D), BF16)
GRAD_TURNED = ((3 * D, ROWS), BF16)
GAINS = ((8, D), F32)
BIAS = ((ROWS, 128), BF16)
EXTRAS = SLOTS + 16
PARCEL = SEGS * SEG_LEN + SLOTS
CHUNKS = 4
LONG_ROWS = HALF // CHUNKS
SHORT_ROWS = LONG_ROWS // 2
CHUNK = LONG_ROWS + SHORT_ROWS
PACK = ((4, 2, CHUNKS, CHUNK, D), BF16)


def pack_of(blocks):
    return ((blocks * HALF, D), BF16)


def twice(item):
    return ((SEGS,) + item[0], item[1])


def call(body, kinds, outs, scratch, copies, name, aliases={}):
    out_kinds, outs = zip(*outs)
    specs = {"s": SCALAR, "v": HELD, "f": FAR}
    inputs = len(kinds)

    def kernel(*refs):
        ins, results = refs[:inputs], refs[inputs : inputs + len(outs)]
        held, sems = refs[inputs + len(outs) : -1], refs[-1]
        body(Mover(sems), ins, results, held)

    light = name in ("unpack", "assemble")
    cost = pl.CostEstimate(
        flops=1_000_000 if light else 20_000_000_000, bytes_accessed=1_000_000 if light else 10_000_000, transcendentals=0
    )
    return pl.pallas_call(
        kernel,
        out_shape=[jax.ShapeDtypeStruct(shape, kind) for shape, kind in outs],
        in_specs=[specs[kind] for kind in kinds],
        out_specs=[specs[kind] for kind in out_kinds],
        scratch_shapes=[pltpu.VMEM(shape, kind) for shape, kind in scratch] + [pltpu.SemaphoreType.DMA((copies,))],
        compiler_params=pltpu.CompilerParams(vmem_limit_bytes=63 * 2**20),
        cost_estimate=cost,
        input_output_aliases=aliases,
        name=name,
    )


def own_gains(own, other, front):
    return jnp.where(front, own[...], other[...])


def document_rows(core, segment):
    return pl.ds(pl.multiple_of((core * SEGS + segment) * SEG_LEN, SEG_LEN), SEG_LEN)


def column_halves(core):
    return [pl.ds(pl.multiple_of(side * (D // 2), D // 2), D // 2) for side in (core, 1 - core)]


def first_kernel(mover, ins, outs, held):
    tokens, m, gains_own, gains_other, qkv_own, qkv_other, proj_own, proj_other = ins
    x, n, qt, kv, probs, inv, mixt, hidden, vt, wqkv, wproj, bias = held
    core = lax.axis_index("pipe")
    gains = own_gains(gains_own, gains_other, core == 0)
    bias[...] = jnp.zeros_like(bias)
    mover.bring(x, tokens.at[document_rows(core, 0)])
    mover.bring_either(wqkv, core == 0, qkv_own, qkv_other)
    mover.bring_either(wproj, core == 0, proj_own, proj_other)
    targets = dict(zip((id(ref) for ref in (hidden, n, qt, kv, probs, inv, mixt)), outs))

    def ready(*sources):
        for source in sources:
            mover.send(source, targets[id(source)])

    encoder_attention(
        mover.need, x, m, bias, gains[0:1], wqkv, wproj, n, qt, kv, vt, probs, inv, mixt, hidden, ready
    )
    mover.finish()


FIRST = (ROW_FULL, ALL_LOW, TURNED, KEYS_VALUES, PROBS, INVERSE, TURNED)


def first_call(tokens, m, gains, weights):
    return call(
        first_kernel,
        "fvvvffff",
        [("f", item) for item in FIRST],
        [ROW_LOW, ALL_LOW, TURNED, KEYS_VALUES, PROBS, INVERSE, TURNED, ROW_FULL, ALL_TURNED, WEIGHTS[0], WEIGHTS[1], BIAS],
        10,
        "encoder_attention",
    )(tokens, m, *gains, *weights[0], *weights[1])


MEMORY_KEPT = (
    ALL_LOW, KEYS_VALUES, SQUARE, ALL_LOW, ((1, D), F32), SQUARE, SLOT_LOW, SLOT_FULL, SLOT_FULL,
    SLOT_LOW, SLOT_WIDE, SLOT_WIDE, SLOT_FULL,
)
MEMORY_GRADS = (SLOT_LOW, SLOT_WIDE, SLOT_LOW, SLOT_LOW, KEYS_VALUES)


def middle_kernel(mover, ins, outs, held):
    lengths, m0, gains_own, gains_other, cot_memory, hidden0, tokens, cots = ins[:8]
    pairs = ins[8:]
    (parcel, mine, theirs, out_nf, out_act, out_slope, out_n, out_mixt, out_gb, out_ga, out_gqkvt, out_grad_y, out_grad_x,
     out_grad_m, out_gains) = outs
    out_y = [parcel.at[pl.ds(k * SEG_LEN, SEG_LEN)] for k in range(SEGS)]
    out_final = parcel.at[pl.ds(SEGS * SEG_LEN, SLOTS)]
    enc_weights, mem_weights, held = held[:4], held[4:8], held[8:]
    kept, held = held[: len(MEMORY_KEPT)], held[len(MEMORY_KEPT) :]
    grads, held = held[: len(MEMORY_GRADS)], held[len(MEMORY_GRADS) :]
    (x, cot, cot_slots, hidden, n, qt, kv, probs, inv, mixt, nf, act, slope, y0, y1, turned, total, gnf, gmt, gb, ga,
     gqkvt, grad_y, grad_x, m1, final, grad_m, grad_m1, stage, short_stage, act_t, nf_t, mixed_t, slots_t, bias) = held
    core = lax.axis_index("pipe")
    front = core == 0
    enc_gains = own_gains(gains_own, gains_other, front)
    mem_gains = own_gains(gains_other, gains_own, front)
    valid_rows = lengths[core] - SEG_LEN
    lanes = iota(BIAS[0], 1) % HEAD_DIM == 0
    bias[...] = jnp.where(lanes & ~valid_keys(BIAS[0], valid_rows), masked_bias, 0.0).astype(BF16)
    need = mover.need
    wqkv, wproj, win, wout = enc_weights
    mover.bring(hidden, hidden0)
    tiles = []
    for index in range(FF // TILE):
        span = pl.ds(index * TILE, TILE)
        tile = win.at[:, span], wout.at[span]
        mover.bring_either(tile[0], front, pairs[4].at[:, span], pairs[5].at[:, span])
        mover.bring_either(tile[1], front, pairs[6].at[span], pairs[7].at[span])
        tiles.append(tile)

    def first_tile(tile):
        need(*tiles[tile])
        if tile:
            return
        for index in range(4):
            own, other = pairs[2 * index : 2 * index + 2]
            mover.bring_either(mem_weights[index], front, other, own)
        mover.bring(x, tokens.at[document_rows(core, 1)])
        for index in (0, 1):
            mover.bring_either(enc_weights[index], front, *pairs[2 * index : 2 * index + 2])
        mover.bring(cot_slots, cot_memory.at[core])
        mover.bring(cot, cots.at[document_rows(core, 1)])

    enc_attn, enc_ffn = enc_gains[0:1], enc_gains[1:2]
    mem_attn, mem_ffn = mem_gains[0:1], mem_gains[1:2]

    encoder_ffn(need, hidden, enc_ffn, win, wout, y0, nf, act, slope, total, first_tile)
    mover.send(y0, out_y[0])
    early = [mover.send(nf, out_nf.at[0]), mover.send(act, out_act.at[0]), mover.send(slope, out_slope.at[0])]
    memory_forward(need, y0, m0, None, mem_attn, mem_ffn, mem_weights, m1, kept, 0, turned)
    encoder_attention(need, x, m1, bias, enc_attn, wqkv, wproj, n, qt, kv, turned, probs, inv, mixt, hidden)
    mover.send(n, out_n)
    mover.send(mixt, out_mixt)
    mover.left(*early)
    encoder_ffn(need, hidden, enc_ffn, win, wout, y1, nf, act, slope, total)
    mover.send(y1, out_y[1])
    mover.send(nf, out_nf.at[1])
    mover.send(act, out_act.at[1])
    memory_forward(need, y1, m1, valid_rows, mem_attn, mem_ffn, mem_weights, final, kept, 1, turned)
    mover.send(final, out_final)

    need(cot_slots)
    attn_gain1, ffn_gain1 = memory_backward(
        cot_slots, y1, m1, mem_attn, mem_ffn, mem_weights, kept, 1, grad_y, grad_m, grads
    )
    out_gains[1:2] = encoder_ffn_backward(need, cot, grad_y, hidden, enc_ffn, win, wout, slope, gb, gnf, ga, total)
    mover.send(gb, out_gb)
    mover.send(ga, out_ga)
    mover.send(slope, out_slope.at[1])
    out_gains[0:1] = encoder_attention_backward(
        need, x, m1, enc_attn, wqkv, wproj, qt, kv, probs, inv, mixt, ga, total, turned, gmt, gqkvt, grad_x, grad_m1
    )
    turned_out = mover.send(gqkvt, out_gqkvt)
    mover.send(grad_x, out_grad_x)
    grad_m[...] = grad_m[...] + grad_m1[...].astype(BF16).astype(F32)
    attn_gain0, ffn_gain0 = memory_backward(
        grad_m, y0, m0, mem_attn, mem_ffn, mem_weights, kept, 0, grad_y, out_grad_m, grads
    )
    mover.send(grad_y, out_grad_y)
    out_gains[2:3] = attn_gain0 + attn_gain1
    out_gains[3:4] = ffn_gain0 + ffn_gain1
    out_gains[4:8] = jnp.zeros((4, D), F32)
    mover.left(turned_out)
    memory_weights(
        mover, core, kept, grads, (mine, theirs), stage, short_stage, act_t, nf_t, mixed_t, slots_t,
        gqkvt.at[pl.ds(0, D)], gqkvt.at[pl.ds(D, D)],
    )
    mover.finish()


def middle_call(lengths, m0, gains, cot_memory, hidden, tokens, cots, weights):
    outs = [
        ("f", ((PARCEL, D), BF16)), ("f", PACK), ("f", PACK), ("f", twice(ROW_LOW)), ("f", twice(WIDE)),
        ("f", twice(WIDE)), ("f", ALL_LOW), ("f", TURNED), ("f", ROW_LOW), ("f", ROW_LOW), ("f", GRAD_TURNED),
        ("f", ROW_LOW), ("f", ROW_LOW), ("v", SLOT_FULL), ("v", GAINS),
    ]
    scratch = [
        *WEIGHTS, *WEIGHTS, *[twice(item) for item in MEMORY_KEPT], *[twice(item) for item in MEMORY_GRADS],
        ROW_LOW, ROW_LOW, SLOT_LOW, ROW_FULL, ALL_LOW, TURNED, KEYS_VALUES, PROBS, INVERSE, TURNED, ROW_LOW, WIDE,
        WIDE, ROW_LOW, ROW_LOW, ALL_TURNED, ROW_FULL, ROW_FULL, TURNED, ROW_LOW, ROW_LOW, GRAD_TURNED, ROW_LOW,
        ROW_LOW, SLOT_LOW, SLOT_LOW, SLOT_FULL, SLOT_FULL, ((8, 1, CHUNKS, LONG_ROWS, D), BF16), ((4, 2, CHUNKS, SHORT_ROWS, D), BF16),
        ((FF, SEGS * SLOTS), BF16),
        SLOT_TURNED, SLOT_TURNED, SLOT_TURNED, BIAS,
    ]
    return call(middle_kernel, "svvvffff" + "f" * 8, outs, scratch, 72, "middle")(
        lengths, m0, *gains, cot_memory, hidden, tokens, cots,
        *[item for pair in weights for item in pair],
    )


def feed_kernel(mover, ins, outs, held):
    gains_own, gains_other, grad_gains, cots, grad_y0, hidden0, slopes, in_own, in_other, out_own, out_other = ins
    out_gpre, out_gb, out_ga, out_ghidden, out_gains = outs
    win, wout, cot, grad_y, hidden, gpre, gb, gnf, ga, ghidden = held
    core = lax.axis_index("pipe")
    gains = own_gains(gains_own, gains_other, core == 0)
    mover.bring(cot, cots.at[document_rows(core, 0)])
    mover.bring(grad_y, grad_y0)
    spans = [pl.ds(index * TILE, TILE) for index in range(FF // TILE)]
    tiles = []
    for span in spans:
        tile = wout.at[span], gpre.at[:, span], win.at[:, span]
        mover.bring_either(tile[0], core == 0, out_own.at[span], out_other.at[span])
        mover.bring(tile[1], slopes.at[0, :, span])
        mover.bring_either(tile[2], core == 0, in_own.at[:, span], in_other.at[:, span])
        tiles.append(tile)
    mover.bring(hidden, hidden0)
    gain_grad = encoder_ffn_backward(
        mover.need, cot, grad_y, hidden, gains[1:2], win, wout, gpre, gb, gnf, ga, ghidden,
        lambda index: mover.need(*tiles[index]),
        lambda index: mover.send(gpre.at[:, spans[index]], out_gpre.at[:, spans[index]]),
    )
    for source, target in ((gb, out_gb), (ga, out_ga), (ghidden, out_ghidden)):
        mover.send(source, target)
    out_gains[...] = grad_gains[...]
    out_gains[1:2] = grad_gains[1:2] + gain_grad
    mover.finish()


def feed_call(gains, grad_gains, cots, grad_y, hidden, slopes, weights):
    return call(
        feed_kernel,
        "vvvffffffff",
        [("f", WIDE), ("f", ROW_LOW), ("f", ROW_LOW), ("f", ROW_FULL), ("v", GAINS)],
        [WEIGHTS[2], WEIGHTS[3], ROW_LOW, ROW_LOW, ROW_FULL, WIDE, ROW_LOW, ROW_FULL, ROW_LOW, ROW_FULL],
        24,
        "encoder_feed",
    )(*gains, grad_gains, cots, grad_y, hidden, slopes, *weights[2], *weights[3])


def ordered_pieces(device):
    pieces = []
    for part in range(2):
        stays = (device >> part) & 1
        pieces.append((2 * part + 1 - stays, 2 * part + stays))
    return pieces


def send_pieces(mover, device, packs, mine, soon, late, rows):
    for part, (goes, stays) in enumerate(ordered_pieces(device)):
        goes = pl.ds(pl.multiple_of(goes * rows, rows), rows)
        stays = pl.ds(pl.multiple_of(stays * rows, rows), rows)
        mover.send(packs[1].at[goes], soon[part] if isinstance(soon, (list, tuple)) else soon.at[pl.ds(part * rows, rows)])
        mover.send(packs[0].at[goes], mine.at[pl.ds(part * rows, rows)])
        mover.send(packs[0].at[stays], mine.at[pl.ds((2 + part) * rows, rows)])
        mover.send(packs[1].at[stays], late.at[pl.ds(part * rows, rows)])


LONG = 2 * HALF
SHORT = HALF


def outer_kernel(mover, ins, outs, held):
    acts, slopes, nfs, gpre0, gb0, gb1 = ins[:6]
    (m0, gains_own, gains_other, grad_gains, grad_m, tokens, qt0, kv0, probs0, inv0, mixt0, ga0, ghidden0, grad_x1,
     qkv_own, qkv_other, proj_own, proj_other) = ins[6:]
    mine, soon, late, out_keep, out_gqkvt, parcel = outs
    acts_held, nfs_held, gpres_held, gbs_held = [held[2 * k : 2 * k + 2] for k in range(4)]
    packs, left, left_nf = held[8:10], held[10], held[11]
    (wqkv, wproj, x, qt, kv, probs, inv, mixt, ga, ghidden, gqkvt, kt, gmt, grad_x, grad_x1_held, grad_m0,
     extras) = held[12:]
    core, device = lax.axis_index("pipe"), lax.axis_index("dp")
    gains = own_gains(gains_own, gains_other, core == 0)
    need = mover.need
    for target, source in zip(gbs_held, (gb0, gb1)):
        mover.bring(target, source)
    for k in range(SEGS):
        mover.bring(acts_held[k], acts.at[k])
    need(*gbs_held, *acts_held)
    for k in range(SEGS):
        mover.bring(nfs_held[k], nfs.at[k])
    mover.bring(gpres_held[0], gpre0)
    mover.bring(gpres_held[1], slopes.at[1])
    mover.bring_either(wproj, core == 0, proj_own, proj_other)
    mover.bring(ga, ga0)
    mover.bring(kv, kv0)
    mover.bring(inv, inv0)
    mover.bring(mixt, mixt0)
    mover.bring(qt, qt0)
    mover.bring(probs, probs0)
    mover.bring_either(wqkv, core == 0, qkv_own, qkv_other)
    mover.bring(x, tokens.at[document_rows(core, 0)])
    mover.bring(ghidden, ghidden0)
    mover.bring(grad_x1_held, grad_x1)
    encoder_ffn_weights(need, core, acts_held, gbs_held, nfs_held, gpres_held, packs, left, left_nf)
    send_pieces(mover, device, packs, mine, soon, late, LONG)
    gain_grad = encoder_attention_backward(
        need, x, m0, gains[0:1], wqkv, wproj, qt, kv, probs, inv, mixt, ga, ghidden, kt, gmt, gqkvt, grad_x, grad_m0
    )
    mover.send(gqkvt, out_gqkvt)
    extras[:SLOTS] = (grad_m[...] + grad_m0[...]).astype(BF16)
    low = jnp.concatenate(
        [grad_gains[0:1] + gain_grad, grad_gains[1:4], jnp.zeros((EXTRAS - SLOTS - 4, D), F32)], axis=0
    )
    extras[SLOTS:] = low.astype(BF16)
    mover.send(extras, parcel.at[pl.ds(0, EXTRAS)])
    keep, give = column_halves(core)
    for segment, source in enumerate((grad_x, grad_x1_held)):
        need(source)
        columns = pl.ds(segment * (D // 2), D // 2)
        mover.send(source.at[:, keep], out_keep.at[:, columns])
        mover.send(source.at[:, give], parcel.at[pl.ds(EXTRAS, SEG_LEN), columns])
    mover.finish()


def outer_call(
    acts, slopes, nfs, gpre0, gb0, gb1, m0, gains, grad_gains, grad_m, tokens, qt0, kv0, probs0, inv0, mixt0, ga0,
    ghidden0, grad_x1, weights,
):
    return call(
        outer_kernel,
        "ffffff" + "vvvvv" + "f" * 13,
        [
            ("f", ((4 * LONG, D), BF16)), ("f", ((2 * LONG, D), BF16)), ("f", ((2 * LONG, D), BF16)), ("f", ROW_LOW),
            ("f", GRAD_TURNED), ("f", ((EXTRAS + SEG_LEN, D), BF16)),
        ],
        [
            WIDE, WIDE, ROW_LOW, ROW_LOW, WIDE, WIDE, ROW_LOW, ROW_LOW, ((4 * LONG, D), BF16), ((4 * LONG, D), BF16),
            twice(SQUARE), twice(SQUARE), WEIGHTS[0], WEIGHTS[1], ROW_LOW, TURNED, KEYS_VALUES, PROBS, INVERSE,
            TURNED, ROW_LOW, ROW_FULL, GRAD_TURNED, ALL_TURNED, TURNED, ROW_LOW, ROW_LOW, SLOT_FULL,
            ((EXTRAS, D), BF16),
        ],
        33,
        "encoder_outer",
    )(
        acts, slopes, nfs, gpre0, gb0, gb1, m0, *gains, grad_gains, grad_m, tokens, qt0, kv0, probs0, inv0, mixt0,
        ga0, ghidden0, grad_x1, *weights[0], *weights[1],
    )


def inner_kernel(mover, ins, outs, held):
    mine, *soon, late = outs
    packs, left = held[8:10], held[10]
    for target, source in zip(held, ins):
        mover.bring(target, source)
    encoder_attention_weights(
        mover.need, lax.axis_index("pipe"), held[0:2], held[2:4], held[4:6], held[6:8], packs, left
    )
    send_pieces(mover, lax.axis_index("dp"), packs, mine, soon, late, SHORT)
    mover.finish()


def inner_call(*operands):
    pack = ((4 * SHORT, D), BF16)
    return call(
        inner_kernel,
        "ffffffff",
        [("f", pack), ("f", ((SHORT, D), BF16)), ("f", ((SHORT, D), BF16)), ("f", ((2 * SHORT, D), BF16))],
        [TURNED, TURNED, ROW_LOW, ROW_LOW, ALL_LOW, ALL_LOW, GRAD_TURNED, GRAD_TURNED, pack, pack, twice(ALL_TURNED)],
        16,
        "encoder_inner",
    )(*operands)


def assemble_kernel(mover, ins, outs, held):
    parcel, parcel_other, keep0, last_other = ins
    activations, final_memory, grad_tokens = outs
    core = lax.axis_index("pipe")
    rows = SEGS * SEG_LEN
    start = 0
    for source, y, final in zip((parcel, parcel_other), held[0:2], held[2:4]):
        mover.bring(y, source.at[pl.ds(start, rows)])
        mover.bring(final, source.at[pl.ds(start + rows, SLOTS)])
    keep, give = held[4:6]
    mover.bring(keep, keep0)
    mover.bring(give, last_other.at[pl.ds(EXTRAS, SEG_LEN)])
    for document, y, final, grads in zip((core, 1 - core), held[0:2], held[2:4], held[4:6]):
        mover.need(y, final, grads)
        mover.send(y, activations.at[pl.ds(pl.multiple_of(document * rows, rows), rows)])
        mover.send(final, final_memory.at[document])
        for segment in range(SEGS):
            columns = grads.at[:, pl.ds(segment * (D // 2), D // 2)]
            mover.send(columns, grad_tokens.at[document_rows(document, segment)])
    mover.finish()


def assemble_call(*operands):
    rows = 2 * SEGS * SEG_LEN
    outs = [("f", ((rows, D), BF16)), ("f", ((2, SLOTS, D), BF16)), ("f", ((rows, D // 2), BF16))]
    y = ((SEGS * SEG_LEN, D), BF16)
    return call(
        assemble_kernel, "ffff", outs, [y, y, SLOT_LOW, SLOT_LOW, ROW_LOW, ROW_LOW], 16, "assemble"
    )(*operands)


def place_block(block):
    if block < 4:
        return 0, lambda row: (pl.ds(block * TILE + row, HALF), slice(None))
    if block < 8:
        return 1, lambda row: (pl.ds(row, HALF), slice((block - 4) * TILE, (block - 3) * TILE))
    if block == 8:
        return 2, lambda row: (pl.ds(row, HALF), slice(None))
    return 3, lambda row: (pl.ds(row, HALF), slice((block - 9) * TILE, (block - 8) * TILE))


def unpack_kernel(distance, mover, ins, outs, held):
    pieces, wide, short_wide = held
    core = lax.axis_index("pipe")
    device = lax.axis_index("dp")
    for index in range(4):
        mover.bring_either(pieces.at[index], core == 0, ins[index], ins[4 + index])
    arrivals = list(mover.coming.values())
    for index in range(4):
        side, part = index // 2, index % 2
        pltpu.make_async_copy(*arrivals[index]).wait()
        near = (device >> part) & 1
        piece = 2 * part + (near if distance == 0 else 1 - near)
        row = pl.multiple_of((core if side == 0 else 1 - core) * HALF, HALF)
        for half in range(2):
            value = pieces[index, half, :, :LONG_ROWS].reshape(HALF, D).astype(F32)
            wide[index, half] = value
            if part == 0:
                start = pl.multiple_of((2 * piece + half) * TILE + row, HALF)
                mover.send(wide.at[index, half], outs[0].at[pl.ds(start, HALF)])
            else:
                column = pl.multiple_of((2 * (piece - 2) + half) * TILE, TILE)
                mover.send(wide.at[index, half], outs[1].at[pl.ds(row, HALF), pl.ds(column, TILE)])
        short_wide[index] = pieces[index, :, :, LONG_ROWS:].reshape(HALF, D).astype(F32)
        if part == 0:
            sem = mover.slot()
            targets = (outs[2].at[pl.ds(row, HALF)], outs[3].at[pl.ds(row, HALF), pl.ds(0, TILE)])
            for which, target in enumerate(targets):

                @pl.when(piece == which)
                def _(target=target):
                    pltpu.make_async_copy(short_wide.at[index], target, sem).start()

            mover.leaving.append(pltpu.make_async_copy(short_wide.at[index], targets[0], sem))
        else:
            column = pl.multiple_of((piece - 1) * TILE, TILE)
            mover.send(short_wide.at[index], outs[3].at[pl.ds(row, HALF), pl.ds(column, TILE)])
    mover.finish()


def unpack_call(distance, sources, begun):
    outs = [((FF, D), F32), ((D, FF), F32), ((D, D), F32), ((D, 3 * D), F32)]

    def body(mover, ins, results, held):
        unpack_kernel(distance, mover, ins, results, held)

    return call(
        body,
        "f" * (len(sources) + len(begun)),
        [("f", item) for item in outs],
        [((4, 2, CHUNKS, CHUNK, D), BF16), ((4, 2, HALF, D), F32), ((4, HALF, D), F32)],
        16,
        "unpack",
        {len(sources) + k: k for k in range(len(begun))},
    )(*sources, *begun)


def total_of(blocks):
    return sum(block.astype(F32) for block in blocks).astype(BF16)


def fold(outputs):
    arrays = []
    plan = []
    if any(rows % 16 for entries in outputs for rows, _ in entries):
        device = lax.axis_index("dp")
        sums = [
            [total_of([rows_of(array, start(device), rows) for array, start in pieces]) for rows, pieces in entries]
            for entries in outputs
        ]
        return [jnp.concatenate(entries, axis=0) for entries in sums]
    for entries in outputs:
        for rows, pieces in entries:
            for array, start in pieces:
                if not any(array is other for other in arrays):
                    arrays.append(array)
    for entries in outputs:
        plan.append([
            (rows, [([array is other for other in arrays].index(True), start) for array, start in pieces])
            for rows, pieces in entries
        ])
    sizes = [sum(rows for rows, _ in entries) for entries in plan]
    total = sum(rows * len(pieces) for entries in plan for rows, pieces in entries)

    def body(mover, ins, results, held):
        gathered, summed = held
        device = lax.axis_index("dp")
        arrivals, done = [], 0
        for entries in plan:
            for rows, pieces in entries:
                group = []
                for index, start in pieces:
                    target = gathered.at[pl.ds(done, rows)]
                    first = pl.multiple_of(jnp.asarray(start(device), jnp.int32), 16)
                    mover.bring(target, ins[index].at[pl.ds(first, rows)])
                    group.append((target, done))
                    done += rows
                arrivals.append(group)
        arrivals, done = iter(arrivals), 0
        for entries, size, result in zip(plan, sizes, results):
            begin = done
            for rows, pieces in entries:
                group = next(arrivals)
                mover.need(*[target for target, _ in group])
                summed[done : done + rows] = total_of([gathered[row : row + rows] for _, row in group])
                done += rows
            mover.send(summed.at[pl.ds(begin, size)], result)
        mover.finish()

    pieces_count = sum(len(pieces) for entries in plan for _, pieces in entries)
    return call(
        body, "f" * len(arrays), [("f", ((size, D), BF16)) for size in sizes],
        [((total, D), BF16), ((sum(sizes), D), BF16)], pieces_count + len(sizes), "fold",
    )(*arrays)


def swap(block):
    return lax.ppermute(block, "pipe", [(0, 1), (1, 0)])


def neighbour(block, bit):
    devices = lax.axis_size("dp")
    return lax.ppermute(block, "dp", [(k, k ^ (1 << bit)) for k in range(devices)])


def bit_of(bit):
    return (lax.axis_index("dp") >> bit) & 1


def after(value, *others):
    return lax.optimization_barrier((value,) + others)[0]


def rows_of(block, start, size):
    return lax.dynamic_slice_in_dim(block, start, size)


class Part:
    def __init__(self, size, pieces):
        self.size = size
        self.pieces = pieces

    def sum_of(self, shift, size):
        return total_of([rows_of(array, start + shift, size) for array, start in self.pieces])

    def value(self):
        return self.sum_of(0, self.size)


class Lazy:
    def __init__(self, size, pieces):
        self.size = size
        self.pieces = [(array, start if callable(start) else (lambda device, start=start: start)) for array, start in pieces]

    def entry(self):
        return self.size, self.pieces

    def half(self, bit, stays):
        size = self.size // 2

        def moved(start):
            def first(device):
                here = (device >> bit) & 1
                return start(device) + (here if stays else 1 - here) * size

            return first

        return Lazy(size, [(array, moved(start)) for array, start in self.pieces])

    def settled(self, bit, came, row):
        kept = self.half(bit, True)
        return Lazy(kept.size, kept.pieces + [(came, lambda device: row)])


def settle_lazy(parts, bit, came):
    results, done = [], 0
    for part in parts:
        results.append(part.settled(bit, came, done))
        done += results[-1].size
    return results


class Line:
    def __init__(self):
        self.last = None

    def send(self, block, bit):
        if self.last is not None:
            block = after(block, self.last)
        self.last = block
        return neighbour(block, bit)

    def trade(self, parts, bit, extra=None):
        give = [part.sum_of((1 - bit_of(bit)) * (part.size // 2), part.size // 2) for part in parts]
        if extra is not None:
            give.append(extra)
        return self.send(jnp.concatenate(give, axis=0) if len(give) > 1 else give[0], bit)


def settle(parts, bit, came):
    results, done = [], 0
    for part in parts:
        half = part.size // 2
        shift = bit_of(bit) * half
        results.append(Part(half, [(array, start + shift) for array, start in part.pieces] + [(came, done)]))
        done += half
    return results, came[done:]


def as_piece(block):
    rows = block.shape[1]
    if rows != CHUNK:
        long = rows * LONG_ROWS // CHUNK
        long, short = block[:, :long].reshape(-1, LONG_ROWS, D), block[:, long:].reshape(-1, SHORT_ROWS, D)
        block = jnp.concatenate([long, short], axis=1)
    return block.reshape(PACK[0][1:])


def join(block, came, bit):
    low = bit_of(bit) == 0
    return jnp.concatenate([jnp.where(low, block, came), jnp.where(low, came, block)], axis=0)


def local(
    tokens, lengths, memory_init, attn_gain, qkv_weight, proj_weight, ffn_gain, in_weight, out_weight,
    cot_tokens, cot_memory,
):
    core = lax.axis_index("pipe")
    front = core == 0
    gains = jnp.concatenate([attn_gain, ffn_gain], axis=0)
    gains = (gains, swap(gains))
    weights = [(held[0], swap(held[0])) for held in (qkv_weight, proj_weight, in_weight, out_weight)]

    hidden0, n0, qt0, kv0, probs0, inv0, mixt0 = first_call(tokens, memory_init, gains, weights)
    (parcel, mem_mine, mem_theirs, nfs, acts, slopes, n1, mixt1, gb1, ga1, gqkvt1, grad_y0, grad_x1, grad_m,
     grad_gains) = middle_call(lengths, memory_init, gains, cot_memory, hidden0, tokens, cot_tokens, weights)
    mem_theirs, parcel_other = swap(mem_theirs), swap(parcel)
    gpre0, gb0, ga0, ghidden0, grad_gains = feed_call(
        gains, grad_gains, cot_tokens, grad_y0, hidden0, slopes, weights
    )

    bits = lax.axis_size("dp").bit_length() - 1
    line = Line()
    both = range(2)
    mem_theirs, gb0 = lax.optimization_barrier((mem_theirs, gb0))
    rows = 2 * PIECE
    mem_mine, mem_theirs = mem_mine.reshape(-1, D), mem_theirs.reshape(-1, D)
    mem = [[Part(rows, [(mem_mine, k * rows), (mem_theirs, k * rows)])] for k in both]
    mem_came = [line.trade(mem[k], k) for k in both]
    long_mine, long_soon, long_late, out_keep, gqkvt0, last_parcel = outer_call(
        acts, slopes, nfs, gpre0, after(gb0, line.last), gb1, memory_init, gains, grad_gains, grad_m, tokens, qt0, kv0,
        probs0, inv0, mixt0, ga0, ghidden0, grad_x1, weights,
    )
    long_soon, last_other, long_late = swap(long_soon), swap(last_parcel), swap(long_late)
    *mem_came, gqkvt0 = lax.optimization_barrier((*mem_came, gqkvt0))
    mem = [settle(mem[k], k, mem_came[k])[0] for k in both]
    mem_came = [line.trade(mem[k], 1 - k) for k in both]
    short_mine, *short_soon, short_late = inner_call(
        mixt0, mixt1, ga0, ga1, n0, n1, after(gqkvt0, line.last), gqkvt1
    )
    short_soon, short_late = [swap(block) for block in short_soon], swap(short_late)
    *mem_came, short_mine = lax.optimization_barrier((*mem_came, short_mine))
    rest = list(range(2, bits))
    extras = Lazy(EXTRAS, [(last_parcel, 0), (last_other, 0)])
    enc = [
        [
            Lazy(LONG, [(long_mine, k * LONG), (long_soon, k * LONG)]),
            Lazy(SHORT, [(short_mine, k * SHORT), (short_soon[k], 0)]),
        ]
        for k in both
    ]
    gives = fold([[part.entry() for part in enc[0] + [extras]], [part.entry() for part in enc[1]]])
    enc_came = [line.send(gives[k], k) for k in both]
    extras = Lazy(EXTRAS, extras.pieces + [(enc_came[0], lambda device: PIECE)])
    mem = [settle(mem[k], 1 - k, mem_came[k])[0] for k in both]
    mem = mem[0] + mem[1]
    for bit in rest:
        mem = settle(mem, bit, line.trade(mem, bit))[0]
    mem = jnp.concatenate([part.value() for part in mem], axis=0)[None]
    enc = [
        [
            Lazy(LONG, [(long_mine, (2 + k) * LONG), (long_late, k * LONG), (enc_came[k], 0)]),
            Lazy(SHORT, [(short_mine, (2 + k) * SHORT), (short_late, k * SHORT), (enc_came[k], LONG)]),
        ]
        for k in both
    ]
    gives = fold([
        [part.half(1, False).entry() for part in enc[0]] + [extras.entry()],
        [part.half(0, False).entry() for part in enc[1]],
    ])
    enc_came = [line.send(gives[k], 1 - k) for k in both]
    extras = Lazy(EXTRAS, extras.pieces + [(enc_came[0], PIECE // 2)])
    for bit in rest[:0:-1]:
        mem = join(mem, line.send(mem, bit), bit)
    enc = settle_lazy(enc[0], 1, enc_came[0]) + settle_lazy(enc[1], 0, enc_came[1])
    for bit in rest:
        rows = sum(part.size for part in enc) // 2
        (give,) = fold([[part.half(bit, False).entry() for part in enc] + [extras.entry()]])
        came = line.send(give, bit)
        enc = settle_lazy(enc, bit, came)
        extras = Lazy(EXTRAS, extras.pieces + [(came, rows)])
        if bit == rest[0]:
            mem = join(mem, line.send(mem, bit), bit)

    def split(block):
        rows = block.shape[1] // 2
        return block[:, :rows], block[:, rows:]

    mem_parts = split(mem)
    enc, extras = fold([[part.entry() for part in enc], [extras.entry()]])
    enc = enc[None]
    mem_came = [line.send(mem_parts[k], 1 - k) for k in both]
    for bit in rest[::-1]:
        if bit == rest[0]:
            mem_near = [join(mem_parts[k], mem_came[k], 1 - k) for k in both]
            mem_far = [line.send(mem_near[k], k) for k in both]
        enc = join(enc, line.send(enc, bit), bit)
    *mem_far, enc = lax.optimization_barrier((*mem_far, enc))
    enc_parts = split(enc)
    enc_came = [line.send(enc_parts[k], 1 - k) for k in both]
    *enc_came, activations, final_memory, grad_tokens = lax.optimization_barrier(
        (*enc_came, *assemble_call(parcel, parcel_other, out_keep, last_other))
    )
    enc_near = [join(enc_parts[k], enc_came[k], 1 - k) for k in both]
    enc_far = [line.send(enc_near[k], k) for k in both]

    def with_other(blocks, whole_rows=False):
        blocks = [block.reshape(PACK[0][1:]) if whole_rows else as_piece(block) for block in blocks]
        return blocks + [swap(block) for block in blocks]

    begun = unpack_call(0, with_other(enc_near) + with_other(mem_near, True), ())
    tied = lax.optimization_barrier((*enc_far, *begun))
    enc_far, begun = tied[:2], tied[2:]
    grad_out, grad_in, grad_proj, grad_qkv = unpack_call(1, with_other(enc_far) + with_other(mem_far, True), begun)
    extras = extras.astype(F32)
    gain_grads = jnp.where(front, extras[SLOTS : SLOTS + 2], extras[SLOTS + 2 : SLOTS + 4])
    return (
        activations,
        final_memory,
        grad_tokens,
        extras[:SLOTS],
        gain_grads[0:1],
        grad_qkv[None],
        grad_proj[None],
        gain_grads[1:2],
        grad_in[None],
        grad_out[None],
    )


def solution(mesh):
    placed = (
        P("dp", None),
        P("dp"),
        P(),
        P("pipe", None),
        P("pipe", None, None),
        P("pipe", None, None),
        P("pipe", None),
        P("pipe", None, None),
        P("pipe", None, None),
        P("dp", None),
        P("dp", None, None),
    )
    return jax.shard_map(
        local,
        mesh=mesh,
        in_specs=placed,
        out_specs=(
            P("dp", None),
            P("dp", None, None),
            P("dp", "pipe"),
            P(),
            P("pipe", None),
            P("pipe", None, None),
            P("pipe", None, None),
            P("pipe", None),
            P("pipe", None, None),
            P("pipe", None, None),
        ),
        check_vma=False,
    )
```

```python
import jax
import jax.numpy as jnp
from jax import lax
from jax.experimental import pallas as pl
from jax.experimental.pallas import tpu as pltpu
from jax.sharding import PartitionSpec as P

D = 512
HEADS = 8
HEAD_DIM = 64
FF = 2048
SLOTS = 64
SEG_LEN = 512
SEGS = 2
ROWS = SEG_LEN + SLOTS
TILE = 512
BLOCKS = 12
HALF = TILE // 2
PIECE = 3 * HALF

epsilon = 1e-05
masked_bias = -1000000000.0
score_scale = HEAD_DIM ** (-0.5)
exponent_scale = score_scale * 1.4426950408889634
gelu_a = 0.7978845608028654
gelu_b = 0.044715 * gelu_a

BF16 = jnp.bfloat16
F32 = jnp.float32


def dot(left, right):
    return jnp.dot(left, right, preferred_element_type=F32)


def dot_t(left, right):
    return lax.dot_general(left, right, (((1,), (1,)), ((), ())), preferred_element_type=F32)


def normalise(values):
    centred = values - jnp.mean(values, axis=-1, keepdims=True)
    spread = jnp.mean(centred * centred, axis=-1, keepdims=True)
    inverse = lax.rsqrt(spread + epsilon)
    return centred * inverse, inverse


def layer_norm(values, gain):
    return normalise(values)[0] * gain


def layer_norm_back(values, gain, grads):
    scaled, inverse = normalise(values)
    gain_grad = jnp.sum(grads * scaled, axis=0, keepdims=True)
    inner = grads * gain
    mean_inner = jnp.mean(inner, axis=-1, keepdims=True)
    mean_scaled = jnp.mean(inner * scaled, axis=-1, keepdims=True)
    return inverse * (inner - mean_inner - scaled * mean_scaled), gain_grad


def gelu_both(values):
    square = values * values
    tangent = jnp.tanh(values * (gelu_a + gelu_b * square))
    half = 0.5 + 0.5 * tangent
    slope = half + (0.5 * values) * (1.0 - tangent * tangent) * (gelu_a + 3.0 * gelu_b * square)
    return values * half, slope


def iota(shape, dim):
    return lax.broadcasted_iota(jnp.int32, shape, dim)


def repeat_matrix():
    return (iota((SLOTS, D), 0) == iota((SLOTS, D), 1) % SLOTS).astype(BF16)


def head_blocks():
    return iota((D, D), 0) // HEAD_DIM == iota((D, D), 1) // SLOTS


class Mover:
    def __init__(self, sems):
        self.sems = sems
        self.used = 0
        self.coming = {}
        self.leaving = []

    def slot(self):
        self.used += 1
        return self.sems.at[self.used - 1]

    def bring(self, target, source):
        sem = self.slot()
        pltpu.make_async_copy(source, target, sem).start()
        self.coming[id(target)] = (source, target, sem)

    def bring_either(self, target, pick_first, first, second):
        sem = self.slot()

        @pl.when(pick_first)
        def _():
            pltpu.make_async_copy(first, target, sem).start()

        @pl.when(jnp.logical_not(pick_first))
        def _():
            pltpu.make_async_copy(second, target, sem).start()

        self.coming[id(target)] = (first, target, sem)

    def need(self, *targets):
        for target in targets:
            if id(target) in self.coming:
                pltpu.make_async_copy(*self.coming.pop(id(target))).wait()

    def send(self, source, target):
        copy = pltpu.make_async_copy(source, target, self.slot())
        copy.start()
        self.leaving.append(copy)
        return copy

    def left(self, *copies):
        for copy in copies:
            copy.wait()
            self.leaving = [other for other in self.leaving if other is not copy]

    def finish(self):
        for copy in self.leaving:
            copy.wait()


def valid_keys(shape, valid_rows):
    row = iota(shape, 0)
    return (row < valid_rows) | (row >= SEG_LEN)


def encoder_attention(
    need, x, m, bias, gain, wqkv, wproj, n, qt, kv, vt, probs, inv, mixt, hidden, ready=lambda *refs: None,
    behind=None,
):
    need(x, m)
    n[:SEG_LEN] = layer_norm(x[...].astype(F32), gain).astype(BF16)
    n[SEG_LEN:] = layer_norm(m[...].astype(F32), gain).astype(BF16)
    need(wqkv)
    qt[...] = dot_t(wqkv[:, :D].T, n[:SEG_LEN]).astype(BF16)
    kv[:, :D] = dot(n[...], wqkv[:, D : 2 * D]).astype(BF16)
    values = dot(n[...], wqkv[:, 2 * D :]).astype(BF16)
    kv[:, D:] = values
    vt[...] = values.T
    ready(n, qt, kv)
    low_lanes = iota((ROWS, 128), 1) < HEAD_DIM
    ones_row = (iota((HEAD_DIM, SEG_LEN), 0) == 0).astype(BF16)

    def pair(index, carry):
        base = pl.multiple_of(index * 128, 128)
        keys = kv[:, pl.ds(base, 128)]
        spans = [pl.ds(pl.multiple_of(base + half * HEAD_DIM, HEAD_DIM), HEAD_DIM) for half in range(2)]
        left = jnp.where(low_lanes, keys, bias[...]), jnp.where(low_lanes, bias[...], keys)
        right = (
            jnp.concatenate([qt[spans[0]], ones_row], axis=0), jnp.concatenate([ones_row, qt[spans[1]]], axis=0)
        )
        both = [dot(left[half], right[half]) for half in range(2)]
        for half, scores in enumerate(both):
            head, rows = 2 * index + half, spans[half]
            top = jnp.max(scores, axis=0, keepdims=True)
            grown = jnp.exp2(scores * exponent_scale - top * exponent_scale)
            inverse = 1.0 / jnp.sum(grown, axis=0, keepdims=True)
            low = grown.astype(BF16)
            probs[head] = low
            inv[head] = inverse
            mixt[rows] = (dot(vt[rows], low) * inverse).astype(BF16)
        return carry

    if behind is None:
        lax.fori_loop(0, HEADS // 2, pair, 0)
    else:
        for index in range(HEADS // 2):
            pair(index, 0)
            behind(index)
    ready(inv, mixt)
    need(wproj)
    hidden[...] = x[...].astype(F32) + dot(mixt[...].T, wproj[...])
    ready(hidden)


def encoder_ffn(need, hidden, gain, win, wout, y, nf, act, slope, total, before=None):
    need(hidden)
    nf[...] = layer_norm(hidden[...], gain).astype(BF16)
    total[...] = hidden[...]
    need(win, wout)

    def step(index, carry):
        span = pl.ds(pl.multiple_of(index * TILE, TILE), TILE)
        active, grad = gelu_both(dot(nf[...], win[:, span]))
        low = active.astype(BF16)
        act[:, span] = low
        slope[:, span] = grad.astype(BF16)
        total[...] += dot(low, wout[span])
        return carry

    if before is None:
        lax.fori_loop(0, FF // TILE, step, 0)
    else:
        for index in range(FF // TILE):
            before(index)
            step(index, 0)
    y[...] = total[...].astype(BF16)


def memory_forward(need, y, m, valid_rows, gain, ffn_gain, weights, result, kept, index, vt):
    wqkv, wproj, win, wout = weights
    n, kv, keyed, probs, inv, mixm, mixed, attended, hidden, nf, act, slope, branch = [ref.at[index] for ref in kept]
    need(m)
    mf = m[...].astype(F32)
    n[:SEG_LEN] = layer_norm(y[...].astype(F32), gain).astype(BF16)
    slots = layer_norm(mf, gain).astype(BF16)
    n[SEG_LEN:] = slots
    need(wqkv)
    kv[:, :D] = dot(n[...], wqkv[:, D : 2 * D]).astype(BF16)
    values = dot(n[...], wqkv[:, 2 * D :]).astype(BF16)
    kv[:, D:] = values
    vt[...] = values.T
    blocks = head_blocks()
    queries = dot_t(wqkv[:, :D].T, jnp.concatenate([slots] * HEADS, axis=0))
    keyed[...] = jnp.where(blocks, queries, 0.0).astype(BF16)
    scores = dot(kv[:, :D], keyed[...])
    if valid_rows is not None:
        scores = jnp.where(valid_keys((ROWS, D), valid_rows), scores, masked_bias)
    top = jnp.max(scores, axis=0, keepdims=True)
    grown = jnp.exp2(scores * exponent_scale - top * exponent_scale)
    inverse = 1.0 / jnp.sum(grown, axis=0, keepdims=True)
    probs[...] = grown.astype(BF16)
    inv[...] = inverse
    mixm[...] = jnp.where(blocks, dot(vt[...], probs[...]) * inverse, 0.0).astype(BF16)
    mixed[...] = dot_t(repeat_matrix(), mixm[...]).astype(BF16)
    need(wproj)
    attended[...] = dot(mixed[...], wproj[...])
    hidden[...] = mf + attended[...]
    nf[...] = layer_norm(hidden[...], ffn_gain).astype(BF16)
    need(win)
    active, grad = gelu_both(dot(nf[...], win[...]))
    act[...] = active.astype(BF16)
    slope[...] = grad.astype(BF16)
    need(wout)
    branch[...] = dot(act[...], wout[...])
    result[...] = (mf + jax.nn.sigmoid(branch[...]) * attended[...]).astype(BF16)


def memory_backward(go, y, m, gain, ffn_gain, weights, kept, index, grad_y, grad_m, grads):
    wqkv, wproj, win, wout = weights
    n, kv, keyed, probs, inv, mixm, mixed, attended, hidden, nf, act, slope, branch = [ref.at[index] for ref in kept]
    gb, gpre, ga, gq, gkv = [ref.at[index] for ref in grads]
    blocks = head_blocks()
    gate = jax.nn.sigmoid(branch[...])
    gof = go[...].astype(F32)
    gb[...] = (gof * attended[...] * gate * (1.0 - gate)).astype(BF16)
    gpre[...] = (slope[...].astype(F32) * dot_t(gb[...], wout[...])).astype(BF16)
    ghidden, ffn_gain_grad = layer_norm_back(hidden[...], ffn_gain, dot_t(gpre[...], win[...]))
    gattended = (ghidden + gof * gate).astype(BF16)
    ga[...] = gattended
    gmixed = dot_t(wproj[...], jnp.concatenate([gattended] * HEADS, axis=0)).astype(BF16).astype(F32)
    gmixed = jnp.where(blocks, gmixed * inv[...], 0.0)
    low_mixed = gmixed.astype(BF16)
    centre = jnp.sum(mixm[...].astype(F32) * gmixed, axis=0, keepdims=True)
    gprobs = dot(kv[:, D:], low_mixed)
    gscores = (probs[...].astype(F32) * (gprobs - centre)).astype(BF16)
    gqueries = dot(kv[:, :D].T, gscores) * score_scale
    gqueries = jnp.where(blocks, gqueries, 0.0).astype(BF16)
    gq[...] = dot_t(repeat_matrix(), gqueries).astype(BF16)
    gkv[:, :D] = (dot_t(gscores, keyed[...]) * score_scale).astype(BF16)
    gkv[:, D:] = dot_t(probs[...], low_mixed).astype(BF16)
    grows = dot_t(gkv[...], wqkv[:, D:])
    gslots = grows[SEG_LEN:] + dot_t(gq[...], wqkv[:, :D])
    grad_rows, gain_rows = layer_norm_back(y[...].astype(F32), gain, grows[:SEG_LEN])
    grad_slots, gain_slots = layer_norm_back(m[...].astype(F32), gain, gslots)
    grad_y[...] = grad_rows.astype(BF16)
    grad_m[...] = grad_slots + ghidden + gof
    return gain_rows + gain_slots, ffn_gain_grad


def encoder_ffn_backward(
    need, cot, grad_y, hidden, gain, win, wout, slope, gb, gnf, ga, ghidden, before=None, behind=None
):
    need(cot, grad_y)
    go = cot[...].astype(F32) + grad_y[...].astype(F32)
    gb[...] = go.astype(BF16)
    ghidden[...] = go
    gnf[...] = jnp.zeros_like(gnf)
    need(wout, slope, win)

    def step(index, carry):
        span = pl.ds(pl.multiple_of(index * TILE, TILE), TILE)
        low = (slope[:, span].astype(F32) * dot_t(gb[...], wout[span])).astype(BF16)
        slope[:, span] = low
        gnf[...] += dot_t(low, win[:, span])
        return carry

    if before is None:
        lax.fori_loop(0, FF // TILE, step, 0)
    else:
        for index in range(FF // TILE):
            before(index)
            step(index, 0)
            behind(index)
    need(hidden)
    grad, gain_grad = layer_norm_back(hidden[...], gain, gnf[...])
    grad = grad + ghidden[...]
    ghidden[...] = grad
    ga[...] = grad.astype(BF16)
    return gain_grad


def encoder_attention_backward(
    need, x, m, gain, wqkv, wproj, qt, kv, probs, inv, mixt, ga, ghidden, kt, gmt, gqkvt, grad_x, grad_m
):
    need(wproj, ga)
    gmt[...] = dot_t(wproj[...], ga[...]).astype(BF16)
    need(kv)
    kt[...] = kv[:, :D].T
    gqkvt[:D, SEG_LEN:] = jnp.zeros((D, SLOTS), BF16)
    empty = jnp.zeros((HEAD_DIM, SEG_LEN), BF16)
    need(inv, mixt, qt, probs)

    def pair(index, carry):
        base = pl.multiple_of(index * 128, 128)
        values = kv[:, pl.ds(pl.multiple_of(D + base, 128), 128)]
        work = []
        for half in range(2):
            head = 2 * index + half
            start = pl.multiple_of(base + half * HEAD_DIM, HEAD_DIM)
            rows = pl.ds(start, HEAD_DIM)
            scaled = gmt[rows].astype(F32) * inv[head]
            centre = jnp.sum(mixt[rows].astype(F32) * scaled, axis=0, keepdims=True)
            low = scaled.astype(BF16)
            right = jnp.concatenate([low, empty] if half == 0 else [empty, low], axis=0)
            work.append((head, start, rows, centre, low, dot(values, right)))
        for head, start, rows, centre, low, gprobs in work:
            gscores = (probs[head].astype(F32) * (gprobs - centre)).astype(BF16)
            gqkvt[pl.ds(pl.multiple_of(2 * D + start, HEAD_DIM), HEAD_DIM)] = dot_t(low, probs[head]).astype(BF16)
            gqkvt[rows, :SEG_LEN] = (dot(kt[rows], gscores) * score_scale).astype(BF16)
            gqkvt[pl.ds(pl.multiple_of(D + start, HEAD_DIM), HEAD_DIM)] = (
                dot_t(qt[rows], gscores) * score_scale
            ).astype(BF16)
        return carry

    lax.fori_loop(0, HEADS // 2, pair, 0)
    need(wqkv, x, m, ghidden)
    grows = dot(wqkv[...], gqkvt[...]).T
    grad_rows, gain_rows = layer_norm_back(x[...].astype(F32), gain, grows[:SEG_LEN])
    grad_slots, gain_slots = layer_norm_back(m[...].astype(F32), gain, grows[SEG_LEN:])
    grad_x[...] = (grad_rows + ghidden[...]).astype(BF16)
    grad_m[...] = grad_slots
    return gain_rows + gain_slots


def spot_of(block):
    if block < 8:
        return block // 2, pl.ds(block % 2, 1), slice(0, LONG_ROWS)
    return block - 8, pl.ds(0, 2), slice(LONG_ROWS, CHUNK)


def halves(core):
    return [pl.ds(pl.multiple_of(side * HALF, HALF), HALF) for side in (core, 1 - core)]


def memory_weights(mover, core, kept, grads, packs, stage, short_stage, act_t, nf_t, mixed_t, slots_t, n0_t, n1_t):
    n, kv, keyed, probs, inv, mixm, mixed, attended, hidden, nf, act, slope, branch = kept
    gb, gpre, ga, gq, gkv = grads

    def both(ref, *index):
        return jnp.concatenate([ref[(k,) + index] for k in range(SEGS)], axis=0)

    whole = slice(None)
    for block in range(4):
        span = slice(block * TILE, (block + 1) * TILE)
        act_t[span] = both(act, whole, span).T
    nf_t[...] = both(nf).T
    mixed_t[...] = both(mixed).T
    slots_t[...] = both(n, slice(SEG_LEN, ROWS)).T
    n0_t[...] = n[0].T
    n1_t[...] = n[1].T
    flying = [None] * BLOCKS
    for pack, rows in zip(packs, halves(core)):

        def put(block, value, pack=pack):
            if flying[block] is not None:
                mover.left(flying[block])
            piece, half, rows = spot_of(block)
            held = stage.at[block] if block < 8 else short_stage.at[block - 8]
            held[...] = value.astype(BF16).reshape(held.shape)
            flying[block] = mover.send(held, pack.at[piece, half, :, rows])

        for block in range(4):
            span = slice(block * TILE, (block + 1) * TILE)
            put(block, dot(act_t.at[span][rows], both(gb)))
            put(4 + block, dot(nf_t[rows], both(gpre, whole, span)))
        put(8, dot(mixed_t[rows], both(ga)))
        put(9, dot(slots_t[rows], both(gq)))
        for block in range(2):
            span = slice(block * TILE, (block + 1) * TILE)
            put(10 + block, dot(n0_t[rows], gkv[0, :, span]) + dot(n1_t[rows], gkv[1, :, span]))


def encoder_ffn_weights(need, core, acts, gbs, nfs, gpres, packs, left, left_nf):
    need(*gbs, *acts)

    def outer(block, carry):
        span = pl.ds(pl.multiple_of(block * TILE, TILE), TILE)
        for k in range(SEGS):
            left[k] = acts[k][:, span].T
        start = pl.multiple_of(block * HALF, HALF)
        for pack, rows in zip(packs, halves(core)):
            pack[pl.ds(start, HALF)] = (
                dot(left[0, rows], gbs[0][...]) + dot(left[1, rows], gbs[1][...])
            ).astype(BF16)
        return carry

    lax.fori_loop(0, 4, outer, 0)
    need(*nfs, *gpres)
    for k in range(SEGS):
        left_nf[k] = nfs[k][...].T

    def inner(block, carry):
        span = pl.ds(pl.multiple_of(block * TILE, TILE), TILE)
        start = pl.multiple_of((4 + block) * HALF, HALF)
        for pack, rows in zip(packs, halves(core)):
            pack[pl.ds(start, HALF)] = (
                dot(left_nf[0, rows], gpres[0][:, span]) + dot(left_nf[1, rows], gpres[1][:, span])
            ).astype(BF16)
        return carry

    lax.fori_loop(0, 4, inner, 0)


def encoder_attention_weights(need, core, mixts, gas, ns, gqkvts, packs, left, before=None):
    need(*mixts, *gas)
    for pack, rows in zip(packs, halves(core)):
        pack[:HALF] = (dot(mixts[0][rows], gas[0][...]) + dot(mixts[1][rows], gas[1][...])).astype(BF16)
    need(*ns, *gqkvts)
    for k in range(SEGS):
        left[k] = ns[k][...].T

    def third(block, carry):
        span = pl.ds(pl.multiple_of(block * TILE, TILE), TILE)
        start = pl.multiple_of((1 + block) * HALF, HALF)
        for pack, rows in zip(packs, halves(core)):
            pack[pl.ds(start, HALF)] = (
                dot_t(left[0, rows], gqkvts[0][span]) + dot_t(left[1, rows], gqkvts[1][span])
            ).astype(BF16)
        return carry

    if before is not None:
        for block in range(3):
            before(block)
    lax.fori_loop(0, 3, third, 0)


SCALAR = pl.BlockSpec(memory_space=pltpu.SMEM)
HELD = pl.BlockSpec(memory_space=pltpu.VMEM)
FAR = pl.BlockSpec(memory_space=pl.ANY)

WEIGHTS = (((D, 3 * D), BF16), ((D, D), BF16), ((D, FF), BF16), ((FF, D), BF16))
ROW_LOW = ((SEG_LEN, D), BF16)
ROW_FULL = ((SEG_LEN, D), F32)
WIDE = ((SEG_LEN, FF), BF16)
ALL_LOW = ((ROWS, D), BF16)
ALL_TURNED = ((D, ROWS), BF16)
TURNED = ((D, SEG_LEN), BF16)
SLOT_LOW = ((SLOTS, D), BF16)
SLOT_FULL = ((SLOTS, D), F32)
SLOT_WIDE = ((SLOTS, FF), BF16)
SLOT_TURNED = ((D, SEGS * SLOTS), BF16)
SQUARE = ((D, D), BF16)
PROBS = ((HEADS, ROWS, SEG_LEN), BF16)
INVERSE = ((HEADS, 1, SEG_LEN), F32)
KEYS_VALUES = ((ROWS, 2 * D), BF16)
GRAD_TURNED = ((3 * D, ROWS), BF16)
GAINS = ((8, D), F32)
BIAS = ((ROWS, 128), BF16)
EXTRAS = SLOTS + 16
PARCEL = SEGS * SEG_LEN + SLOTS
CHUNKS = 4
LONG_ROWS = HALF // CHUNKS
SHORT_ROWS = LONG_ROWS // 2
CHUNK = LONG_ROWS + SHORT_ROWS
PACK = ((4, 2, CHUNKS, CHUNK, D), BF16)


def pack_of(blocks):
    return ((blocks * HALF, D), BF16)


def twice(item):
    return ((SEGS,) + item[0], item[1])


def call(body, kinds, outs, scratch, copies, name, aliases={}):
    out_kinds, outs = zip(*outs)
    specs = {"s": SCALAR, "v": HELD, "f": FAR}
    inputs = len(kinds)

    def kernel(*refs):
        ins, results = refs[:inputs], refs[inputs : inputs + len(outs)]
        held, sems = refs[inputs + len(outs) : -1], refs[-1]
        body(Mover(sems), ins, results, held)

    light = name in ("unpack", "assemble")
    cost = pl.CostEstimate(
        flops=1_000_000 if light else 20_000_000_000, bytes_accessed=1_000_000 if light else 10_000_000, transcendentals=0
    )
    return pl.pallas_call(
        kernel,
        out_shape=[jax.ShapeDtypeStruct(shape, kind) for shape, kind in outs],
        in_specs=[specs[kind] for kind in kinds],
        out_specs=[specs[kind] for kind in out_kinds],
        scratch_shapes=[pltpu.VMEM(shape, kind) for shape, kind in scratch] + [pltpu.SemaphoreType.DMA((copies,))],
        compiler_params=pltpu.CompilerParams(vmem_limit_bytes=63 * 2**20),
        cost_estimate=cost,
        input_output_aliases=aliases,
        name=name,
    )


def own_gains(own, other, front):
    return jnp.where(front, own[...], other[...])


def document_rows(core, segment):
    return pl.ds(pl.multiple_of((core * SEGS + segment) * SEG_LEN, SEG_LEN), SEG_LEN)


def column_halves(core):
    return [pl.ds(pl.multiple_of(side * (D // 2), D // 2), D // 2) for side in (core, 1 - core)]


def first_kernel(mover, ins, outs, held):
    tokens, m, gains_own, gains_other, qkv_own, qkv_other, proj_own, proj_other = ins
    x, n, qt, kv, probs, inv, mixt, hidden, vt, wqkv, wproj, bias = held
    core = lax.axis_index("pipe")
    gains = own_gains(gains_own, gains_other, core == 0)
    bias[...] = jnp.zeros_like(bias)
    mover.bring(x, tokens.at[document_rows(core, 0)])
    mover.bring_either(wqkv, core == 0, qkv_own, qkv_other)
    mover.bring_either(wproj, core == 0, proj_own, proj_other)
    targets = dict(zip((id(ref) for ref in (hidden, n, qt, kv, probs, inv, mixt)), outs))

    def ready(*sources):
        for source in sources:
            mover.send(source, targets[id(source)])

    encoder_attention(
        mover.need, x, m, bias, gains[0:1], wqkv, wproj, n, qt, kv, vt, probs, inv, mixt, hidden, ready,
        lambda index: mover.send(probs.at[pl.ds(2 * index, 2)], targets[id(probs)].at[pl.ds(2 * index, 2)]),
    )
    mover.finish()


FIRST = (ROW_FULL, ALL_LOW, TURNED, KEYS_VALUES, PROBS, INVERSE, TURNED)


def first_call(tokens, m, gains, weights):
    return call(
        first_kernel,
        "fvvvffff",
        [("f", item) for item in FIRST],
        [ROW_LOW, ALL_LOW, TURNED, KEYS_VALUES, PROBS, INVERSE, TURNED, ROW_FULL, ALL_TURNED, WEIGHTS[0], WEIGHTS[1], BIAS],
        13,
        "encoder_attention",
    )(tokens, m, *gains, *weights[0], *weights[1])


MEMORY_KEPT = (
    ALL_LOW, KEYS_VALUES, SQUARE, ALL_LOW, ((1, D), F32), SQUARE, SLOT_LOW, SLOT_FULL, SLOT_FULL,
    SLOT_LOW, SLOT_WIDE, SLOT_WIDE, SLOT_FULL,
)
MEMORY_GRADS = (SLOT_LOW, SLOT_WIDE, SLOT_LOW, SLOT_LOW, KEYS_VALUES)


def middle_kernel(mover, ins, outs, held):
    lengths, m0, gains_own, gains_other, cot_memory, hidden0, tokens, cots = ins[:8]
    pairs = ins[8:]
    (parcel, mine, theirs, out_nf, out_act, out_slope, out_n, out_mixt, out_gb, out_ga, out_gqkvt, out_grad_y, out_grad_x,
     out_grad_m, out_gains) = outs
    out_y = [parcel.at[pl.ds(k * SEG_LEN, SEG_LEN)] for k in range(SEGS)]
    out_final = parcel.at[pl.ds(SEGS * SEG_LEN, SLOTS)]
    enc_weights, mem_weights, held = held[:4], held[4:8], held[8:]
    kept, held = held[: len(MEMORY_KEPT)], held[len(MEMORY_KEPT) :]
    grads, held = held[: len(MEMORY_GRADS)], held[len(MEMORY_GRADS) :]
    (x, cot, cot_slots, hidden, n, qt, kv, probs, inv, mixt, nf, act, slope, y0, y1, turned, total, gnf, gmt, gb, ga,
     gqkvt, grad_y, grad_x, m1, final, grad_m, grad_m1, stage, short_stage, act_t, nf_t, mixed_t, slots_t, bias) = held
    core = lax.axis_index("pipe")
    front = core == 0
    enc_gains = own_gains(gains_own, gains_other, front)
    mem_gains = own_gains(gains_other, gains_own, front)
    valid_rows = lengths[core] - SEG_LEN
    lanes = iota(BIAS[0], 1) % HEAD_DIM == 0
    bias[...] = jnp.where(lanes & ~valid_keys(BIAS[0], valid_rows), masked_bias, 0.0).astype(BF16)
    need = mover.need
    wqkv, wproj, win, wout = enc_weights
    mover.bring(hidden, hidden0)
    tiles = []
    for index in range(FF // TILE):
        span = pl.ds(index * TILE, TILE)
        tile = win.at[:, span], wout.at[span]
        mover.bring_either(tile[0], front, pairs[4].at[:, span], pairs[5].at[:, span])
        mover.bring_either(tile[1], front, pairs[6].at[span], pairs[7].at[span])
        tiles.append(tile)

    def first_tile(tile):
        need(*tiles[tile])
        if tile:
            return
        for index in range(4):
            own, other = pairs[2 * index : 2 * index + 2]
            mover.bring_either(mem_weights[index], front, other, own)
        mover.bring(x, tokens.at[document_rows(core, 1)])
        for index in (0, 1):
            mover.bring_either(enc_weights[index], front, *pairs[2 * index : 2 * index + 2])
        mover.bring(cot_slots, cot_memory.at[core])
        mover.bring(cot, cots.at[document_rows(core, 1)])

    enc_attn, enc_ffn = enc_gains[0:1], enc_gains[1:2]
    mem_attn, mem_ffn = mem_gains[0:1], mem_gains[1:2]

    encoder_ffn(need, hidden, enc_ffn, win, wout, y0, nf, act, slope, total, first_tile)
    mover.send(y0, out_y[0])
    early = [mover.send(nf, out_nf.at[0]), mover.send(act, out_act.at[0]), mover.send(slope, out_slope.at[0])]
    memory_forward(need, y0, m0, None, mem_attn, mem_ffn, mem_weights, m1, kept, 0, turned)
    encoder_attention(need, x, m1, bias, enc_attn, wqkv, wproj, n, qt, kv, turned, probs, inv, mixt, hidden)
    mover.send(n, out_n)
    mover.send(mixt, out_mixt)
    mover.left(*early)
    encoder_ffn(need, hidden, enc_ffn, win, wout, y1, nf, act, slope, total)
    mover.send(y1, out_y[1])
    mover.send(nf, out_nf.at[1])
    mover.send(act, out_act.at[1])
    memory_forward(need, y1, m1, valid_rows, mem_attn, mem_ffn, mem_weights, final, kept, 1, turned)
    mover.send(final, out_final)

    need(cot_slots)
    attn_gain1, ffn_gain1 = memory_backward(
        cot_slots, y1, m1, mem_attn, mem_ffn, mem_weights, kept, 1, grad_y, grad_m, grads
    )
    out_gains[1:2] = encoder_ffn_backward(need, cot, grad_y, hidden, enc_ffn, win, wout, slope, gb, gnf, ga, total)
    mover.send(gb, out_gb)
    mover.send(ga, out_ga)
    mover.send(slope, out_slope.at[1])
    out_gains[0:1] = encoder_attention_backward(
        need, x, m1, enc_attn, wqkv, wproj, qt, kv, probs, inv, mixt, ga, total, turned, gmt, gqkvt, grad_x, grad_m1
    )
    turned_out = mover.send(gqkvt, out_gqkvt)
    mover.send(grad_x, out_grad_x)
    grad_m[...] = grad_m[...] + grad_m1[...].astype(BF16).astype(F32)
    attn_gain0, ffn_gain0 = memory_backward(
        grad_m, y0, m0, mem_attn, mem_ffn, mem_weights, kept, 0, grad_y, out_grad_m, grads
    )
    mover.send(grad_y, out_grad_y)
    out_gains[2:3] = attn_gain0 + attn_gain1
    out_gains[3:4] = ffn_gain0 + ffn_gain1
    out_gains[4:8] = jnp.zeros((4, D), F32)
    mover.left(turned_out)
    memory_weights(
        mover, core, kept, grads, (mine, theirs), stage, short_stage, act_t, nf_t, mixed_t, slots_t,
        gqkvt.at[pl.ds(0, D)], gqkvt.at[pl.ds(D, D)],
    )
    mover.finish()


def middle_call(lengths, m0, gains, cot_memory, hidden, tokens, cots, weights):
    outs = [
        ("f", ((PARCEL, D), BF16)), ("f", PACK), ("f", PACK), ("f", twice(ROW_LOW)), ("f", twice(WIDE)),
        ("f", twice(WIDE)), ("f", ALL_LOW), ("f", TURNED), ("f", ROW_LOW), ("f", ROW_LOW), ("f", GRAD_TURNED),
        ("f", ROW_LOW), ("f", ROW_LOW), ("v", SLOT_FULL), ("v", GAINS),
    ]
    scratch = [
        *WEIGHTS, *WEIGHTS, *[twice(item) for item in MEMORY_KEPT], *[twice(item) for item in MEMORY_GRADS],
        ROW_LOW, ROW_LOW, SLOT_LOW, ROW_FULL, ALL_LOW, TURNED, KEYS_VALUES, PROBS, INVERSE, TURNED, ROW_LOW, WIDE,
        WIDE, ROW_LOW, ROW_LOW, ALL_TURNED, ROW_FULL, ROW_FULL, TURNED, ROW_LOW, ROW_LOW, GRAD_TURNED, ROW_LOW,
        ROW_LOW, SLOT_LOW, SLOT_LOW, SLOT_FULL, SLOT_FULL, ((8, 1, CHUNKS, LONG_ROWS, D), BF16), ((4, 2, CHUNKS, SHORT_ROWS, D), BF16),
        ((FF, SEGS * SLOTS), BF16),
        SLOT_TURNED, SLOT_TURNED, SLOT_TURNED, BIAS,
    ]
    return call(middle_kernel, "svvvffff" + "f" * 8, outs, scratch, 72, "middle")(
        lengths, m0, *gains, cot_memory, hidden, tokens, cots,
        *[item for pair in weights for item in pair],
    )


def feed_kernel(mover, ins, outs, held):
    gains_own, gains_other, grad_gains, cots, grad_y0, hidden0, slopes, in_own, in_other, out_own, out_other = ins
    out_gpre, out_gb, out_ga, out_ghidden, out_gains = outs
    win, wout, cot, grad_y, hidden, gpre, gb, gnf, ga, ghidden = held
    core = lax.axis_index("pipe")
    gains = own_gains(gains_own, gains_other, core == 0)
    mover.bring(cot, cots.at[document_rows(core, 0)])
    mover.bring(grad_y, grad_y0)
    spans = [pl.ds(index * TILE, TILE) for index in range(FF // TILE)]
    tiles = []
    for span in spans:
        tile = wout.at[span], gpre.at[:, span], win.at[:, span]
        mover.bring_either(tile[0], core == 0, out_own.at[span], out_other.at[span])
        mover.bring(tile[1], slopes.at[0, :, span])
        mover.bring_either(tile[2], core == 0, in_own.at[:, span], in_other.at[:, span])
        tiles.append(tile)
    mover.bring(hidden, hidden0)
    gain_grad = encoder_ffn_backward(
        mover.need, cot, grad_y, hidden, gains[1:2], win, wout, gpre, gb, gnf, ga, ghidden,
        lambda index: mover.need(*tiles[index]),
        lambda index: mover.send(gpre.at[:, spans[index]], out_gpre.at[:, spans[index]]),
    )
    for source, target in ((gb, out_gb), (ga, out_ga), (ghidden, out_ghidden)):
        mover.send(source, target)
    out_gains[...] = grad_gains[...]
    out_gains[1:2] = grad_gains[1:2] + gain_grad
    mover.finish()


def feed_call(gains, grad_gains, cots, grad_y, hidden, slopes, weights):
    return call(
        feed_kernel,
        "vvvffffffff",
        [("f", WIDE), ("f", ROW_LOW), ("f", ROW_LOW), ("f", ROW_FULL), ("v", GAINS)],
        [WEIGHTS[2], WEIGHTS[3], ROW_LOW, ROW_LOW, ROW_FULL, WIDE, ROW_LOW, ROW_FULL, ROW_LOW, ROW_FULL],
        24,
        "encoder_feed",
    )(*gains, grad_gains, cots, grad_y, hidden, slopes, *weights[2], *weights[3])


def ordered_pieces(device):
    pieces = []
    for part in range(2):
        stays = (device >> part) & 1
        pieces.append((2 * part + 1 - stays, 2 * part + stays))
    return pieces


def send_pieces(mover, device, packs, mine, soon, late, rows):
    for part, (goes, stays) in enumerate(ordered_pieces(device)):
        goes = pl.ds(pl.multiple_of(goes * rows, rows), rows)
        stays = pl.ds(pl.multiple_of(stays * rows, rows), rows)
        mover.send(packs[1].at[goes], soon[part] if isinstance(soon, (list, tuple)) else soon.at[pl.ds(part * rows, rows)])
        mover.send(packs[0].at[goes], mine.at[pl.ds(part * rows, rows)])
        mover.send(packs[0].at[stays], mine.at[pl.ds((2 + part) * rows, rows)])
        mover.send(packs[1].at[stays], late.at[pl.ds(part * rows, rows)])


LONG = 2 * HALF
SHORT = HALF


def outer_kernel(mover, ins, outs, held):
    acts, slopes, nfs, gpre0, gb0, gb1 = ins[:6]
    (m0, gains_own, gains_other, grad_gains, grad_m, tokens, qt0, kv0, probs0, inv0, mixt0, ga0, ghidden0, grad_x1,
     qkv_own, qkv_other, proj_own, proj_other) = ins[6:]
    mine, soon, late, out_keep, out_gqkvt, parcel = outs
    acts_held, nfs_held, gpres_held, gbs_held = [held[2 * k : 2 * k + 2] for k in range(4)]
    packs, left, left_nf = held[8:10], held[10], held[11]
    (wqkv, wproj, x, qt, kv, probs, inv, mixt, ga, ghidden, gqkvt, kt, gmt, grad_x, grad_x1_held, grad_m0,
     extras) = held[12:]
    core, device = lax.axis_index("pipe"), lax.axis_index("dp")
    gains = own_gains(gains_own, gains_other, core == 0)
    need = mover.need
    for target, source in zip(gbs_held, (gb0, gb1)):
        mover.bring(target, source)
    for k in range(SEGS):
        mover.bring(acts_held[k], acts.at[k])
    need(*gbs_held, *acts_held)
    for k in range(SEGS):
        mover.bring(nfs_held[k], nfs.at[k])
    mover.bring(gpres_held[0], gpre0)
    mover.bring(gpres_held[1], slopes.at[1])
    mover.bring_either(wproj, core == 0, proj_own, proj_other)
    mover.bring(ga, ga0)
    mover.bring(kv, kv0)
    mover.bring(inv, inv0)
    mover.bring(mixt, mixt0)
    mover.bring(qt, qt0)
    mover.bring(probs, probs0)
    mover.bring_either(wqkv, core == 0, qkv_own, qkv_other)
    mover.bring(x, tokens.at[document_rows(core, 0)])
    mover.bring(ghidden, ghidden0)
    mover.bring(grad_x1_held, grad_x1)
    encoder_ffn_weights(need, core, acts_held, gbs_held, nfs_held, gpres_held, packs, left, left_nf)
    send_pieces(mover, device, packs, mine, soon, late, LONG)
    gain_grad = encoder_attention_backward(
        need, x, m0, gains[0:1], wqkv, wproj, qt, kv, probs, inv, mixt, ga, ghidden, kt, gmt, gqkvt, grad_x, grad_m0
    )
    mover.send(gqkvt, out_gqkvt)
    extras[:SLOTS] = (grad_m[...] + grad_m0[...]).astype(BF16)
    low = jnp.concatenate(
        [grad_gains[0:1] + gain_grad, grad_gains[1:4], jnp.zeros((EXTRAS - SLOTS - 4, D), F32)], axis=0
    )
    extras[SLOTS:] = low.astype(BF16)
    mover.send(extras, parcel.at[pl.ds(0, EXTRAS)])
    keep, give = column_halves(core)
    for segment, source in enumerate((grad_x, grad_x1_held)):
        need(source)
        columns = pl.ds(segment * (D // 2), D // 2)
        mover.send(source.at[:, keep], out_keep.at[:, columns])
        mover.send(source.at[:, give], parcel.at[pl.ds(EXTRAS, SEG_LEN), columns])
    mover.finish()


def outer_call(
    acts, slopes, nfs, gpre0, gb0, gb1, m0, gains, grad_gains, grad_m, tokens, qt0, kv0, probs0, inv0, mixt0, ga0,
    ghidden0, grad_x1, weights,
):
    return call(
        outer_kernel,
        "ffffff" + "vvvvv" + "f" * 13,
        [
            ("f", ((4 * LONG, D), BF16)), ("f", ((2 * LONG, D), BF16)), ("f", ((2 * LONG, D), BF16)), ("f", ROW_LOW),
            ("f", GRAD_TURNED), ("f", ((EXTRAS + SEG_LEN, D), BF16)),
        ],
        [
            WIDE, WIDE, ROW_LOW, ROW_LOW, WIDE, WIDE, ROW_LOW, ROW_LOW, ((4 * LONG, D), BF16), ((4 * LONG, D), BF16),
            twice(SQUARE), twice(SQUARE), WEIGHTS[0], WEIGHTS[1], ROW_LOW, TURNED, KEYS_VALUES, PROBS, INVERSE,
            TURNED, ROW_LOW, ROW_FULL, GRAD_TURNED, ALL_TURNED, TURNED, ROW_LOW, ROW_LOW, SLOT_FULL,
            ((EXTRAS, D), BF16),
        ],
        33,
        "encoder_outer",
    )(
        acts, slopes, nfs, gpre0, gb0, gb1, m0, *gains, grad_gains, grad_m, tokens, qt0, kv0, probs0, inv0, mixt0,
        ga0, ghidden0, grad_x1, *weights[0], *weights[1],
    )


def inner_kernel(mover, ins, outs, held):
    mine, *soon, late = outs
    packs, left = held[8:10], held[10]
    for target, source in zip(held[:6], ins):
        mover.bring(target, source)
    tiles = []
    for block in range(3):
        span = pl.ds(block * TILE, TILE)
        tiles.append([held[6 + k].at[span] for k in range(SEGS)])
        for k in range(SEGS):
            mover.bring(tiles[block][k], ins[6 + k].at[span])
    encoder_attention_weights(
        mover.need, lax.axis_index("pipe"), held[0:2], held[2:4], held[4:6], held[6:8], packs, left,
        lambda block: mover.need(*tiles[block]),
    )
    send_pieces(mover, lax.axis_index("dp"), packs, mine, soon, late, SHORT)
    mover.finish()


def inner_call(*operands):
    pack = ((4 * SHORT, D), BF16)
    return call(
        inner_kernel,
        "ffffffff",
        [("f", pack), ("f", ((SHORT, D), BF16)), ("f", ((SHORT, D), BF16)), ("f", ((2 * SHORT, D), BF16))],
        [TURNED, TURNED, ROW_LOW, ROW_LOW, ALL_LOW, ALL_LOW, GRAD_TURNED, GRAD_TURNED, pack, pack, twice(ALL_TURNED)],
        24,
        "encoder_inner",
    )(*operands)


def assemble_kernel(mover, ins, outs, held):
    parcel, parcel_other, keep0, last_other = ins
    activations, final_memory, grad_tokens = outs
    core = lax.axis_index("pipe")
    rows = SEGS * SEG_LEN
    start = 0
    for source, y, final in zip((parcel, parcel_other), held[0:2], held[2:4]):
        mover.bring(y, source.at[pl.ds(start, rows)])
        mover.bring(final, source.at[pl.ds(start + rows, SLOTS)])
    keep, give = held[4:6]
    mover.bring(keep, keep0)
    mover.bring(give, last_other.at[pl.ds(EXTRAS, SEG_LEN)])
    for document, y, final, grads in zip((core, 1 - core), held[0:2], held[2:4], held[4:6]):
        mover.need(y, final, grads)
        mover.send(y, activations.at[pl.ds(pl.multiple_of(document * rows, rows), rows)])
        mover.send(final, final_memory.at[document])
        for segment in range(SEGS):
            columns = grads.at[:, pl.ds(segment * (D // 2), D // 2)]
            mover.send(columns, grad_tokens.at[document_rows(document, segment)])
    mover.finish()


def assemble_call(*operands):
    rows = 2 * SEGS * SEG_LEN
    outs = [("f", ((rows, D), BF16)), ("f", ((2, SLOTS, D), BF16)), ("f", ((rows, D // 2), BF16))]
    y = ((SEGS * SEG_LEN, D), BF16)
    return call(
        assemble_kernel, "ffff", outs, [y, y, SLOT_LOW, SLOT_LOW, ROW_LOW, ROW_LOW], 16, "assemble"
    )(*operands)


def place_block(block):
    if block < 4:
        return 0, lambda row: (pl.ds(block * TILE + row, HALF), slice(None))
    if block < 8:
        return 1, lambda row: (pl.ds(row, HALF), slice((block - 4) * TILE, (block - 3) * TILE))
    if block == 8:
        return 2, lambda row: (pl.ds(row, HALF), slice(None))
    return 3, lambda row: (pl.ds(row, HALF), slice((block - 9) * TILE, (block - 8) * TILE))


def unpack_kernel(distance, sides, mover, ins, outs, held):
    pieces, wide, short_wide = held
    core = lax.axis_index("pipe")
    device = lax.axis_index("dp")
    count = 2 * len(sides)
    for index in range(count):
        mover.bring_either(pieces.at[index], core == 0, ins[index], ins[count + index])
    arrivals = list(mover.coming.values())
    for index in range(count):
        side, part = sides[index // 2], index % 2
        pltpu.make_async_copy(*arrivals[index]).wait()
        near = (device >> part) & 1
        piece = 2 * part + (near if distance == 0 else 1 - near)
        row = pl.multiple_of((core if side == 0 else 1 - core) * HALF, HALF)
        for half in range(2):
            value = pieces[index, half, :, :LONG_ROWS].reshape(HALF, D).astype(F32)
            wide[index, half] = value
            if part == 0:
                start = pl.multiple_of((2 * piece + half) * TILE + row, HALF)
                mover.send(wide.at[index, half], outs[0].at[pl.ds(start, HALF)])
            else:
                column = pl.multiple_of((2 * (piece - 2) + half) * TILE, TILE)
                mover.send(wide.at[index, half], outs[1].at[pl.ds(row, HALF), pl.ds(column, TILE)])
        short_wide[index] = pieces[index, :, :, LONG_ROWS:].reshape(HALF, D).astype(F32)
        if part == 0:
            sem = mover.slot()
            targets = (outs[2].at[pl.ds(row, HALF)], outs[3].at[pl.ds(row, HALF), pl.ds(0, TILE)])
            for which, target in enumerate(targets):

                @pl.when(piece == which)
                def _(target=target):
                    pltpu.make_async_copy(short_wide.at[index], target, sem).start()

            mover.leaving.append(pltpu.make_async_copy(short_wide.at[index], targets[0], sem))
        else:
            column = pl.multiple_of((piece - 1) * TILE, TILE)
            mover.send(short_wide.at[index], outs[3].at[pl.ds(row, HALF), pl.ds(column, TILE)])
    mover.finish()


def unpack_call(distance, sides, sources, begun):
    outs = [((FF, D), F32), ((D, FF), F32), ((D, D), F32), ((D, 3 * D), F32)]

    def body(mover, ins, results, held):
        unpack_kernel(distance, sides, mover, ins, results, held)

    return call(
        body,
        "f" * (len(sources) + len(begun)),
        [("f", item) for item in outs],
        [((4, 2, CHUNKS, CHUNK, D), BF16), ((4, 2, HALF, D), F32), ((4, HALF, D), F32)],
        16,
        "unpack",
        {len(sources) + k: k for k in range(len(begun))},
    )(*sources, *begun)


def total_of(blocks):
    return sum(block.astype(F32) for block in blocks).astype(BF16)


def fold(outputs):
    arrays = []
    plan = []
    if any(rows % 16 for entries in outputs for rows, _ in entries):
        device = lax.axis_index("dp")
        sums = [
            [total_of([rows_of(array, start(device), rows) for array, start in pieces]) for rows, pieces in entries]
            for entries in outputs
        ]
        return [jnp.concatenate(entries, axis=0) for entries in sums]
    for entries in outputs:
        for rows, pieces in entries:
            for array, start in pieces:
                if not any(array is other for other in arrays):
                    arrays.append(array)
    for entries in outputs:
        plan.append([
            (rows, [([array is other for other in arrays].index(True), start) for array, start in pieces])
            for rows, pieces in entries
        ])
    sizes = [sum(rows for rows, _ in entries) for entries in plan]
    total = sum(rows * len(pieces) for entries in plan for rows, pieces in entries)

    def body(mover, ins, results, held):
        gathered, summed = held
        device = lax.axis_index("dp")
        arrivals, done = [], 0
        for entries in plan:
            for rows, pieces in entries:
                group = []
                for index, start in pieces:
                    target = gathered.at[pl.ds(done, rows)]
                    first = pl.multiple_of(jnp.asarray(start(device), jnp.int32), 16)
                    mover.bring(target, ins[index].at[pl.ds(first, rows)])
                    group.append((target, done))
                    done += rows
                arrivals.append(group)
        arrivals, done = iter(arrivals), 0
        for entries, size, result in zip(plan, sizes, results):
            begin = done
            for rows, pieces in entries:
                group = next(arrivals)
                mover.need(*[target for target, _ in group])
                summed[done : done + rows] = total_of([gathered[row : row + rows] for _, row in group])
                done += rows
            mover.send(summed.at[pl.ds(begin, size)], result)
        mover.finish()

    pieces_count = sum(len(pieces) for entries in plan for _, pieces in entries)
    return call(
        body, "f" * len(arrays), [("f", ((size, D), BF16)) for size in sizes],
        [((total, D), BF16), ((sum(sizes), D), BF16)], pieces_count + len(sizes), "fold",
    )(*arrays)


def swap(block):
    return lax.ppermute(block, "pipe", [(0, 1), (1, 0)])


def neighbour(block, bit):
    devices = lax.axis_size("dp")
    return lax.ppermute(block, "dp", [(k, k ^ (1 << bit)) for k in range(devices)])


def bit_of(bit):
    return (lax.axis_index("dp") >> bit) & 1


def after(value, *others):
    return lax.optimization_barrier((value,) + others)[0]


def rows_of(block, start, size):
    return lax.dynamic_slice_in_dim(block, start, size)


class Part:
    def __init__(self, size, pieces):
        self.size = size
        self.pieces = pieces

    def sum_of(self, shift, size):
        return total_of([rows_of(array, start + shift, size) for array, start in self.pieces])

    def value(self):
        return self.sum_of(0, self.size)


class Lazy:
    def __init__(self, size, pieces):
        self.size = size
        self.pieces = [(array, start if callable(start) else (lambda device, start=start: start)) for array, start in pieces]

    def entry(self):
        return self.size, self.pieces

    def half(self, bit, stays):
        size = self.size // 2

        def moved(start):
            def first(device):
                here = (device >> bit) & 1
                return start(device) + (here if stays else 1 - here) * size

            return first

        return Lazy(size, [(array, moved(start)) for array, start in self.pieces])

    def settled(self, bit, came, row):
        kept = self.half(bit, True)
        return Lazy(kept.size, kept.pieces + [(came, lambda device: row)])


def settle_lazy(parts, bit, came):
    results, done = [], 0
    for part in parts:
        results.append(part.settled(bit, came, done))
        done += results[-1].size
    return results


class Line:
    def __init__(self):
        self.last = None

    def send(self, block, bit):
        if self.last is not None:
            block = after(block, self.last)
        self.last = block
        return neighbour(block, bit)

    def trade(self, parts, bit, extra=None):
        give = [part.sum_of((1 - bit_of(bit)) * (part.size // 2), part.size // 2) for part in parts]
        if extra is not None:
            give.append(extra)
        return self.send(jnp.concatenate(give, axis=0) if len(give) > 1 else give[0], bit)


def settle(parts, bit, came):
    results, done = [], 0
    for part in parts:
        half = part.size // 2
        shift = bit_of(bit) * half
        results.append(Part(half, [(array, start + shift) for array, start in part.pieces] + [(came, done)]))
        done += half
    return results, came[done:]


def as_piece(block):
    rows = block.shape[1]
    if rows != CHUNK:
        long = rows * LONG_ROWS // CHUNK
        long, short = block[:, :long].reshape(-1, LONG_ROWS, D), block[:, long:].reshape(-1, SHORT_ROWS, D)
        block = jnp.concatenate([long, short], axis=1)
    return block.reshape(PACK[0][1:])


def join(block, came, bit):
    low = bit_of(bit) == 0
    return jnp.concatenate([jnp.where(low, block, came), jnp.where(low, came, block)], axis=0)


def local(
    tokens, lengths, memory_init, attn_gain, qkv_weight, proj_weight, ffn_gain, in_weight, out_weight,
    cot_tokens, cot_memory,
):
    core = lax.axis_index("pipe")
    front = core == 0
    gains = jnp.concatenate([attn_gain, ffn_gain], axis=0)
    gains = (gains, swap(gains))
    weights = [(held[0], swap(held[0])) for held in (qkv_weight, proj_weight, in_weight, out_weight)]

    hidden0, n0, qt0, kv0, probs0, inv0, mixt0 = first_call(tokens, memory_init, gains, weights)
    (parcel, mem_mine, mem_theirs, nfs, acts, slopes, n1, mixt1, gb1, ga1, gqkvt1, grad_y0, grad_x1, grad_m,
     grad_gains) = middle_call(lengths, memory_init, gains, cot_memory, hidden0, tokens, cot_tokens, weights)
    mem_theirs, parcel_other = swap(mem_theirs), swap(parcel)
    gpre0, gb0, ga0, ghidden0, grad_gains = feed_call(
        gains, grad_gains, cot_tokens, grad_y0, hidden0, slopes, weights
    )

    bits = lax.axis_size("dp").bit_length() - 1
    line = Line()
    both = range(2)
    mem_theirs, gb0 = lax.optimization_barrier((mem_theirs, gb0))
    rows = 2 * PIECE
    mem_mine, mem_theirs = mem_mine.reshape(-1, D), mem_theirs.reshape(-1, D)
    mem = [[Part(rows, [(mem_mine, k * rows), (mem_theirs, k * rows)])] for k in both]
    mem_came = [line.trade(mem[k], k) for k in both]
    long_mine, long_soon, long_late, out_keep, gqkvt0, last_parcel = outer_call(
        acts, slopes, nfs, gpre0, after(gb0, line.last), gb1, memory_init, gains, grad_gains, grad_m, tokens, qt0, kv0,
        probs0, inv0, mixt0, ga0, ghidden0, grad_x1, weights,
    )
    long_soon, last_other, long_late = swap(long_soon), swap(last_parcel), swap(long_late)
    *mem_came, gqkvt0 = lax.optimization_barrier((*mem_came, gqkvt0))
    mem = [settle(mem[k], k, mem_came[k])[0] for k in both]
    mem_came = [line.trade(mem[k], 1 - k) for k in both]
    short_mine, *short_soon, short_late = inner_call(
        mixt0, mixt1, ga0, ga1, n0, n1, after(gqkvt0, line.last), gqkvt1
    )
    short_soon, short_late = [swap(block) for block in short_soon], swap(short_late)
    *mem_came, short_mine = lax.optimization_barrier((*mem_came, short_mine))
    rest = list(range(2, bits))
    extras = Lazy(EXTRAS, [(last_parcel, 0), (last_other, 0)])
    enc = [
        [
            Lazy(LONG, [(long_mine, k * LONG), (long_soon, k * LONG)]),
            Lazy(SHORT, [(short_mine, k * SHORT), (short_soon[k], 0)]),
        ]
        for k in both
    ]
    gives = fold([[part.entry() for part in enc[0] + [extras]], [part.entry() for part in enc[1]]])
    enc_came = [line.send(gives[k], k) for k in both]
    extras = Lazy(EXTRAS, extras.pieces + [(enc_came[0], lambda device: PIECE)])
    mem = [settle(mem[k], 1 - k, mem_came[k])[0] for k in both]
    mem = mem[0] + mem[1]
    for bit in rest:
        mem = settle(mem, bit, line.trade(mem, bit))[0]
    mem = jnp.concatenate([part.value() for part in mem], axis=0)[None]
    enc = [
        [
            Lazy(LONG, [(long_mine, (2 + k) * LONG), (long_late, k * LONG), (enc_came[k], 0)]),
            Lazy(SHORT, [(short_mine, (2 + k) * SHORT), (short_late, k * SHORT), (enc_came[k], LONG)]),
        ]
        for k in both
    ]
    gives = fold([
        [part.half(1, False).entry() for part in enc[0]] + [extras.entry()],
        [part.half(0, False).entry() for part in enc[1]],
    ])
    enc_came = [line.send(gives[k], 1 - k) for k in both]
    extras = Lazy(EXTRAS, extras.pieces + [(enc_came[0], PIECE // 2)])
    for bit in rest[:0:-1]:
        mem = join(mem, line.send(mem, bit), bit)
    enc = settle_lazy(enc[0], 1, enc_came[0]) + settle_lazy(enc[1], 0, enc_came[1])
    for bit in rest:
        rows = sum(part.size for part in enc) // 2
        (give,) = fold([[part.half(bit, False).entry() for part in enc] + [extras.entry()]])
        came = line.send(give, bit)
        enc = settle_lazy(enc, bit, came)
        extras = Lazy(EXTRAS, extras.pieces + [(came, rows)])
        if bit == rest[0]:
            mem = join(mem, line.send(mem, bit), bit)

    def split(block):
        rows = block.shape[1] // 2
        return block[:, :rows], block[:, rows:]

    mem_parts = split(mem)
    enc, extras = fold([[part.entry() for part in enc], [extras.entry()]])
    enc = enc[None]
    mem_came = [line.send(mem_parts[k], 1 - k) for k in both]
    for bit in rest[::-1]:
        if bit == rest[0]:
            mem_near = [join(mem_parts[k], mem_came[k], 1 - k) for k in both]
            mem_far = [line.send(mem_near[k], k) for k in both]
        enc = join(enc, line.send(enc, bit), bit)
    *mem_far, enc = lax.optimization_barrier((*mem_far, enc))
    enc_parts = split(enc)
    enc_came = [line.send(enc_parts[k], 1 - k) for k in both]
    *enc_came, activations, final_memory, grad_tokens = lax.optimization_barrier(
        (*enc_came, *assemble_call(parcel, parcel_other, out_keep, last_other))
    )
    enc_near = [join(enc_parts[k], enc_came[k], 1 - k) for k in both]
    enc_far = [line.send(enc_near[k], k) for k in both]

    enc_near, enc_far = [[as_piece(block) for block in blocks] for blocks in (enc_near, enc_far)]
    mem_near, mem_far = [[block.reshape(PACK[0][1:]) for block in blocks] for blocks in (mem_near, mem_far)]

    def swapped(blocks):
        return [swap(block) for block in blocks]

    begun = unpack_call(0, (0, 1), enc_near + swapped(enc_near) + mem_near + swapped(mem_near), ())
    tied = lax.optimization_barrier((*enc_far, *begun))
    enc_far, begun = tied[:2], tied[2:]
    enc_last, mem_last = swapped(enc_far), swapped(mem_far)
    begun = unpack_call(1, (0,), [*enc_far, *mem_far], begun)
    grad_out, grad_in, grad_proj, grad_qkv = unpack_call(1, (1,), enc_last + mem_last, begun)
    extras = extras.astype(F32)
    gain_grads = jnp.where(front, extras[SLOTS : SLOTS + 2], extras[SLOTS + 2 : SLOTS + 4])
    return (
        activations,
        final_memory,
        grad_tokens,
        extras[:SLOTS],
        gain_grads[0:1],
        grad_qkv[None],
        grad_proj[None],
        gain_grads[1:2],
        grad_in[None],
        grad_out[None],
    )


def solution(mesh):
    placed = (
        P("dp", None),
        P("dp"),
        P(),
        P("pipe", None),
        P("pipe", None, None),
        P("pipe", None, None),
        P("pipe", None),
        P("pipe", None, None),
        P("pipe", None, None),
        P("dp", None),
        P("dp", None, None),
    )
    return jax.shard_map(
        local,
        mesh=mesh,
        in_specs=placed,
        out_specs=(
            P("dp", None),
            P("dp", None, None),
            P("dp", "pipe"),
            P(),
            P("pipe", None),
            P("pipe", None, None),
            P("pipe", None, None),
            P("pipe", None),
            P("pipe", None, None),
            P("pipe", None, None),
        ),
        check_vma=False,
    )
```
